32 devices in a mesh: section: 4 (over y, x), dp: 8 (over z, core).
Axes of the slice: x: 2, y: 2, z: 4, core: 2. Of those that a mesh axis runs over, the one named last changes fastest.
Arguments:
- pixels: bfloat16 [16, 1536, 1536], P('dp'), may hold values from -6 to 6
- token_order: int32 [16, 1536], P('dp'), may hold values from 0 to 1535, each once within a row
- visible: int32 [16], P('dp'), may hold values from 192 to 576, as said below
- wide_weight: float32 [1024, 8576], P('dp'), may hold values from -0.1875 to 0.1875
- tall_weight: float32 [5632, 1024], P('dp'), may hold values from -0.09375 to 0.09375
- pred_weight: float32 [384, 4096], P('dp'), may hold values from -0.3125 to 0.3125
- pred_down: float32 [1536, 384], P('dp'), may hold values from -0.15625 to 0.15625
- enc_gains: float32 [1024, 3], P('dp'), may hold values from 0.15 to 5
- pred_gains: float32 [384, 4], P('dp'), may hold values from -3 to 5
- wide_first: float32 [1024, 8576], P('dp'), may hold values from -7.6293945e-06 to 7.6293945e-06
- tall_first: float32 [5632, 1024], P('dp'), may hold values from -7.6293945e-06 to 7.6293945e-06
- pred_first: float32 [384, 4096], P('dp'), may hold values from -7.6293945e-06 to 7.6293945e-06
- pred_down_first: float32 [1536, 384], P('dp'), may hold values from -7.6293945e-06 to 7.6293945e-06
- enc_gains_first: float32 [1024, 3], P('dp'), may hold values from -3.0517578e-05 to 3.0517578e-05
- pred_gains_first: float32 [384, 4], P('dp'), may hold values from -3.0517578e-05 to 3.0517578e-05
- wide_second: float32 [1024, 8576], P('dp'), may hold values from 1.4955474e-13 to 5.9821896e-13
- tall_second: float32 [5632, 1024], P('dp'), may hold values from 1.4955474e-13 to 5.9821896e-13
- pred_second: float32 [384, 4096], P('dp'), may hold values from 1.4955474e-13 to 5.9821896e-13
- pred_down_second: float32 [1536, 384], P('dp'), may hold values from 1.4955474e-13 to 5.9821896e-13
- enc_gains_second: float32 [1024, 3], P('dp'), may hold values from 2.3928758e-12 to 9.571503e-12
- pred_gains_second: float32 [384, 4], P('dp'), may hold values from 2.3928758e-12 to 9.571503e-12
- teacher_wide: float32 [1024, 8192], P('dp'), may hold values from -0.1875 to 0.1875
- teacher_tall: float32 [5632, 1024], P('dp'), may hold values from -0.09375 to 0.09375
- teacher_gains: float32 [1024, 3], P('dp'), may hold values from 0.15 to 5
Outputs:
- loss_sum: float32 [], replicated
- target_count: float32 [], replicated
- grad_norm: float32 [], replicated
- wide_new: float32 [1024, 8576], P('dp')
- tall_new: float32 [5632, 1024], P('dp')
- pred_new: float32 [384, 4096], P('dp')
- pred_down_new: float32 [1536, 384], P('dp')
- enc_gains_new: float32 [1024, 3], P('dp')
- pred_gains_new: float32 [384, 4], P('dp')
- wide_first_new: float32 [1024, 8576], P('dp')
- tall_first_new: float32 [5632, 1024], P('dp')
- pred_first_new: float32 [384, 4096], P('dp')
- pred_down_first_new: float32 [1536, 384], P('dp')
- enc_gains_first_new: float32 [1024, 3], P('dp')
- pred_gains_first_new: float32 [384, 4], P('dp')
- wide_second_new: float32 [1024, 8576], P('dp')
- tall_second_new: float32 [5632, 1024], P('dp')
- pred_second_new: float32 [384, 4096], P('dp')
- pred_down_second_new: float32 [1536, 384], P('dp')
- enc_gains_second_new: float32 [1024, 3], P('dp')
- pred_gains_second_new: float32 [384, 4], P('dp')
- wide_copy: bfloat16 [1024, 8576], P('dp')
- tall_copy: bfloat16 [5632, 1024], P('dp')
- pred_copy: bfloat16 [384, 4096], P('dp')
- pred_down_copy: bfloat16 [1536, 384], P('dp')
- enc_gains_copy: bfloat16 [1024, 3], P('dp')
- pred_gains_copy: bfloat16 [384, 4], P('dp')
- teacher_wide_new: float32 [1024, 8192], P('dp')
- teacher_tall_new: float32 [5632, 1024], P('dp')
- teacher_gains_new: float32 [1024, 3], P('dp')
The draws below stay inside these ranges and needn't reach their ends.
Inputs may be any that keep to these rules, and one draw needn't show every extreme that they name: Some clip has exactly 576 visible tokens and some clip exactly 192.
All inputs are finite; a program needn't handle non-finite values.
Results may differ from the reference program's by a relative error of at most 0.005.
The reference program's roundings to bfloat16 on the way count: a program that leaves them out, or rounds other values in their place, can miss the bound.
Values may be sent and summed in bfloat16 or wider, within the bound.
A program may use at most 640 MiB of HBM per device.

```python
import math
import jax
import jax.numpy as jnp
from jax import lax

D = 1024
HE = 16
FF = 4096
PD = 384
PH = 12
PF = 1536
PATCH = 1536
L = 1536
STEP = 10
VIS = 576
VIS_LO = 192
CLIPS = 16
NPARAM = 16716288


def ramp_gain(key, row_count, col_count, first_end, last_end, spread_width):
    rising = first_end + (last_end - first_end) * jnp.arange(row_count, dtype=jnp.float32)[:, None] / row_count
    jitter = jnp.clip(jax.random.normal(key, (row_count, col_count), jnp.float32), -3.0, 3.0)
    return rising * jnp.exp(spread_width * jitter)


def draw_visible(key, part):
    key = jax.random.fold_in(key, 11)
    counts = jax.random.randint(key, (CLIPS,), VIS_LO, VIS + 1)
    picks = jax.random.permutation(jax.random.fold_in(key, 1), CLIPS)
    counts = counts.at[picks[0]].set(VIS).at[picks[1]].set(VIS_LO)
    return counts.astype(jnp.int32)


def draw_enc_gains(key, part):
    key = jax.random.fold_in(key, 21)
    return ramp_gain(key, D, 3, 0.6, 1.8, 0.15)


def draw_pred_gains(key, part):
    key = jax.random.fold_in(key, 22)
    token_key = jax.random.fold_in(key, 5)
    mask_token = jnp.clip(jax.random.normal(token_key, (PD, 1), jnp.float32), -3.0, 3.0)
    return jnp.concatenate([ramp_gain(key, PD, 3, 0.6, 1.8, 0.15), mask_token], axis=1)


def draw_teacher_gains(key, part):
    key = jax.random.fold_in(key, 23)
    return ramp_gain(key, D, 3, 1.8, 0.6, 0.15)


def levels(stream_key, dims, shards, low, largest):
    gain = 1.0
    for position, shards_of in shards:
        draws = jax.random.uniform(jax.random.fold_in(jax.random.fold_in(stream_key, 6), position), (shards_of,), jnp.float32, low / len(shards), largest / len(shards))
        gain = gain * jnp.repeat(jnp.exp(draws), dims[position] // shards_of).reshape((-1,) + (1,) * (len(dims) - 1 - position))
    return gain


def scatter_about(key, shape, deviation, most, shards=(), kind=jnp.bfloat16):
    array = jax.random.normal(key, shape, jnp.float32) * deviation
    if len(shards) > 0:
        array = levels(key, shape, shards, -0.22, 0.18) * array
    return jnp.clip(array, min=-most, max=most).astype(kind)


def setup_inputs(seed: int = 0) -> dict:
    streams_of = jax.random.split(jax.random.key(seed), 25)
    pixels = scatter_about(streams_of[0], (CLIPS, L, PATCH), 1.0, 6.0, ((0, 8),))
    token_order = jax.vmap(lambda own: jax.random.permutation(own, L))(jax.random.split(streams_of[1], CLIPS)).reshape((CLIPS, L)).astype(jnp.int32)
    visible = draw_visible(jax.random.fold_in(streams_of[24], 71), 0)
    wide_weight = scatter_about(streams_of[3], (D, 4 * D + FF + PD), D ** -0.5, 0.1875, ((0, 8),), jnp.float32)
    tall_weight = scatter_about(streams_of[4], (PATCH + FF, D), FF ** -0.5, 0.09375, ((0, 8),), jnp.float32)
    pred_weight = scatter_about(streams_of[5], (PD, 4 * PD + PF + D), PD ** -0.5, 0.3125, ((0, 8),), jnp.float32)
    pred_down = scatter_about(streams_of[6], (PF, PD), PF ** -0.5, 0.15625, ((0, 8),), jnp.float32)
    enc_gains = draw_enc_gains(jax.random.fold_in(streams_of[24], 71), 0)
    pred_gains = draw_pred_gains(jax.random.fold_in(streams_of[24], 71), 0)
    wide_first = scatter_about(streams_of[9], (D, 4 * D + FF + PD), (0.0055 / NPARAM ** 0.5), 7.62939453125e-06, ((0, 8),), jnp.float32)
    tall_first = scatter_about(streams_of[10], (PATCH + FF, D), (0.0055 / NPARAM ** 0.5), 7.62939453125e-06, ((0, 8),), jnp.float32)
    pred_first = scatter_about(streams_of[11], (PD, 4 * PD + PF + D), (0.0055 / NPARAM ** 0.5), 7.62939453125e-06, ((0, 8),), jnp.float32)
    pred_down_first = scatter_about(streams_of[12], (PF, PD), (0.0055 / NPARAM ** 0.5), 7.62939453125e-06, ((0, 8),), jnp.float32)
    enc_gains_first = scatter_about(streams_of[13], (D, 3), (0.022 / NPARAM ** 0.5), 3.0517578125e-05, ((0, 8),), jnp.float32)
    pred_gains_first = scatter_about(streams_of[14], (PD, 4), (0.022 / NPARAM ** 0.5), 3.0517578125e-05, ((0, 8),), jnp.float32)
    wide_second = jnp.clip(jnp.exp(math.log(5.982189570097329e-13) - 1.3862944 * jax.random.uniform(streams_of[15], (D, 4 * D + FF + PD), jnp.float32) ** levels(streams_of[15], (D, 4 * D + FF + PD), ((0, 8),), -0.2, 0.2)), 1.4955473925243323e-13, 5.982189570097329e-13)
    tall_second = jnp.clip(jnp.exp(math.log(5.982189570097329e-13) - 1.3862944 * jax.random.uniform(streams_of[16], (PATCH + FF, D), jnp.float32) ** levels(streams_of[16], (PATCH + FF, D), ((0, 8),), -0.2, 0.2)), 1.4955473925243323e-13, 5.982189570097329e-13)
    pred_second = jnp.clip(jnp.exp(math.log(5.982189570097329e-13) - 1.3862944 * jax.random.uniform(streams_of[17], (PD, 4 * PD + PF + D), jnp.float32) ** levels(streams_of[17], (PD, 4 * PD + PF + D), ((0, 8),), -0.2, 0.2)), 1.4955473925243323e-13, 5.982189570097329e-13)
    pred_down_second = jnp.clip(jnp.exp(math.log(5.982189570097329e-13) - 1.3862944 * jax.random.uniform(streams_of[18], (PF, PD), jnp.float32) ** levels(streams_of[18], (PF, PD), ((0, 8),), -0.2, 0.2)), 1.4955473925243323e-13, 5.982189570097329e-13)
    enc_gains_second = jnp.clip(jnp.exp(math.log(9.571503312155727e-12) - 1.3862944 * jax.random.uniform(streams_of[19], (D, 3), jnp.float32) ** levels(streams_of[19], (D, 3), ((0, 8),), -0.2, 0.2)), 2.3928758280389317e-12, 9.571503312155727e-12)
    pred_gains_second = jnp.clip(jnp.exp(math.log(9.571503312155727e-12) - 1.3862944 * jax.random.uniform(streams_of[20], (PD, 4), jnp.float32) ** levels(streams_of[20], (PD, 4), ((0, 8),), -0.2, 0.2)), 2.3928758280389317e-12, 9.571503312155727e-12)
    teacher_wide = scatter_about(streams_of[21], (D, 4 * D + FF), D ** -0.5, 0.1875, ((0, 8),), jnp.float32)
    teacher_tall = scatter_about(streams_of[22], (PATCH + FF, D), FF ** -0.5, 0.09375, ((0, 8),), jnp.float32)
    teacher_gains = draw_teacher_gains(jax.random.fold_in(streams_of[24], 71), 0)
    return {"pixels": pixels, "token_order": token_order, "visible": visible, "wide_weight": wide_weight, "tall_weight": tall_weight, "pred_weight": pred_weight, "pred_down": pred_down, "enc_gains": enc_gains, "pred_gains": pred_gains, "wide_first": wide_first, "tall_first": tall_first, "pred_first": pred_first, "pred_down_first": pred_down_first, "enc_gains_first": enc_gains_first, "pred_gains_first": pred_gains_first, "wide_second": wide_second, "tall_second": tall_second, "pred_second": pred_second, "pred_down_second": pred_down_second, "enc_gains_second": enc_gains_second, "pred_gains_second": pred_gains_second, "teacher_wide": teacher_wide, "teacher_tall": teacher_tall, "teacher_gains": teacher_gains}


@jax.custom_vjp
def low(v):
    return lax.optimization_barrier(v.astype(jnp.bfloat16)).astype(jnp.float32)

@jax.custom_vjp
def low_back(v):
    return v

def low_keep(v):
    return (low(v), None)

def low_pass(kept, grad):
    return (grad,)

def back_keep(v):
    return (v, None)

def back_low(kept, grad):
    return (low(grad),)
low.defvjp(low_keep, low_pass)
low_back.defvjp(back_keep, back_low)
HIGHEST_PREC = lax.Precision.HIGHEST
BETA_ONE = 0.9
BETA_TWO = 0.999
EPSILON = 1e-08
RATE = 0.02
GAIN_RATE = 0.5
DECAY = 0.05
CLIP_AT = 0.05
KEEP_RATE = 0.8
NEGATIVE = -1e+30

def narrow(value):
    return low_back(low(value))

def matmul(left, right):
    return jnp.dot(left, right, precision=HIGHEST_PREC, preferred_element_type=jnp.float32)

def normed(stream):
    centred = stream - lax.optimization_barrier(jnp.mean(stream, axis=-1, keepdims=True))
    return centred * lax.rsqrt(lax.optimization_barrier(jnp.mean(centred * centred, axis=-1, keepdims=True)) + 1e-06)

def position_table(positions, feature_width):
    frequency = jnp.exp(jnp.arange(feature_width // 2, dtype=jnp.float32) * (-2.0 * math.log(10000.0) / feature_width))
    angles = positions.astype(jnp.float32)[:, None] * frequency[None, :]
    return jnp.concatenate([jnp.sin(angles), jnp.cos(angles)], axis=1)

def attend(stream, gain_vec, w_in, w_out, num_heads, key_keep):
    row_count, feature_width = stream.shape
    head_size = feature_width // num_heads
    normal_in = narrow(normed(stream) * gain_vec)
    packed = narrow(matmul(normal_in, w_in))
    queries = packed[:, :feature_width].reshape(row_count, num_heads, head_size)
    key_heads = packed[:, feature_width:2 * feature_width].reshape(row_count, num_heads, head_size)
    value_heads = packed[:, 2 * feature_width:].reshape(row_count, num_heads, head_size)
    logits = low_back(jnp.einsum('qhd,khd->hqk', queries, key_heads, precision=HIGHEST_PREC) * head_size ** (-0.5))
    if key_keep is not None:
        logits = jnp.where(key_keep[None, None, :], logits, NEGATIVE)
    attn_probs = low(jax.nn.softmax(logits, axis=-1))
    merged = narrow(jnp.einsum('hqk,khd->qhd', attn_probs, value_heads, precision=HIGHEST_PREC).reshape(row_count, feature_width))
    return stream + low_back(matmul(merged, w_out))

def feed_forward(stream, gain_vec, w_up, w_down):
    normal_in = narrow(normed(stream) * gain_vec)
    raised = low_back(matmul(normal_in, w_up))
    hidden = narrow(jax.nn.gelu(raised, approximate=False))
    return stream + low_back(matmul(hidden, w_down))

def teacher_goal(teacher, frame_rows, order_row):
    teach_wide, teach_tall, teach_gain = teacher
    positions = lax.iota(jnp.int32, L)
    stream = matmul(frame_rows, teach_tall[:PATCH]) + position_table(positions, D)
    stream = narrow(attend(stream, teach_gain[:, 0], teach_wide[:, :3 * D], teach_wide[:, 3 * D:4 * D], HE, None))
    stream = feed_forward(stream, teach_gain[:, 1], teach_wide[:, 4 * D:], teach_tall[PATCH:])
    return low(normed(normed(stream) * teach_gain[:, 2])[order_row])

def clip_loss(params, frame_rows, order_row, count_here, goal_rows):
    w_wide, w_tall, w_pred, w_down, enc_gain, pred_gain = params
    positions = lax.iota(jnp.int32, L)
    row_ids = order_row[:VIS]
    key_keep = positions[:VIS] < count_here
    stream = low_back(matmul(frame_rows[row_ids], w_tall[:PATCH])) + position_table(row_ids, D)
    stream = narrow(attend(stream, enc_gain[:, 0], w_wide[:, :3 * D], w_wide[:, 3 * D:4 * D], HE, key_keep))
    stream = feed_forward(stream, enc_gain[:, 1], w_wide[:, 4 * D:4 * D + FF], w_tall[PATCH:])
    encoded = narrow(normed(stream) * enc_gain[:, 2])
    projected = low_back(matmul(encoded, w_wide[:, 4 * D + FF:]))
    filled = jnp.concatenate([projected, jnp.zeros((L - VIS, PD), jnp.float32)], axis=0)
    context = (positions < count_here)[:, None]
    stream = jnp.where(context, filled, pred_gain[:, 3][None, :]) + position_table(order_row, PD)
    stream = narrow(attend(stream, pred_gain[:, 0], w_pred[:, :3 * PD], w_pred[:, 3 * PD:4 * PD], PH, None))
    stream = feed_forward(stream, pred_gain[:, 1], w_pred[:, 4 * PD:4 * PD + PF], w_down)
    final = narrow(normed(stream) * pred_gain[:, 2])
    guess = low_back(matmul(final, w_pred[:, 4 * PD + PF:]))
    residual = guess - goal_rows
    errors = jnp.sqrt(residual * residual + 1.0) - 1.0
    return jnp.sum(jnp.where((positions >= count_here)[:, None], errors, 0.0))

def adamw_step(weight, grad_now, first, second, decay, rate):
    first = BETA_ONE * first + (1.0 - BETA_ONE) * grad_now
    second = BETA_TWO * second + (1.0 - BETA_TWO) * grad_now * grad_now
    ratio = first / (1.0 - BETA_ONE ** STEP) / (jnp.sqrt(second / (1.0 - BETA_TWO ** STEP)) + EPSILON)
    return (weight - rate * (ratio + decay * weight), first, second)

def reference(pixels, token_order, visible, wide_weight, tall_weight, pred_weight, pred_down, enc_gains, pred_gains, wide_first, tall_first, pred_first, pred_down_first, enc_gains_first, pred_gains_first, wide_second, tall_second, pred_second, pred_down_second, enc_gains_second, pred_gains_second, teacher_wide, teacher_tall, teacher_gains):
    masters = (wide_weight, tall_weight, pred_weight, pred_down, enc_gains, pred_gains)
    firsts = (wide_first, tall_first, pred_first, pred_down_first, enc_gains_first, pred_gains_first)
    seconds = (wide_second, tall_second, pred_second, pred_down_second, enc_gains_second, pred_gains_second)
    weights = tuple((member.astype(jnp.bfloat16).astype(jnp.float32) for member in masters))
    teacher = tuple((member.astype(jnp.bfloat16).astype(jnp.float32) for member in (teacher_wide, teacher_tall, teacher_gains)))
    frames = pixels.astype(jnp.float32)
    goals = lax.map(lambda entry: teacher_goal(teacher, entry[0], entry[1]), (frames, token_order))
    target_count = jnp.sum(L - visible).astype(jnp.float32)

    def total_loss(params):

        def clip_step(carried_through, entry):
            return (carried_through + jax.checkpoint(clip_loss)(params, entry[0], entry[1], entry[2], entry[3]), None)
        loss_total, discarded_value = lax.scan(clip_step, jnp.float32(0.0), (frames, token_order, visible, goals))
        return loss_total
    loss_sum, backward_fn = jax.vjp(total_loss, weights)
    grads = backward_fn(1.0 / target_count)[0]
    grad_norm = jnp.sqrt(sum((jnp.sum(member * member) for member in grads)))
    factor = jnp.minimum(1.0, CLIP_AT / (grad_norm + 1e-06))
    decays = (DECAY, DECAY, DECAY, DECAY, 0.0, 0.0)
    rates = (RATE, RATE, RATE, RATE, GAIN_RATE, GAIN_RATE)
    results = [adamw_step(masters[group_idx], grads[group_idx] * factor, firsts[group_idx], seconds[group_idx], decays[group_idx], rates[group_idx]) for group_idx in range(6)]
    news = [entry[0] for entry in results]
    teacher_wide_new = KEEP_RATE * teacher_wide + (1.0 - KEEP_RATE) * news[0][:, :4 * D + FF]
    teacher_tall_new = KEEP_RATE * teacher_tall + (1.0 - KEEP_RATE) * news[1]
    teacher_gains_new = KEEP_RATE * teacher_gains + (1.0 - KEEP_RATE) * news[4]
    return (loss_sum, target_count, grad_norm, news[0], news[1], news[2], news[3], news[4], news[5], results[0][1], results[1][1], results[2][1], results[3][1], results[4][1], results[5][1], results[0][2], results[1][2], results[2][2], results[3][2], results[4][2], results[5][2], news[0].astype(jnp.bfloat16), news[1].astype(jnp.bfloat16), news[2].astype(jnp.bfloat16), news[3].astype(jnp.bfloat16), news[4].astype(jnp.bfloat16), news[5].astype(jnp.bfloat16), teacher_wide_new, teacher_tall_new, teacher_gains_new)
```

```python
import functools
import math

import jax
import jax.numpy as jnp
from jax import lax
from jax.experimental import pallas as pl
from jax.experimental.pallas import tpu as pltpu
from jax.sharding import PartitionSpec as P

D = 1024
HE = 16
FF = 4096
PD = 384
PH = 12
PF = 1536
PATCH = 1536
L = 1536
STEP = 10
VIS = 576
VIS_LO = 192
HALF = L // 2
SEEN = VIS // 2
SKIP = VIS_LO // 2
LANES = 128
VMEM_LIMIT = 50 * 1024 * 1024


BETA_ONE = 0.9
BETA_TWO = 0.999
EPSILON = 1e-08
RATE = 0.02
GAIN_RATE = 0.5
DECAY = 0.05
CLIP_AT = 0.05
KEEP_RATE = 0.8
NEGATIVE = -1e30


def shortened(x):
    return jax.tree.map(lambda a: a.astype(jnp.bfloat16) if a.dtype == jnp.float32 else a, x)


def normed(stream):
    centred = stream - jnp.mean(stream, axis=-1, keepdims=True)
    return centred * lax.rsqrt(jnp.mean(centred * centred, axis=-1, keepdims=True) + 1e-06)


def scaled(stream, gain_vec):
    return normed(stream) * gain_vec


def position_table(positions, feature_width):
    frequency = jnp.exp(
        jnp.arange(feature_width // 2, dtype=jnp.float32)
        * (-2.0 * math.log(10000.0) / feature_width)
    )
    angles = positions.astype(jnp.float32)[:, None] * frequency[None, :]
    return jnp.concatenate([jnp.sin(angles), jnp.cos(angles)], axis=1)


def matmul(left, right):
    return jnp.dot(left, right, preferred_element_type=jnp.float32)


def inner_rows(left, right):
    return lax.dot_general(
        left, right, (((0,), (0,)), ((), ())), preferred_element_type=jnp.float32
    )


def outer_rows(left, right):
    return lax.dot_general(
        left, right, (((1,), (1,)), ((), ())), preferred_element_type=jnp.float32
    )


def gelu_exact(raised):
    return jax.nn.gelu(raised, approximate=False)


def head_scores(queries, key_heads, kept):
    logits = outer_rows(queries, key_heads)
    if kept is None:
        return logits
    key_ids = lax.broadcasted_iota(jnp.int32, logits.shape, 1)
    return jnp.where(key_ids < kept, logits, NEGATIVE)


def attend_kernel(head_size, masked, kept_ref, q_ref, k0_ref, v0_ref, k1_ref, v1_ref, o_ref, l_ref):
    exponent = head_size ** (-0.5) * math.log2(math.e)
    lane_head = lax.broadcasted_iota(jnp.int32, (1, LANES), 1) // head_size
    kept = (kept_ref[0], kept_ref[1]) if masked else (None, None)
    queries = q_ref[...]
    merged = jnp.zeros(o_ref.shape, jnp.float32)
    log_totals = jnp.zeros(o_ref.shape, jnp.float32)
    for head in range(LANES // head_size):
        chosen = lane_head == head
        head_queries = jnp.where(chosen, queries, jnp.zeros_like(queries))
        near = head_scores(head_queries, k0_ref[...], kept[0])
        far = head_scores(head_queries, k1_ref[...], kept[1])
        row_max = exponent * jnp.maximum(
            jnp.max(near, axis=1, keepdims=True), jnp.max(far, axis=1, keepdims=True)
        )
        near = jnp.exp2(near * exponent - row_max)
        far = jnp.exp2(far * exponent - row_max)
        row_total = jnp.sum(near, axis=1, keepdims=True) + jnp.sum(far, axis=1, keepdims=True)
        outcome = matmul(near.astype(jnp.bfloat16), v0_ref[...]) + matmul(
            far.astype(jnp.bfloat16), v1_ref[...]
        )
        merged = jnp.where(chosen, outcome / row_total, merged)
        log_totals = jnp.where(chosen, row_max + jnp.log2(row_total), log_totals)
    o_ref[...] = merged.astype(o_ref.dtype)
    l_ref[...] = log_totals


def attend_rows(queries, kv_near, kv_far, kept, num_heads, block_rows):
    row_count, width = queries.shape
    keys = kv_near.shape[0]
    groups = width // LANES
    masked = kept is not None
    if not masked:
        kept = jnp.zeros((2,), jnp.int32)
    row_spec = pl.BlockSpec((block_rows, LANES), lambda g, b, kept: (b, g))
    k_spec = pl.BlockSpec((keys, LANES), lambda g, b, kept: (0, g))
    v_spec = pl.BlockSpec((keys, LANES), lambda g, b, kept: (0, g + groups))
    return pl.pallas_call(
        functools.partial(attend_kernel, width // num_heads, masked),
        grid_spec=pltpu.PrefetchScalarGridSpec(
            num_scalar_prefetch=1,
            grid=(groups, row_count // block_rows),
            in_specs=[row_spec, k_spec, v_spec, k_spec, v_spec],
            out_specs=[row_spec, row_spec],
        ),
        out_shape=[
            jax.ShapeDtypeStruct((row_count, width), jnp.bfloat16),
            jax.ShapeDtypeStruct((row_count, width), jnp.float32),
        ],
        compiler_params=pltpu.CompilerParams(vmem_limit_bytes=VMEM_LIMIT),
        cost_estimate=pl.CostEstimate(
            flops=8 * row_count * keys * width,
            bytes_accessed=8 * (row_count + keys) * width,
            transcendentals=2 * row_count * keys * num_heads,
        ),
    )(kept, queries, kv_near, kv_near, kv_far, kv_far)


def attend_back_kernel(
    head_size, masked, kept_ref, q_ref, g_ref, l_ref, k0_ref, v0_ref, k1_ref, v1_ref,
    dq_ref, dk0_ref, dv0_ref, dk1_ref, dv1_ref,
):
    scaling = head_size ** (-0.5)
    exponent = scaling * math.log2(math.e)
    lane_head = lax.broadcasted_iota(jnp.int32, (1, LANES), 1) // head_size
    kept = (kept_ref[0], kept_ref[1]) if masked else (None, None)

    @pl.when(pl.program_id(1) == 0)
    def _():
        for ref in (dk0_ref, dv0_ref, dk1_ref, dv1_ref):
            ref[...] = jnp.zeros_like(ref)

    queries, grads, log_totals = q_ref[...], g_ref[...], l_ref[...]
    grad_queries = jnp.zeros(dq_ref.shape, jnp.float32)
    for head in range(LANES // head_size):
        chosen = lane_head == head
        head_queries = jnp.where(chosen, queries, jnp.zeros_like(queries))
        head_grads = jnp.where(chosen, grads, jnp.zeros_like(grads))
        log_total = log_totals[:, head * head_size : head * head_size + 1]
        probs, steps, totals = [], [], 0.0
        for k_ref, v_ref, count in ((k0_ref, v0_ref, kept[0]), (k1_ref, v1_ref, kept[1])):
            attn = jnp.exp2(head_scores(head_queries, k_ref[...], count) * exponent - log_total)
            step = outer_rows(head_grads, v_ref[...]) * attn
            totals = totals + jnp.sum(step, axis=1, keepdims=True)
            probs.append(attn)
            steps.append(step)
        outcome = 0.0
        for attn, step, k_ref, dk_ref, dv_ref in zip(
            probs, steps, (k0_ref, k1_ref), (dk0_ref, dk1_ref), (dv0_ref, dv1_ref)
        ):
            grad_logits = (step - attn * totals).astype(jnp.bfloat16)
            dv_ref[...] += inner_rows(attn.astype(jnp.bfloat16), head_grads)
            dk_ref[...] += inner_rows(grad_logits, head_queries) * scaling
            outcome = outcome + matmul(grad_logits, k_ref[...])
        grad_queries = jnp.where(chosen, outcome * scaling, grad_queries)
    dq_ref[...] = grad_queries.astype(dq_ref.dtype)


def attend_rows_back(queries, grads, log_totals, kv_near, kv_far, kept, num_heads, block_rows):
    row_count, width = queries.shape
    keys = kv_near.shape[0]
    groups = width // LANES
    masked = kept is not None
    if not masked:
        kept = jnp.zeros((2,), jnp.int32)
    row_spec = pl.BlockSpec((block_rows, LANES), lambda g, b, kept: (b, g))
    k_spec = pl.BlockSpec((keys, LANES), lambda g, b, kept: (0, g))
    v_spec = pl.BlockSpec((keys, LANES), lambda g, b, kept: (0, g + groups))
    key_shape = jax.ShapeDtypeStruct((keys, width), jnp.float32)
    return pl.pallas_call(
        functools.partial(attend_back_kernel, width // num_heads, masked),
        grid_spec=pltpu.PrefetchScalarGridSpec(
            num_scalar_prefetch=1,
            grid=(groups, row_count // block_rows),
            in_specs=[row_spec, row_spec, row_spec, k_spec, v_spec, k_spec, v_spec],
            out_specs=[row_spec, k_spec, k_spec, k_spec, k_spec],
        ),
        out_shape=[jax.ShapeDtypeStruct((row_count, width), jnp.bfloat16)] + [key_shape] * 4,
        compiler_params=pltpu.CompilerParams(vmem_limit_bytes=VMEM_LIMIT),
        cost_estimate=pl.CostEstimate(
            flops=20 * row_count * keys * width,
            bytes_accessed=8 * (row_count + 4 * keys) * width,
            transcendentals=2 * row_count * keys * num_heads,
        ),
    )(kept, queries, grads, log_totals, kv_near, kv_near, kv_far, kv_far)


def padded_rows(block, before, after):
    return jnp.pad(block, ((before, after), (0, 0)))


def scaled_back(stream, gain_vec, grad_out):
    discarded_value, backward_fn = jax.vjp(scaled, stream, gain_vec)
    return backward_fn(grad_out)


def feed_fwd(stream, gain_vec, w_up, w_down):
    normal_in = scaled(stream, gain_vec).astype(jnp.bfloat16)
    raised = matmul(normal_in, w_up)
    hidden = gelu_exact(raised).astype(jnp.bfloat16)
    return (stream + matmul(hidden, w_down), (normal_in, raised, hidden))


def feed_back(stream, gain_vec, w_up, w_down, stored, grad_out):
    normal_in, raised, hidden = stored
    branch_grad = grad_out.astype(jnp.bfloat16)
    grad_wdown = inner_rows(hidden, branch_grad)
    grad_hidden = outer_rows(branch_grad, w_down).astype(jnp.bfloat16).astype(jnp.float32)
    discarded_value, backward_fn = jax.vjp(gelu_exact, raised)
    grad_raised = backward_fn(grad_hidden)[0].astype(jnp.bfloat16)
    grad_wup = inner_rows(normal_in, grad_raised)
    grad_normal = outer_rows(grad_raised, w_up).astype(jnp.bfloat16).astype(jnp.float32)
    grad_stream, grad_gain = scaled_back(stream, gain_vec, grad_normal)
    return (grad_out + grad_stream, grad_wup, grad_wdown, grad_gain)


def swapped(block):
    devices = range(lax.axis_size("dp"))
    return lax.ppermute(block, "dp", [(i, i ^ 1) for i in devices])


def attend_fwd(stream, gain_vec, w_in, w_out, num_heads, kept, skip, block_rows):
    width = stream.shape[1]
    normal_in = scaled(stream, gain_vec).astype(jnp.bfloat16)
    kv_near = matmul(normal_in, w_in[:, width:]).astype(jnp.bfloat16)
    kv_far = swapped(kv_near)
    queries = matmul(normal_in[skip:], w_in[:, :width]).astype(jnp.bfloat16)
    merged, log_totals = attend_rows(queries, kv_near, kv_far, kept, num_heads, block_rows)
    outcome = stream[skip:] + matmul(merged, w_out)
    return (outcome, (normal_in, queries, kv_near, kv_far, merged, log_totals))


def attend_back(stream, gain_vec, w_in, w_out, num_heads, kept, skip, block_rows, stored, grad_out):
    normal_in, queries, kv_near, kv_far, merged, log_totals = stored
    branch_grad = grad_out.astype(jnp.bfloat16)
    grad_wout = inner_rows(merged, branch_grad)
    grad_merged = outer_rows(branch_grad, w_out).astype(jnp.bfloat16)
    dq, dk_near, dv_near, dk_far, dv_far = attend_rows_back(
        queries, grad_merged, log_totals, kv_near, kv_far, kept, num_heads, block_rows
    )
    dk = (dk_near + swapped(dk_far)).astype(jnp.bfloat16)
    dv = (dv_near + swapped(dv_far)).astype(jnp.bfloat16)
    grad_packed = jnp.concatenate([padded_rows(dq, skip, 0), dk, dv], axis=1)
    grad_win = inner_rows(normal_in, grad_packed)
    grad_normal = outer_rows(grad_packed, w_in).astype(jnp.bfloat16).astype(jnp.float32)
    grad_stream, grad_gain = scaled_back(stream, gain_vec, grad_normal)
    return (padded_rows(grad_out, skip, 0) + grad_stream, grad_win, grad_wout, grad_gain)


MESH = pl.DeviceIdType.MESH


def gather_kernel(count, zn, *refs):
    ins, outs = refs[:count], refs[count : 2 * count]
    local_sem, z_send, z_recv, p_send, p_recv = refs[2 * count :]
    section, place = lax.axis_index("section"), lax.axis_index("dp")
    z, core = place // 2, place % 2
    near = {"section": section + 1 - 2 * (section % 2)}
    far = {"section": (section + 2) % 4}
    mate = {"dp": place + 1 - 2 * core}
    ahead = {"dp": place + 2}
    behind = {"dp": place - 2}

    barrier = pltpu.get_barrier_semaphore()
    line = [{"dp": (z + j) % zn * 2 + core} for j in range(1, zn)]
    for other in [near, far, mate] + line:
        pl.semaphore_signal(barrier, inc=1, device_id=other, device_id_type=MESH)
    pl.semaphore_wait(barrier, 3 + len(line))

    def block(ref, a, owner_z, quarter=None, rows=None, owner_core=core):
        size = ins[a].shape[0]
        start, length = (0, size) if rows is None else rows
        offset = pl.multiple_of((owner_z * 2 + owner_core) * size + start, 16)
        if quarter is None:
            return ref.at[pl.ds(offset, length), :]
        width = ins[a].shape[1] // 4
        return ref.at[pl.ds(offset, length), pl.ds(pl.multiple_of(quarter * width, 128), width)]

    def own_quarter(a):
        width = ins[a].shape[1] // 4
        return ins[a].at[:, pl.ds(pl.multiple_of(section * width, 128), width)]

    def copy(src, dst, sends, recvs, index, device):
        return pltpu.make_async_remote_copy(
            src_ref=src,
            dst_ref=dst,
            send_sem=sends.at[index],
            recv_sem=recvs.at[index],
            device_id=device,
            device_id_type=MESH,
        )

    def along(a, step, upward):
        device = ahead if upward else behind
        source_z = z - (step - 1) if upward else z + (step - 1)
        src = own_quarter(a) if step == 1 else block(outs[a], a, source_z, section)
        index = (a * (zn - 1) + step - 1) * 2 + (0 if upward else 1)
        return copy(src, block(outs[a], a, source_z, section), z_send, z_recv, index, device)

    def sends_along(step, upward):
        if upward:
            return (z - (step - 1) >= 0) & (z < zn - 1)
        return (z + (step - 1) <= zn - 1) & (z > 0)

    def first_half(a):
        size = ins[a].shape[0]
        return (0, (size + 31) // 32 * 16)

    def second_half(a):
        size = ins[a].shape[0]
        start = (size + 31) // 32 * 16
        return (start, size - start)

    def in_plane(a, step, upward, kind):
        owner_z = z - step if upward else z + step
        index = ((a * (zn - 1) + step - 1) * 2 + (0 if upward else 1)) * 5 + kind
        x_quarter, y_quarter = near["section"], far["section"]
        part = [
            lambda: block(outs[a], a, owner_z, section),
            lambda: block(outs[a], a, owner_z, section),
            lambda: block(outs[a], a, owner_z, x_quarter, first_half(a)),
            lambda: block(outs[a], a, owner_z, y_quarter, second_half(a)),
            lambda: block(outs[a], a, owner_z),
        ][kind]()
        return copy(part, part, p_send, p_recv, index, (near, far, far, near, mate)[kind])

    own = []
    for a in range(count):
        for upward in (True, False):

            @pl.when(sends_along(1, upward))
            def _(a=a, upward=upward):
                along(a, 1, upward).start()

    for a in range(count):
        keep = pltpu.make_async_copy(ins[a], block(outs[a], a, z), local_sem.at[a])
        keep.start()
        base = count * (zn - 1) * 10
        give = copy(ins[a], block(outs[a], a, z), p_send, p_recv, base + a, mate)
        give.start()
        own.append((keep, give))

    items = [
        (a, step, upward)
        for step in range(1, zn)
        for a in range(count)
        for upward in (True, False)
    ]

    def arrives(step, upward):
        return z - step >= 0 if upward else z + step <= zn - 1

    def received(a, step, upward):
        @pl.when(arrives(step, upward))
        def _():
            along(a, step, upward).wait_recv()
            in_plane(a, step, upward, 0).start()
            in_plane(a, step, upward, 1).start()

        if step < zn - 1:

            @pl.when(arrives(step, upward) & sends_along(step + 1, upward))
            def _():
                along(a, step + 1, upward).start()

    def passed_on(a, step, upward):
        @pl.when(arrives(step, upward))
        def _():
            in_plane(a, step, upward, 0).wait_recv()
            in_plane(a, step, upward, 2).start()
            in_plane(a, step, upward, 1).wait_recv()
            in_plane(a, step, upward, 3).start()

    def completed(a, step, upward):
        @pl.when(arrives(step, upward))
        def _():
            in_plane(a, step, upward, 2).wait_recv()
            in_plane(a, step, upward, 3).wait_recv()
            in_plane(a, step, upward, 4).start()

    lag = 4
    for i in range(len(items) + 2 * lag):
        if i < len(items):
            received(*items[i])
        if 0 <= i - lag < len(items):
            passed_on(*items[i - lag])
        if 0 <= i - 2 * lag < len(items):
            completed(*items[i - 2 * lag])

    for keep, give in own:
        keep.wait()
        give.wait()
    for a, step, upward in items:

        @pl.when(sends_along(step, upward))
        def _(a=a, step=step, upward=upward):
            along(a, step, upward).wait_send()

        @pl.when(arrives(step, upward))
        def _(a=a, step=step, upward=upward):
            for kind in range(5):
                in_plane(a, step, upward, kind).wait_send()
            in_plane(a, step, upward, 4).wait_recv()


def gather_blocks(blocks):
    count = len(blocks)
    dp_size = lax.axis_size("dp")
    zn = dp_size // 2
    return pl.pallas_call(
        functools.partial(gather_kernel, count, zn),
        in_specs=[pl.BlockSpec(memory_space=pl.ANY)] * count,
        out_specs=[pl.BlockSpec(memory_space=pl.ANY)] * count,
        out_shape=[
            jax.ShapeDtypeStruct((member.shape[0] * dp_size, member.shape[1]), member.dtype)
            for member in blocks
        ],
        scratch_shapes=[
            pltpu.SemaphoreType.DMA((count,)),
            pltpu.SemaphoreType.DMA((count * (zn - 1) * 2,)),
            pltpu.SemaphoreType.DMA((count * (zn - 1) * 2,)),
            pltpu.SemaphoreType.DMA((count * ((zn - 1) * 10 + 1),)),
            pltpu.SemaphoreType.DMA((count * ((zn - 1) * 10 + 1),)),
        ],
        compiler_params=pltpu.CompilerParams(collective_id=0, has_side_effects=True),
    )(*blocks)


def upper_rows(size):
    return (size + 31) // 32 * 16


def add_blocks(rows, targets):
    def step(i, carried_through):
        at = pl.ds(pl.multiple_of(i * 16, 16), 16)
        for out, terms in targets:
            out[at, :] = sum(term[at, :].astype(jnp.float32) for term in terms).astype(out.dtype)
        return carried_through

    lax.fori_loop(0, rows // 16, step, 0)


def reduce_kernel(count, zn, *refs):
    ins, refs = refs[: count + 1], refs[count + 1 :]
    outs, refs = refs[: count + 1], refs[count + 1 :]
    whole, refs = refs[:count], refs[count:]
    near_one, refs = refs[:count], refs[count:]
    far_one, refs = refs[:count], refs[count:]
    far_two, refs = refs[:count], refs[count:]
    near_two, refs = refs[:count], refs[count:]
    along, refs = refs[:count], refs[count:]
    loaded, refs = refs[:count], refs[count:]
    held, refs = refs[:count], refs[count:]
    done, refs = refs[:count], refs[count:]
    total_ref, side_ref, line_ref, load_sem, move_send, move_recv, side_send, side_recv, line_send, line_recv = refs
    tally, out_total = ins[count], outs[count]
    tally_rows = out_total.shape[0]

    section, place = lax.axis_index("section"), lax.axis_index("dp")
    z, core = place // 2, place % 2
    x_quarter = section + 1 - 2 * (section % 2)
    y_quarter = (section + 2) % 4
    xy_quarter = (x_quarter + 2) % 4
    near, far = {"section": x_quarter}, {"section": y_quarter}
    mate = {"dp": place + 1 - 2 * core}
    sizes = [out.shape[0] for out in outs[:count]]
    widths = [out.shape[1] // 4 for out in outs[:count]]

    barrier = pltpu.get_barrier_semaphore()
    line = [{"dp": (z + j) % zn * 2 + core} for j in range(1, zn)]
    for other in [near, far, mate] + line:
        pl.semaphore_signal(barrier, inc=1, device_id=other, device_id_type=MESH)
    pl.semaphore_wait(barrier, 3 + len(line))

    def rows_at(a, slot, start=0, length=None):
        return pl.ds(pl.multiple_of(slot * sizes[a] + start, 16), sizes[a] if length is None else length)

    def quarter_at(a, quarter):
        return pl.ds(pl.multiple_of(quarter * widths[a], 128), widths[a])

    def upper(a):
        return upper_rows(sizes[a])

    def lower(a):
        return sizes[a] - upper_rows(sizes[a])

    def sent(src, dst, kind, a, slot, device):
        index = (kind * count + a) * (zn + 1) + slot
        return pltpu.make_async_remote_copy(
            src_ref=src,
            dst_ref=dst,
            send_sem=move_send.at[index],
            recv_sem=move_recv.at[index],
            device_id=device,
            device_id_type=MESH,
        )

    def load(a, owner_z):
        source = pl.ds(pl.multiple_of((owner_z * 2 + core) * sizes[a], 16), sizes[a])
        return pltpu.make_async_copy(
            ins[a].at[source, :], loaded[a], load_sem.at[a]
        )

    def give(a, owner_z):
        source = pl.ds(pl.multiple_of((owner_z * 2 + 1 - core) * sizes[a], 16), sizes[a])
        return sent(ins[a].at[source, :], whole[a].at[rows_at(a, owner_z), :], 0, a, owner_z, mate)

    def first_near(a, owner_z, which):
        quarter = (x_quarter, xy_quarter)[which]
        return sent(
            whole[a].at[rows_at(a, owner_z, 0, upper(a)), quarter_at(a, quarter)],
            near_one[a].at[pl.ds(pl.multiple_of((owner_z * 2 + which) * upper(a), 16), upper(a)), :],
            1 + which, a, owner_z, near,
        )

    def first_far(a, owner_z, which):
        quarter = (y_quarter, xy_quarter)[which]
        return sent(
            whole[a].at[rows_at(a, owner_z, upper(a), lower(a)), quarter_at(a, quarter)],
            far_one[a].at[pl.ds(pl.multiple_of((owner_z * 2 + which) * lower(a), 16), lower(a)), :],
            3 + which, a, owner_z, far,
        )

    def second_far(a, owner_z):
        return sent(
            whole[a].at[rows_at(a, owner_z, 0, upper(a)), quarter_at(a, y_quarter)],
            far_two[a].at[pl.ds(pl.multiple_of(owner_z * upper(a), 16), upper(a)), :],
            5, a, owner_z, far,
        )

    def second_near(a, owner_z):
        return sent(
            whole[a].at[rows_at(a, owner_z, upper(a), lower(a)), quarter_at(a, x_quarter)],
            near_two[a].at[pl.ds(pl.multiple_of(owner_z * lower(a), 16), lower(a)), :],
            6, a, owner_z, near,
        )

    def onward(a, owner_z, upward, last):
        slot = zn if last and not upward else owner_z
        return sent(
            held[a].at[rows_at(a, owner_z), :],
            along[a].at[rows_at(a, slot), :],
            7, a, slot, {"dp": place + 2 if upward else place - 2},
        )

    def finished(a, kind):
        quarter = (section, section, x_quarter, y_quarter)[kind]
        columns = quarter_at(a, quarter)
        part = (
            pl.ds(0, sizes[a]), pl.ds(0, sizes[a]), pl.ds(0, upper(a)), pl.ds(upper(a), lower(a))
        )[kind]
        src = done[a] if kind < 2 else outs[a].at[part, columns]
        return sent(src, outs[a].at[part, columns], 8 + kind, a, 0, (near, far, far, near)[kind])

    def keep(a):
        return pltpu.make_async_copy(
            done[a], outs[a].at[:, quarter_at(a, section)], load_sem.at[a]
        )

    legs = [(k, upward) for k in range(zn - 1, 0, -1) for upward in (True, False)] + [(0, True)]
    items = [(a, leg) for leg in range(len(legs)) for a in range(count)]

    def owner_of(leg):
        k, upward = legs[leg]
        return z + k if upward else z - k

    def is_live(leg):
        k, upward = legs[leg]
        return (z + k <= zn - 1) if upward else (z - k >= 0)

    def started(a, leg):
        @pl.when(is_live(leg))
        def _():
            give(a, owner_of(leg)).start()

    def load_started(a, leg):
        @pl.when(is_live(leg))
        def _():
            load(a, owner_of(leg)).start()

    def paired(a, leg):
        @pl.when(is_live(leg))
        def _():
            owner_z = owner_of(leg)
            load(a, owner_z).wait()
            give(a, owner_z).wait_recv()
            target = whole[a].at[rows_at(a, owner_z), :]
            add_blocks(sizes[a], [(target, (target, loaded[a]))])
            for which in (1, 0):
                first_near(a, owner_z, which).start()
                first_far(a, owner_z, which).start()

        if leg + 1 < len(legs):
            load_started(a, leg + 1)

    def from_near(a, owner_z, which):
        start = pl.multiple_of((owner_z * 2 + which) * upper(a), 16)
        return near_one[a].at[pl.ds(start, upper(a)), :]

    def from_far(a, owner_z, which):
        start = pl.multiple_of((owner_z * 2 + which) * lower(a), 16)
        return far_one[a].at[pl.ds(start, lower(a)), :]

    def halved(a, leg):
        @pl.when(is_live(leg))
        def _():
            owner_z = owner_of(leg)
            first_near(a, owner_z, 1).wait_recv()
            target = whole[a].at[rows_at(a, owner_z, 0, upper(a)), quarter_at(a, y_quarter)]
            add_blocks(upper(a), [(target, (target, from_near(a, owner_z, 1)))])
            second_far(a, owner_z).start()
            first_far(a, owner_z, 1).wait_recv()
            target = whole[a].at[
                rows_at(a, owner_z, upper(a), lower(a)), quarter_at(a, x_quarter)
            ]
            add_blocks(lower(a), [(target, (target, from_far(a, owner_z, 1)))])
            second_near(a, owner_z).start()

    def quartered(a, leg):
        k, upward = legs[leg]

        @pl.when(is_live(leg))
        def _():
            owner_z = owner_of(leg)
            own = quarter_at(a, section)
            first_near(a, owner_z, 0).wait_recv()
            second_far(a, owner_z).wait_recv()
            add_blocks(
                upper(a),
                [
                    (
                        held[a].at[rows_at(a, owner_z, 0, upper(a)), :],
                        (
                            whole[a].at[rows_at(a, owner_z, 0, upper(a)), own],
                            from_near(a, owner_z, 0),
                            far_two[a].at[
                                pl.ds(pl.multiple_of(owner_z * upper(a), 16), upper(a)), :
                            ],
                        ),
                    )
                ],
            )
            first_far(a, owner_z, 0).wait_recv()
            second_near(a, owner_z).wait_recv()
            add_blocks(
                lower(a),
                [
                    (
                        held[a].at[rows_at(a, owner_z, upper(a), lower(a)), :],
                        (
                            whole[a].at[rows_at(a, owner_z, upper(a), lower(a)), own],
                            from_far(a, owner_z, 0),
                            near_two[a].at[
                                pl.ds(pl.multiple_of(owner_z * lower(a), 16), lower(a)), :
                            ],
                        ),
                    )
                ],
            )
            target = held[a].at[rows_at(a, owner_z), :]

            def join(upward_from, slot):
                onward(a, owner_z, upward_from, slot is not owner_z or k == 0).wait_recv()
                add_blocks(sizes[a], [(target, (target, along[a].at[rows_at(a, slot), :]))])

            if k > 0:

                @pl.when(z > 0 if upward else z < zn - 1)
                def _():
                    join(upward, owner_z)

                onward(a, owner_z, upward, k == 1).start()
            else:

                @pl.when(z > 0)
                def _():
                    join(True, owner_z)

                @pl.when(z < zn - 1)
                def _():
                    join(False, zn)

                def settle(i, carried_through):
                    at = pl.ds(pl.multiple_of(i * 16, 16), 16)
                    values = target[at, :]
                    done[a][at, :] = values.astype(done[a].dtype)
                    squares = values * values
                    squares = squares[:8] + squares[8:]
                    carried = total_ref[0:8, :]
                    for column in range(0, widths[a], 128):
                        carried = carried + squares[:, column : column + 128]
                    total_ref[0:8, :] = carried
                    return carried_through

                lax.fori_loop(0, sizes[a] // 16, settle, 0)
                keep(a).start()
                finished(a, 0).start()
                finished(a, 1).start()

    total_ref[0:8, :] = jnp.zeros((8, 128), jnp.float32)
    tally_copy = pltpu.make_async_copy(tally, total_ref.at[8:, :], load_sem.at[count])
    tally_copy.start()
    for a, leg in items[:count]:
        load_started(a, leg)
    for a, leg in items:
        started(a, leg)
    lag = 4
    for i in range(len(items) + 2 * lag):
        if i < len(items):
            paired(*items[i])
        if 0 <= i - lag < len(items):
            halved(*items[i - lag])
        if 0 <= i - 2 * lag < len(items):
            quartered(*items[i - 2 * lag])

    tally_copy.wait()

    def exchanged(stage, device):
        return pltpu.make_async_remote_copy(
            src_ref=total_ref,
            dst_ref=side_ref.at[pl.ds(stage * tally_rows, tally_rows), :],
            send_sem=side_send.at[stage],
            recv_sem=side_recv.at[stage],
            device_id=device,
            device_id_type=MESH,
        )

    for stage, device in enumerate((mate, near, far)):
        swap = exchanged(stage, device)
        swap.start()
        swap.wait()
        total_ref[...] += side_ref[stage * tally_rows : (stage + 1) * tally_rows, :]

    def told(from_z, to_z, j):
        index = from_z * zn + to_z
        return pltpu.make_async_remote_copy(
            src_ref=total_ref,
            dst_ref=line_ref.at[pl.ds(pl.multiple_of(from_z * tally_rows, 8), tally_rows), :],
            send_sem=line_send.at[index],
            recv_sem=line_recv.at[index],
            device_id={"dp": to_z * 2 + core},
            device_id_type=MESH,
        )

    for j in range(1, zn):
        told(z, (z + j) % zn, j).start()
    line_ref[pl.ds(pl.multiple_of(z * tally_rows, 8), tally_rows), :] = total_ref[...]
    for j in range(1, zn):
        told((z + j) % zn, z, j).wait_recv()
    grand = line_ref[0:tally_rows, :]
    for j in range(1, zn):
        grand = grand + line_ref[j * tally_rows : (j + 1) * tally_rows, :]
    for j in range(1, zn):
        told(z, (z + j) % zn, j).wait_send()
    total_ref[...] = grand
    show = pltpu.make_async_copy(total_ref, out_total, load_sem.at[count])
    show.start()

    for a in range(count):
        finished(a, 0).wait_recv()
        finished(a, 2).start()
        finished(a, 1).wait_recv()
        finished(a, 3).start()
    for a in range(count):
        keep(a).wait()
        finished(a, 2).wait_recv()
        finished(a, 3).wait_recv()
        for kind in range(4):
            finished(a, kind).wait_send()
    for a, leg in items:
        k, upward = legs[leg]

        @pl.when(is_live(leg))
        def _(a=a, leg=leg, k=k, upward=upward):
            owner_z = owner_of(leg)
            give(a, owner_z).wait_send()
            for which in (0, 1):
                first_near(a, owner_z, which).wait_send()
                first_far(a, owner_z, which).wait_send()
            second_near(a, owner_z).wait_send()
            second_far(a, owner_z).wait_send()
            if k > 0:
                onward(a, owner_z, upward, k == 1).wait_send()

    show.wait()


def reduce_blocks(blocks, tally, result_types):
    count = len(blocks)
    dp_size = lax.axis_size("dp")
    zn = dp_size // 2
    tally_rows = 8 + tally.shape[0]
    shapes = [(member.shape[0] // dp_size, member.shape[1]) for member in blocks]
    vmem = lambda rows, columns, dtype=jnp.bfloat16: pltpu.VMEM((rows, columns), dtype)
    anywhere = pl.BlockSpec(memory_space=pl.ANY)
    moves = 12 * count * (zn + 1)
    return pl.pallas_call(
        functools.partial(reduce_kernel, count, zn),
        in_specs=[anywhere] * (count + 1),
        out_specs=[anywhere] * (count + 1),
        out_shape=[jax.ShapeDtypeStruct(shape, kind) for shape, kind in zip(shapes, result_types)]
        + [jax.ShapeDtypeStruct((tally_rows, 128), jnp.float32)],
        scratch_shapes=[vmem(zn * r, w) for r, w in shapes]
        + [vmem(zn * 2 * upper_rows(r), w // 4) for r, w in shapes]
        + [vmem(zn * 2 * (r - upper_rows(r)), w // 4) for r, w in shapes]
        + [vmem(zn * upper_rows(r), w // 4) for r, w in shapes]
        + [vmem(zn * (r - upper_rows(r)), w // 4) for r, w in shapes]
        + [vmem((zn + 1) * r, w // 4, jnp.float32) for r, w in shapes]
        + [vmem(r, w) for r, w in shapes]
        + [vmem(zn * r, w // 4, jnp.float32) for r, w in shapes]
        + [vmem(r, w // 4, kind) for (r, w), kind in zip(shapes, result_types)]
        + [
            vmem(tally_rows, 128, jnp.float32),
            vmem(3 * tally_rows, 128, jnp.float32),
            vmem(zn * tally_rows, 128, jnp.float32),
            pltpu.SemaphoreType.DMA((count + 1,)),
            pltpu.SemaphoreType.DMA((moves,)),
            pltpu.SemaphoreType.DMA((moves,)),
            pltpu.SemaphoreType.DMA((3,)),
            pltpu.SemaphoreType.DMA((3,)),
            pltpu.SemaphoreType.DMA((zn * zn,)),
            pltpu.SemaphoreType.DMA((zn * zn,)),
        ],
        compiler_params=pltpu.CompilerParams(
            collective_id=1, has_side_effects=True, vmem_limit_bytes=58 * 1024 * 1024
        ),
    )(*blocks, tally)


def adamw_step(weight, grad_now, first, second, decay, rate):
    first = BETA_ONE * first + (1.0 - BETA_ONE) * grad_now
    second = BETA_TWO * second + (1.0 - BETA_TWO) * grad_now * grad_now
    ratio = first / (1.0 - BETA_ONE**STEP) / (jnp.sqrt(second / (1.0 - BETA_TWO**STEP)) + EPSILON)
    return (weight - rate * (ratio + decay * weight), first, second)


def local(
    pixels,
    token_order,
    visible,
    wide_weight,
    tall_weight,
    pred_weight,
    pred_down,
    enc_gains,
    pred_gains,
    wide_first,
    tall_first,
    pred_first,
    pred_down_first,
    enc_gains_first,
    pred_gains_first,
    wide_second,
    tall_second,
    pred_second,
    pred_down_second,
    enc_gains_second,
    pred_gains_second,
    teacher_wide,
    teacher_tall,
    teacher_gains,
):
    masters = (wide_weight, tall_weight, pred_weight, pred_down, enc_gains, pred_gains)
    section_idx = lax.axis_index("section")
    section_count = lax.axis_size("section")
    core = lax.axis_index("dp") % 2
    clips_here = pixels.shape[0]
    assert section_count == 2 * clips_here

    owner = section_idx // clips_here
    clip = section_idx % clips_here
    holds = core == owner
    counts_own = lax.dynamic_index_in_dim(visible, clip, 0)
    order_own = lax.dynamic_index_in_dim(token_order, clip, 0, keepdims=False)
    clip_facts = jnp.concatenate([order_own, counts_own])
    clip_facts = jnp.where(holds, clip_facts, swapped(clip_facts))
    seen = clip_facts[L]
    order_pairs = clip_facts[:L].reshape(HALF, 2)
    order = jnp.where(core == 0, order_pairs[:, 0], order_pairs[:, 1])
    pairs_own = order_own.reshape(HALF, 2)
    order_here = jnp.where(core == 0, pairs_own[:, 0], pairs_own[:, 1])
    order_there = jnp.where(core == 0, pairs_own[:, 1], pairs_own[:, 0])
    pixel_rows = pixels.reshape(clips_here * L, PATCH)
    for_here = pixel_rows[order_here + clip * L]
    for_there = pixel_rows[order_there + clip * L]
    chosen = jnp.where(holds, for_here, swapped(for_there))
    seen_near = (seen - core + 1) // 2
    seen_far = (seen + core) // 2
    kept = jnp.stack([seen_near, seen_far])
    visible_high, visible_low = visible // LANES, visible % LANES
    dp_size = lax.axis_size("dp")
    row_count = wide_weight.shape[0]
    small = jnp.concatenate(
        [
            wide_weight[:, 4 * D + FF :],
            enc_gains,
            teacher_gains,
            jnp.pad(pred_gains, ((0, row_count - pred_gains.shape[0]), (0, 0))),
            jnp.zeros((row_count, LANES - 10 - 2 * clips_here), jnp.float32),
            jnp.broadcast_to(
                jnp.concatenate([visible_high, visible_low]).astype(jnp.float32)[None, :],
                (row_count, 2 * clips_here),
            ),
        ],
        axis=1,
    )
    blocks = (
        teacher_wide,
        teacher_tall,
        wide_weight[:, : 4 * D + FF],
        tall_weight,
        pred_weight.reshape(-1, D),
        small,
        jnp.pad(pred_down, ((0, 0), (0, LANES))),
    )
    teach_wide, teach_tall, w_wide, w_tall, w_pred, w_small, w_down = gather_blocks(
        tuple(member.astype(jnp.bfloat16) for member in blocks)
    )
    w_pred = w_pred.reshape(PD, -1)
    w_down = w_down[:, :PD]
    pred_embed = w_small[:, :PD]
    enc_copy = w_small[:, PD : PD + 3]
    teach_copy = w_small[:, PD + 3 : PD + 6]
    pred_copy = w_small[:, PD + 6 : PD + 10].reshape(dp_size, row_count, 4)
    pred_copy = pred_copy[:, : pred_gains.shape[0]].reshape(PD, 4)
    counts = w_small[::row_count, PD + LANES - 2 * clips_here :].astype(jnp.float32)
    counts = counts[:, :clips_here] * LANES + counts[:, clips_here:]
    target_total = jnp.sum(L - counts)
    enc_gain = enc_copy.astype(jnp.float32)
    pred_gain = pred_copy.astype(jnp.float32)
    teach_gain = teach_copy.astype(jnp.float32)
    enc_attn = (w_wide[:, : 3 * D], w_wide[:, 3 * D : 4 * D])
    enc_feed = (w_wide[:, 4 * D : 4 * D + FF], w_tall[PATCH:])
    pred_attn = (w_pred[:, : 3 * PD], w_pred[:, 3 * PD : 4 * PD])
    pred_feed = (w_pred[:, 4 * PD : 4 * PD + PF], w_down)
    pred_head = w_pred[:, 4 * PD + PF :]

    table = position_table(order, D)
    pred_table = position_table(order, PD)
    row_ids = lax.iota(jnp.int32, HALF)
    context = (row_ids < seen_near)[:, None]

    teach_stream = matmul(chosen, teach_tall[:PATCH]) + table
    teach_stream, discarded_value = attend_fwd(
        teach_stream, teach_gain[:, 0], teach_wide[:, : 3 * D], teach_wide[:, 3 * D : 4 * D],
        HE, None, SKIP, 336,
    )
    teach_stream = teach_stream.astype(jnp.bfloat16).astype(jnp.float32)
    teach_stream, discarded_value = feed_fwd(
        teach_stream, teach_gain[:, 1], teach_wide[:, 4 * D :], teach_tall[PATCH:]
    )
    goal = normed(scaled(teach_stream, teach_gain[:, 2])).astype(jnp.bfloat16).astype(jnp.float32)

    enc_chosen = chosen[:SEEN]
    stream_a = matmul(enc_chosen, w_tall[:PATCH]) + table[:SEEN]
    stream_b, stored_a = attend_fwd(
        stream_a, enc_gain[:, 0], enc_attn[0], enc_attn[1], HE, kept, 0, SEEN
    )
    stream_b = stream_b.astype(jnp.bfloat16).astype(jnp.float32)
    stream_c, stored_b = feed_fwd(stream_b, enc_gain[:, 1], enc_feed[0], enc_feed[1])
    encoded = scaled(stream_c, enc_gain[:, 2]).astype(jnp.bfloat16)

    projected = padded_rows(matmul(encoded, pred_embed), 0, HALF - SEEN)
    stream_d = jnp.where(context, projected, pred_gain[:, 3][None, :]) + pred_table
    stream_e, stored_d = attend_fwd(
        stream_d, pred_gain[:, 0], pred_attn[0], pred_attn[1], PH, None, SKIP, 336
    )
    stream_e = stream_e.astype(jnp.bfloat16).astype(jnp.float32)
    stream_f, stored_e = feed_fwd(stream_e, pred_gain[:, 1], pred_feed[0], pred_feed[1])
    final = scaled(stream_f, pred_gain[:, 2]).astype(jnp.bfloat16)
    residual = matmul(final, pred_head) - goal
    smooth_err = jnp.sqrt(residual * residual + 1.0)
    target_mask = jnp.logical_not(context[SKIP:])
    loss_part = jnp.sum(jnp.where(target_mask, smooth_err - 1.0, 0.0))
    grad_guess = (jnp.where(target_mask, residual / smooth_err, 0.0) / target_total).astype(
        jnp.bfloat16
    )

    grad_head = inner_rows(final, grad_guess)
    grad_final = outer_rows(grad_guess, pred_head).astype(jnp.bfloat16).astype(jnp.float32)
    grad_stream, grad_pg2 = scaled_back(stream_f, pred_gain[:, 2], grad_final)
    grad_stream, grad_pup, grad_down, grad_pg1 = feed_back(
        stream_e, pred_gain[:, 1], pred_feed[0], pred_feed[1], stored_e, grad_stream
    )
    grad_stream = grad_stream.astype(jnp.bfloat16).astype(jnp.float32)
    grad_stream, grad_pin, grad_pout, grad_pg0 = attend_back(
        stream_d, pred_gain[:, 0], pred_attn[0], pred_attn[1], PH, None, SKIP, 336, stored_d, grad_stream
    )
    grad_token = jnp.sum(jnp.where(context, 0.0, grad_stream), axis=0)
    grad_projected = jnp.where(context, grad_stream, 0.0)[:SEEN].astype(jnp.bfloat16)
    grad_embed = inner_rows(encoded, grad_projected)
    grad_encoded = outer_rows(grad_projected, pred_embed).astype(jnp.bfloat16).astype(jnp.float32)
    grad_stream, grad_eg2 = scaled_back(stream_c, enc_gain[:, 2], grad_encoded)
    grad_stream, grad_eup, grad_edown, grad_eg1 = feed_back(
        stream_b, enc_gain[:, 1], enc_feed[0], enc_feed[1], stored_b, grad_stream
    )
    grad_stream = grad_stream.astype(jnp.bfloat16).astype(jnp.float32)
    grad_stream, grad_ein, grad_eout, grad_eg0 = attend_back(
        stream_a, enc_gain[:, 0], enc_attn[0], enc_attn[1], HE, kept, 0, SEEN, stored_a, grad_stream
    )
    grad_patch = inner_rows(enc_chosen, grad_stream.astype(jnp.bfloat16))

    gain_grads = jnp.concatenate(
        [
            jnp.stack([grad_eg0, grad_eg1, grad_eg2], axis=1).reshape(-1, LANES),
            jnp.stack([grad_pg0, grad_pg1, grad_pg2, grad_token], axis=1).reshape(-1, LANES),
        ],
        axis=0,
    )
    gain_rows = 3 * D // LANES
    loss_tile = jnp.zeros((8, LANES), jnp.float32).at[0, 0].set(loss_part)
    tally = jnp.concatenate(
        [loss_tile, gain_grads, jnp.zeros((4, LANES), jnp.float32)], axis=0
    )
    blocks = shortened(
        (
            grad_ein,
            grad_eout,
            grad_eup,
            jnp.pad(grad_embed, ((0, 0), (0, LANES))),
            jnp.concatenate(shortened([grad_patch, grad_edown]), axis=0),
            jnp.concatenate(shortened([grad_pin, grad_pout, grad_pup, grad_head]), axis=1).reshape(-1, D),
            jnp.pad(grad_down, ((0, 0), (0, LANES))),
        )
    )
    *summed, tally = reduce_blocks(
        blocks, tally, [jnp.bfloat16] * 5 + [jnp.float32] * 2
    )
    wide_parts = [summed[0], summed[1], summed[2], summed[3][:, :PD]]
    place = lax.axis_index("dp")
    gains_all = tally[16 : 16 + gain_rows].reshape(D, 3)
    pred_gains_all = tally[16 + gain_rows : 16 + gain_rows + 4 * PD // LANES].reshape(PD, 4)
    shares = (
        jnp.concatenate(wide_parts, axis=1).astype(jnp.float32),
        summed[4].astype(jnp.float32),
        summed[5].reshape(pred_weight.shape).astype(jnp.float32),
        summed[6][:, :PD].astype(jnp.float32),
        lax.dynamic_slice_in_dim(gains_all, place * enc_gains.shape[0], enc_gains.shape[0], 0),
        lax.dynamic_slice_in_dim(pred_gains_all, place * pred_gains.shape[0], pred_gains.shape[0], 0),
    )
    loss_sum = tally[8, 0]
    square_total = jnp.sum(tally[:8]) + jnp.sum(jnp.square(tally[16:]))
    grad_norm = jnp.sqrt(square_total)
    factor = jnp.minimum(1.0, CLIP_AT / (grad_norm + 1e-06))
    firsts = (
        wide_first,
        tall_first,
        pred_first,
        pred_down_first,
        enc_gains_first,
        pred_gains_first,
    )
    seconds = (
        wide_second,
        tall_second,
        pred_second,
        pred_down_second,
        enc_gains_second,
        pred_gains_second,
    )
    decays = (DECAY, DECAY, DECAY, DECAY, 0.0, 0.0)
    rates = (RATE, RATE, RATE, RATE, GAIN_RATE, GAIN_RATE)
    results = [
        adamw_step(
            masters[group_idx],
            shares[group_idx] * factor,
            firsts[group_idx],
            seconds[group_idx],
            decays[group_idx],
            rates[group_idx],
        )
        for group_idx in range(6)
    ]
    news = [entry[0] for entry in results]
    teacher_wide_new = KEEP_RATE * teacher_wide + (1.0 - KEEP_RATE) * news[0][:, : 4 * D + FF]
    teacher_tall_new = KEEP_RATE * teacher_tall + (1.0 - KEEP_RATE) * news[1]
    teacher_gains_new = KEEP_RATE * teacher_gains + (1.0 - KEEP_RATE) * news[4]
    return (
        loss_sum,
        target_total,
        grad_norm,
        news[0],
        news[1],
        news[2],
        news[3],
        news[4],
        news[5],
        results[0][1],
        results[1][1],
        results[2][1],
        results[3][1],
        results[4][1],
        results[5][1],
        results[0][2],
        results[1][2],
        results[2][2],
        results[3][2],
        results[4][2],
        results[5][2],
        news[0].astype(jnp.bfloat16),
        news[1].astype(jnp.bfloat16),
        news[2].astype(jnp.bfloat16),
        news[3].astype(jnp.bfloat16),
        news[4].astype(jnp.bfloat16),
        news[5].astype(jnp.bfloat16),
        teacher_wide_new,
        teacher_tall_new,
        teacher_gains_new,
    )


def solution(mesh):
    return jax.shard_map(
        local,
        mesh=mesh,
        in_specs=(
            P("dp", None, None),
            P("dp", None),
            P("dp"),
            P("dp", None),
            P("dp", None),
            P("dp", None),
            P("dp", None),
            P("dp", None),
            P("dp", None),
            P("dp", None),
            P("dp", None),
            P("dp", None),
            P("dp", None),
            P("dp", None),
            P("dp", None),
            P("dp", None),
            P("dp", None),
            P("dp", None),
            P("dp", None),
            P("dp", None),
            P("dp", None),
            P("dp", None),
            P("dp", None),
            P("dp", None),
        ),
        out_specs=(
            P(),
            P(),
            P(),
            P("dp", None),
            P("dp", None),
            P("dp", None),
            P("dp", None),
            P("dp", None),
            P("dp", None),
            P("dp", None),
            P("dp", None),
            P("dp", None),
            P("dp", None),
            P("dp", None),
            P("dp", None),
            P("dp", None),
            P("dp", None),
            P("dp", None),
            P("dp", None),
            P("dp", None),
            P("dp", None),
            P("dp", None),
            P("dp", None),
            P("dp", None),
            P("dp", None),
            P("dp", None),
            P("dp", None),
            P("dp", None),
            P("dp", None),
            P("dp", None),
        ),
        check_vma=False,
    )
```

```python
import functools
import math

import jax
import jax.numpy as jnp
from jax import lax
from jax.experimental import pallas as pl
from jax.experimental.pallas import tpu as pltpu
from jax.sharding import PartitionSpec as P

D = 1024
HE = 16
FF = 4096
PD = 384
PH = 12
PF = 1536
PATCH = 1536
L = 1536
STEP = 10
VIS = 576
VIS_LO = 192
HALF = L // 2
SEEN = VIS // 2
SKIP = VIS_LO // 2
LANES = 128
VMEM_LIMIT = 50 * 1024 * 1024


BETA_ONE = 0.9
BETA_TWO = 0.999
EPSILON = 1e-08
RATE = 0.02
GAIN_RATE = 0.5
DECAY = 0.05
CLIP_AT = 0.05
KEEP_RATE = 0.8
NEGATIVE = -1e30


def shortened(x):
    return jax.tree.map(lambda a: a.astype(jnp.bfloat16) if a.dtype == jnp.float32 else a, x)


def normed(stream):
    centred = stream - jnp.mean(stream, axis=-1, keepdims=True)
    return centred * lax.rsqrt(jnp.mean(centred * centred, axis=-1, keepdims=True) + 1e-06)


def scaled(stream, gain_vec):
    return normed(stream) * gain_vec


def position_table(positions, feature_width):
    frequency = jnp.exp(
        jnp.arange(feature_width // 2, dtype=jnp.float32)
        * (-2.0 * math.log(10000.0) / feature_width)
    )
    angles = positions.astype(jnp.float32)[:, None] * frequency[None, :]
    return jnp.concatenate([jnp.sin(angles), jnp.cos(angles)], axis=1)


def matmul(left, right):
    return jnp.dot(left, right, preferred_element_type=jnp.float32)


def inner_rows(left, right):
    return lax.dot_general(
        left, right, (((0,), (0,)), ((), ())), preferred_element_type=jnp.float32
    )


def outer_rows(left, right):
    return lax.dot_general(
        left, right, (((1,), (1,)), ((), ())), preferred_element_type=jnp.float32
    )


def head_scores(queries, key_heads, kept):
    logits = outer_rows(queries, key_heads)
    if kept is None:
        return logits
    key_ids = lax.broadcasted_iota(jnp.int32, logits.shape, 1)
    return jnp.where(key_ids < kept, logits, NEGATIVE)


def attend_kernel(head_size, masked, kept_ref, q_ref, k0_ref, v0_ref, k1_ref, v1_ref, o_ref, l_ref):
    exponent = head_size ** (-0.5) * math.log2(math.e)
    lane_head = lax.broadcasted_iota(jnp.int32, (1, LANES), 1) // head_size
    kept = (kept_ref[0], kept_ref[1]) if masked else (None, None)
    queries = q_ref[...]
    merged = jnp.zeros(o_ref.shape, jnp.float32)
    log_totals = jnp.zeros(o_ref.shape, jnp.float32)
    for head in range(LANES // head_size):
        chosen = lane_head == head
        head_queries = jnp.where(chosen, queries, jnp.zeros_like(queries))
        near = head_scores(head_queries, k0_ref[...], kept[0])
        far = head_scores(head_queries, k1_ref[...], kept[1])
        row_max = exponent * jnp.maximum(
            jnp.max(near, axis=1, keepdims=True), jnp.max(far, axis=1, keepdims=True)
        )
        near = jnp.exp2(near * exponent - row_max)
        far = jnp.exp2(far * exponent - row_max)
        row_total = jnp.sum(near, axis=1, keepdims=True) + jnp.sum(far, axis=1, keepdims=True)
        outcome = matmul(near.astype(jnp.bfloat16), v0_ref[...]) + matmul(
            far.astype(jnp.bfloat16), v1_ref[...]
        )
        merged = jnp.where(chosen, outcome / row_total, merged)
        log_totals = jnp.where(chosen, row_max + jnp.log2(row_total), log_totals)
    o_ref[...] = merged.astype(o_ref.dtype)
    l_ref[...] = log_totals


def attend_rows(queries, kv_near, kv_far, kept, num_heads, block_rows):
    row_count, width = queries.shape
    keys = kv_near.shape[0]
    groups = width // LANES
    masked = kept is not None
    if not masked:
        kept = jnp.zeros((2,), jnp.int32)
    row_spec = pl.BlockSpec((block_rows, LANES), lambda g, b, kept: (b, g))
    k_spec = pl.BlockSpec((keys, LANES), lambda g, b, kept: (0, g))
    v_spec = pl.BlockSpec((keys, LANES), lambda g, b, kept: (0, g + groups))
    return pl.pallas_call(
        functools.partial(attend_kernel, width // num_heads, masked),
        grid_spec=pltpu.PrefetchScalarGridSpec(
            num_scalar_prefetch=1,
            grid=(groups, row_count // block_rows),
            in_specs=[row_spec, k_spec, v_spec, k_spec, v_spec],
            out_specs=[row_spec, row_spec],
        ),
        out_shape=[
            jax.ShapeDtypeStruct((row_count, width), jnp.bfloat16),
            jax.ShapeDtypeStruct((row_count, width), jnp.float32),
        ],
        compiler_params=pltpu.CompilerParams(vmem_limit_bytes=VMEM_LIMIT),
        cost_estimate=pl.CostEstimate(
            flops=8 * row_count * keys * width,
            bytes_accessed=8 * (row_count + keys) * width,
            transcendentals=2 * row_count * keys * num_heads,
        ),
    )(kept, queries, kv_near, kv_near, kv_far, kv_far)


def attend_back_kernel(
    head_size, masked, kept_ref, q_ref, g_ref, l_ref, k0_ref, v0_ref, k1_ref, v1_ref,
    dq_ref, dk0_ref, dv0_ref, dk1_ref, dv1_ref,
):
    scaling = head_size ** (-0.5)
    exponent = scaling * math.log2(math.e)
    lane_head = lax.broadcasted_iota(jnp.int32, (1, LANES), 1) // head_size
    kept = (kept_ref[0], kept_ref[1]) if masked else (None, None)

    @pl.when(pl.program_id(1) == 0)
    def _():
        for ref in (dk0_ref, dv0_ref, dk1_ref, dv1_ref):
            ref[...] = jnp.zeros_like(ref)

    queries, grads, log_totals = q_ref[...], g_ref[...], l_ref[...]
    grad_queries = jnp.zeros(dq_ref.shape, jnp.float32)
    for head in range(LANES // head_size):
        chosen = lane_head == head
        head_queries = jnp.where(chosen, queries, jnp.zeros_like(queries))
        head_grads = jnp.where(chosen, grads, jnp.zeros_like(grads))
        log_total = log_totals[:, head * head_size : head * head_size + 1]
        probs, steps, totals = [], [], 0.0
        for k_ref, v_ref, count in ((k0_ref, v0_ref, kept[0]), (k1_ref, v1_ref, kept[1])):
            attn = jnp.exp2(head_scores(head_queries, k_ref[...], count) * exponent - log_total)
            step = outer_rows(head_grads, v_ref[...]) * attn
            totals = totals + jnp.sum(step, axis=1, keepdims=True)
            probs.append(attn)
            steps.append(step)
        outcome = 0.0
        for attn, step, k_ref, dk_ref, dv_ref in zip(
            probs, steps, (k0_ref, k1_ref), (dk0_ref, dk1_ref), (dv0_ref, dv1_ref)
        ):
            grad_logits = (step - attn * totals).astype(jnp.bfloat16)
            dv_ref[...] += inner_rows(attn.astype(jnp.bfloat16), head_grads)
            dk_ref[...] += inner_rows(grad_logits, head_queries) * scaling
            outcome = outcome + matmul(grad_logits, k_ref[...])
        grad_queries = jnp.where(chosen, outcome * scaling, grad_queries)
    dq_ref[...] = grad_queries.astype(dq_ref.dtype)


def attend_rows_back(queries, grads, log_totals, kv_near, kv_far, kept, num_heads, block_rows):
    row_count, width = queries.shape
    keys = kv_near.shape[0]
    groups = width // LANES
    masked = kept is not None
    if not masked:
        kept = jnp.zeros((2,), jnp.int32)
    row_spec = pl.BlockSpec((block_rows, LANES), lambda g, b, kept: (b, g))
    k_spec = pl.BlockSpec((keys, LANES), lambda g, b, kept: (0, g))
    v_spec = pl.BlockSpec((keys, LANES), lambda g, b, kept: (0, g + groups))
    key_shape = jax.ShapeDtypeStruct((keys, width), jnp.float32)
    return pl.pallas_call(
        functools.partial(attend_back_kernel, width // num_heads, masked),
        grid_spec=pltpu.PrefetchScalarGridSpec(
            num_scalar_prefetch=1,
            grid=(groups, row_count // block_rows),
            in_specs=[row_spec, row_spec, row_spec, k_spec, v_spec, k_spec, v_spec],
            out_specs=[row_spec, k_spec, k_spec, k_spec, k_spec],
        ),
        out_shape=[jax.ShapeDtypeStruct((row_count, width), jnp.bfloat16)] + [key_shape] * 4,
        compiler_params=pltpu.CompilerParams(vmem_limit_bytes=VMEM_LIMIT),
        cost_estimate=pl.CostEstimate(
            flops=20 * row_count * keys * width,
            bytes_accessed=8 * (row_count + 4 * keys) * width,
            transcendentals=2 * row_count * keys * num_heads,
        ),
    )(kept, queries, grads, log_totals, kv_near, kv_near, kv_far, kv_far)


def padded_rows(block, before, after):
    return jnp.pad(block, ((before, after), (0, 0)))


def scaled_back(stream, gain_vec, grad_out):
    discarded_value, backward_fn = jax.vjp(scaled, stream, gain_vec)
    return backward_fn(grad_out)


def gelu_erf(raised):
    return 0.5 * raised * (1.0 + lax.erf(raised * 0.5**0.5))


def gelu_slope(raised):
    bell = jnp.exp(-0.5 * raised * raised) * (2.0 * math.pi) ** (-0.5)
    return 0.5 * (1.0 + lax.erf(raised * 0.5**0.5)) + raised * bell


def feed_fwd(stream, gain_vec, w_up, w_down):
    normal_in = scaled(stream, gain_vec).astype(jnp.bfloat16)
    raised = matmul(normal_in, w_up)
    hidden = gelu_erf(raised).astype(jnp.bfloat16)
    return (stream + matmul(hidden, w_down), (normal_in, raised, hidden))


def feed_back(stream, gain_vec, w_up, w_down, stored, grad_out):
    normal_in, raised, hidden = stored
    branch_grad = grad_out.astype(jnp.bfloat16)
    grad_hidden = outer_rows(branch_grad, w_down).astype(jnp.bfloat16).astype(jnp.float32)
    grad_raised = (grad_hidden * gelu_slope(raised)).astype(jnp.bfloat16)
    grad_wup = inner_rows(normal_in, grad_raised)
    grad_normal = outer_rows(grad_raised, w_up).astype(jnp.bfloat16).astype(jnp.float32)
    grad_stream, grad_gain = scaled_back(stream, gain_vec, grad_normal)
    return (grad_out + grad_stream, grad_wup, branch_grad, grad_gain)


def picked_rows(table, row_ids):
    choice = row_ids[:, None] == lax.iota(jnp.int32, table.shape[0])[None, :]
    return matmul(choice.astype(table.dtype), table).astype(table.dtype)


def swapped(block):
    devices = range(lax.axis_size("dp"))
    return lax.ppermute(block, "dp", [(i, i ^ 1) for i in devices])


def attend_fwd(stream, gain_vec, w_in, w_out, num_heads, kept, skip, block_rows):
    width = stream.shape[1]
    normal_in = scaled(stream, gain_vec).astype(jnp.bfloat16)
    kv_near = matmul(normal_in, w_in[:, width:]).astype(jnp.bfloat16)
    kv_far = swapped(kv_near)
    queries = matmul(normal_in[skip:], w_in[:, :width]).astype(jnp.bfloat16)
    merged, log_totals = attend_rows(queries, kv_near, kv_far, kept, num_heads, block_rows)
    outcome = stream[skip:] + matmul(merged, w_out)
    return (outcome, (normal_in, queries, kv_near, kv_far, merged, log_totals))


def attend_back(stream, gain_vec, w_in, w_out, num_heads, kept, skip, block_rows, stored, grad_out):
    normal_in, queries, kv_near, kv_far, merged, log_totals = stored
    branch_grad = grad_out.astype(jnp.bfloat16)
    grad_wout = inner_rows(merged, branch_grad)
    grad_merged = outer_rows(branch_grad, w_out).astype(jnp.bfloat16)
    dq, dk_near, dv_near, dk_far, dv_far = attend_rows_back(
        queries, grad_merged, log_totals, kv_near, kv_far, kept, num_heads, block_rows
    )
    dk = (dk_near + swapped(dk_far)).astype(jnp.bfloat16)
    dv = (dv_near + swapped(dv_far)).astype(jnp.bfloat16)
    grad_packed = jnp.concatenate([padded_rows(dq, skip, 0), dk, dv], axis=1)
    grad_win = inner_rows(normal_in, grad_packed)
    grad_normal = outer_rows(grad_packed, w_in).astype(jnp.bfloat16).astype(jnp.float32)
    grad_stream, grad_gain = scaled_back(stream, gain_vec, grad_normal)
    return (padded_rows(grad_out, skip, 0) + grad_stream, grad_win, grad_wout, grad_gain)


def tall_grad_kernel(first_blocks, x_ref, gx_ref, h_ref, gh_ref, out_ref):
    @pl.when(pl.program_id(0) < first_blocks)
    def _():
        out_ref[...] = inner_rows(x_ref[...], gx_ref[...]).astype(out_ref.dtype)

    @pl.when(pl.program_id(0) >= first_blocks)
    def _():
        out_ref[...] = inner_rows(h_ref[...], gh_ref[...]).astype(out_ref.dtype)


def tall_grad(chosen, grad_stream, hidden, branch_grad):
    rows, width = grad_stream.shape
    block = 512
    first_blocks, blocks = PATCH // block, (PATCH + FF) // block
    return pl.pallas_call(
        functools.partial(tall_grad_kernel, first_blocks),
        grid=(blocks,),
        in_specs=[
            pl.BlockSpec((rows, block), lambda i: (0, jnp.minimum(i, first_blocks - 1))),
            pl.BlockSpec((rows, width), lambda i: (0, 0)),
            pl.BlockSpec((rows, block), lambda i: (0, jnp.maximum(i - first_blocks, 0))),
            pl.BlockSpec((rows, width), lambda i: (0, 0)),
        ],
        out_specs=pl.BlockSpec((block, width), lambda i: (i, 0)),
        out_shape=jax.ShapeDtypeStruct((PATCH + FF, width), jnp.bfloat16),
        compiler_params=pltpu.CompilerParams(vmem_limit_bytes=VMEM_LIMIT),
        cost_estimate=pl.CostEstimate(
            flops=2 * rows * width * (PATCH + FF),
            bytes_accessed=2 * (PATCH + FF) * (rows + width),
            transcendentals=0,
        ),
    )(chosen, grad_stream, hidden, branch_grad)


MESH = pl.DeviceIdType.MESH


def gather_kernel(count, zn, *refs):
    ins, outs = refs[:count], refs[count : 2 * count]
    stages = refs[2 * count : 3 * count]
    local_sem, z_send, z_recv, p_send, p_recv = refs[3 * count :]
    section, place = lax.axis_index("section"), lax.axis_index("dp")
    z, core = place // 2, place % 2
    near = {"section": section + 1 - 2 * (section % 2)}
    far = {"section": (section + 2) % 4}
    mate = {"dp": place + 1 - 2 * core}
    ahead = {"dp": place + 2}
    behind = {"dp": place - 2}

    barrier = pltpu.get_barrier_semaphore()
    line = [{"dp": (z + j) % zn * 2 + core} for j in range(1, zn)]
    for other in [near, far, mate] + line:
        pl.semaphore_signal(barrier, inc=1, device_id=other, device_id_type=MESH)
    pl.semaphore_wait(barrier, 3 + len(line))

    def block(ref, a, owner_z, quarter=None, rows=None, owner_core=core):
        size = ins[a].shape[0]
        start, length = (0, size) if rows is None else rows
        offset = pl.multiple_of((owner_z * 2 + owner_core) * size + start, 16)
        if quarter is None:
            return ref.at[pl.ds(offset, length), :]
        width = ins[a].shape[1] // 4
        return ref.at[pl.ds(offset, length), pl.ds(pl.multiple_of(quarter * width, 128), width)]

    def own_quarter(a):
        width = ins[a].shape[1] // 4
        return ins[a].at[:, pl.ds(pl.multiple_of(section * width, 128), width)]

    def copy(src, dst, sends, recvs, index, device):
        return pltpu.make_async_remote_copy(
            src_ref=src,
            dst_ref=dst,
            send_sem=sends.at[index],
            recv_sem=recvs.at[index],
            device_id=device,
            device_id_type=MESH,
        )

    def along(a, step, upward):
        device = ahead if upward else behind
        source_z = z - (step - 1) if upward else z + (step - 1)
        src = own_quarter(a) if step == 1 else block(outs[a], a, source_z, section)
        index = (a * (zn - 1) + step - 1) * 2 + (0 if upward else 1)
        return copy(src, block(outs[a], a, source_z, section), z_send, z_recv, index, device)

    def sends_along(step, upward):
        if upward:
            return (z - (step - 1) >= 0) & (z < zn - 1)
        return (z + (step - 1) <= zn - 1) & (z > 0)

    def first_half(a):
        size = ins[a].shape[0]
        return (0, (size + 31) // 32 * 16)

    def second_half(a):
        size = ins[a].shape[0]
        start = (size + 31) // 32 * 16
        return (start, size - start)

    def in_plane(a, step, upward, kind):
        owner_z = z - step if upward else z + step
        index = ((a * (zn - 1) + step - 1) * 2 + (0 if upward else 1)) * 5 + kind
        x_quarter, y_quarter = near["section"], far["section"]
        part = [
            lambda: block(outs[a], a, owner_z, section),
            lambda: block(outs[a], a, owner_z, section),
            lambda: block(outs[a], a, owner_z, x_quarter, first_half(a)),
            lambda: block(outs[a], a, owner_z, y_quarter, second_half(a)),
            lambda: block(outs[a], a, owner_z),
        ][kind]()
        return copy(part, part, p_send, p_recv, index, (near, far, far, near, mate)[kind])

    own = []
    ranked = sorted(range(count), key=lambda a: ins[a].shape[0] * ins[a].shape[1])
    for a in ranked:
        for upward in (True, False):

            @pl.when(sends_along(1, upward))
            def _(a=a, upward=upward):
                along(a, 1, upward).start()

    for a in range(count):
        take = pltpu.make_async_copy(ins[a], stages[a], local_sem.at[a])
        take.start()
        base = count * (zn - 1) * 10
        give = copy(ins[a], block(outs[a], a, z), p_send, p_recv, base + a, mate)
        give.start()
        keep = pltpu.make_async_copy(stages[a], block(outs[a], a, z), local_sem.at[a])
        own.append((take, keep, give))

    for take, keep, give in own:
        take.wait()
        keep.start()

    items = [
        (a, step, upward)
        for step in range(1, zn)
        for a in ranked
        for upward in (True, False)
    ]

    def arrives(step, upward):
        return z - step >= 0 if upward else z + step <= zn - 1

    def received(a, step, upward):
        @pl.when(arrives(step, upward))
        def _():
            along(a, step, upward).wait_recv()
            in_plane(a, step, upward, 0).start()
            in_plane(a, step, upward, 1).start()

        if step < zn - 1:

            @pl.when(arrives(step, upward) & sends_along(step + 1, upward))
            def _():
                along(a, step + 1, upward).start()

    def passed_on(a, step, upward):
        @pl.when(arrives(step, upward))
        def _():
            in_plane(a, step, upward, 0).wait_recv()
            in_plane(a, step, upward, 2).start()
            in_plane(a, step, upward, 1).wait_recv()
            in_plane(a, step, upward, 3).start()

    def completed(a, step, upward):
        @pl.when(arrives(step, upward))
        def _():
            in_plane(a, step, upward, 2).wait_recv()
            in_plane(a, step, upward, 3).wait_recv()
            in_plane(a, step, upward, 4).start()

    lag = 4
    for i in range(len(items) + 2 * lag):
        if i < len(items):
            received(*items[i])
        if 0 <= i - lag < len(items):
            passed_on(*items[i - lag])
        if 0 <= i - 2 * lag < len(items):
            completed(*items[i - 2 * lag])

    for take, keep, give in own:
        keep.wait()
        give.wait()
    for a, step, upward in items:

        @pl.when(sends_along(step, upward))
        def _(a=a, step=step, upward=upward):
            along(a, step, upward).wait_send()

        @pl.when(arrives(step, upward))
        def _(a=a, step=step, upward=upward):
            for kind in range(5):
                in_plane(a, step, upward, kind).wait_send()
            in_plane(a, step, upward, 4).wait_recv()


def gather_blocks(blocks):
    count = len(blocks)
    dp_size = lax.axis_size("dp")
    zn = dp_size // 2
    return pl.pallas_call(
        functools.partial(gather_kernel, count, zn),
        in_specs=[pl.BlockSpec(memory_space=pl.ANY)] * count,
        out_specs=[pl.BlockSpec(memory_space=pl.ANY)] * count,
        out_shape=[
            jax.ShapeDtypeStruct((member.shape[0] * dp_size, member.shape[1]), member.dtype)
            for member in blocks
        ],
        scratch_shapes=[pltpu.VMEM(member.shape, member.dtype) for member in blocks]
        + [
            pltpu.SemaphoreType.DMA((count,)),
            pltpu.SemaphoreType.DMA((count * (zn - 1) * 2,)),
            pltpu.SemaphoreType.DMA((count * (zn - 1) * 2,)),
            pltpu.SemaphoreType.DMA((count * ((zn - 1) * 10 + 1),)),
            pltpu.SemaphoreType.DMA((count * ((zn - 1) * 10 + 1),)),
        ],
        compiler_params=pltpu.CompilerParams(
            collective_id=0, has_side_effects=True, vmem_limit_bytes=VMEM_LIMIT
        ),
    )(*blocks)


def upper_rows(size):
    return (size + 31) // 32 * 16


def add_blocks(rows, targets):
    def step(i, carried_through):
        at = pl.ds(pl.multiple_of(i * 16, 16), 16)
        for out, terms in targets:
            out[at, :] = sum(term[at, :].astype(jnp.float32) for term in terms).astype(out.dtype)
        return carried_through

    lax.fori_loop(0, rows // 16, step, 0)


def reduce_kernel(count, zn, *refs):
    ins, refs = refs[: count + 1], refs[count + 1 :]
    outs, refs = refs[: count + 1], refs[count + 1 :]
    whole, refs = refs[:count], refs[count:]
    near_one, refs = refs[:count], refs[count:]
    far_one, refs = refs[:count], refs[count:]
    far_two, refs = refs[:count], refs[count:]
    near_two, refs = refs[:count], refs[count:]
    along, refs = refs[:count], refs[count:]
    loaded, refs = refs[:count], refs[count:]
    held, refs = refs[:count], refs[count:]
    done, refs = refs[:count], refs[count:]
    total_ref, side_ref, line_ref, load_sem, move_send, move_recv, side_send, side_recv, line_send, line_recv = refs
    tally, out_total = ins[count], outs[count]
    tally_rows = out_total.shape[0]

    section, place = lax.axis_index("section"), lax.axis_index("dp")
    z, core = place // 2, place % 2
    x_quarter = section + 1 - 2 * (section % 2)
    y_quarter = (section + 2) % 4
    xy_quarter = (x_quarter + 2) % 4
    near, far = {"section": x_quarter}, {"section": y_quarter}
    mate = {"dp": place + 1 - 2 * core}
    sizes = [out.shape[0] for out in outs[:count]]
    widths = [out.shape[1] // 4 for out in outs[:count]]

    barrier = pltpu.get_barrier_semaphore()
    line = [{"dp": (z + j) % zn * 2 + core} for j in range(1, zn)]
    for other in [near, far, mate] + line:
        pl.semaphore_signal(barrier, inc=1, device_id=other, device_id_type=MESH)
    pl.semaphore_wait(barrier, 3 + len(line))

    def rows_at(a, slot, start=0, length=None):
        return pl.ds(pl.multiple_of(slot * sizes[a] + start, 16), sizes[a] if length is None else length)

    def quarter_at(a, quarter):
        return pl.ds(pl.multiple_of(quarter * widths[a], 128), widths[a])

    def upper(a):
        return upper_rows(sizes[a])

    def lower(a):
        return sizes[a] - upper_rows(sizes[a])

    def sent(src, dst, kind, a, slot, device):
        index = (kind * count + a) * (zn + 1) + slot
        return pltpu.make_async_remote_copy(
            src_ref=src,
            dst_ref=dst,
            send_sem=move_send.at[index],
            recv_sem=move_recv.at[index],
            device_id=device,
            device_id_type=MESH,
        )

    def load(a, owner_z):
        source = pl.ds(pl.multiple_of((owner_z * 2 + core) * sizes[a], 16), sizes[a])
        return pltpu.make_async_copy(
            ins[a].at[source, :], loaded[a].at[rows_at(a, owner_z), :], load_sem.at[a * zn + owner_z]
        )

    def give(a, owner_z):
        source = pl.ds(pl.multiple_of((owner_z * 2 + 1 - core) * sizes[a], 16), sizes[a])
        return sent(ins[a].at[source, :], whole[a].at[rows_at(a, owner_z), :], 0, a, owner_z, mate)

    def first_near(a, owner_z, which):
        quarter = (x_quarter, xy_quarter)[which]
        return sent(
            whole[a].at[rows_at(a, owner_z, 0, upper(a)), quarter_at(a, quarter)],
            near_one[a].at[pl.ds(pl.multiple_of((owner_z * 2 + which) * upper(a), 16), upper(a)), :],
            1 + which, a, owner_z, near,
        )

    def first_far(a, owner_z, which):
        quarter = (y_quarter, xy_quarter)[which]
        return sent(
            whole[a].at[rows_at(a, owner_z, upper(a), lower(a)), quarter_at(a, quarter)],
            far_one[a].at[pl.ds(pl.multiple_of((owner_z * 2 + which) * lower(a), 16), lower(a)), :],
            3 + which, a, owner_z, far,
        )

    def second_far(a, owner_z):
        return sent(
            whole[a].at[rows_at(a, owner_z, 0, upper(a)), quarter_at(a, y_quarter)],
            far_two[a].at[pl.ds(pl.multiple_of(owner_z * upper(a), 16), upper(a)), :],
            5, a, owner_z, far,
        )

    def second_near(a, owner_z):
        return sent(
            whole[a].at[rows_at(a, owner_z, upper(a), lower(a)), quarter_at(a, x_quarter)],
            near_two[a].at[pl.ds(pl.multiple_of(owner_z * lower(a), 16), lower(a)), :],
            6, a, owner_z, near,
        )

    def onward(a, owner_z, upward, last):
        slot = zn if last and not upward else owner_z
        return sent(
            whole[a].at[rows_at(a, owner_z), quarter_at(a, section)],
            along[a].at[rows_at(a, slot), :],
            7, a, slot, {"dp": place + 2 if upward else place - 2},
        )

    def finished(a, kind):
        quarter = (section, section, x_quarter, y_quarter)[kind]
        columns = quarter_at(a, quarter)
        part = (
            pl.ds(0, sizes[a]), pl.ds(0, sizes[a]), pl.ds(0, upper(a)), pl.ds(upper(a), lower(a))
        )[kind]
        src = done[a] if kind < 2 else outs[a].at[part, columns]
        return sent(src, outs[a].at[part, columns], 8 + kind, a, 0, (near, far, far, near)[kind])

    def keep(a):
        return pltpu.make_async_copy(
            done[a], outs[a].at[:, quarter_at(a, section)], load_sem.at[a * zn]
        )

    legs = [(k, upward) for k in range(zn - 1, 0, -1) for upward in (True, False)] + [(0, True)]
    items = [(a, leg) for leg in range(len(legs)) for a in range(count)]

    def owner_of(leg):
        k, upward = legs[leg]
        return z + k if upward else z - k

    def is_live(leg):
        k, upward = legs[leg]
        return (z + k <= zn - 1) if upward else (z - k >= 0)

    def started(a, leg):
        @pl.when(is_live(leg))
        def _():
            give(a, owner_of(leg)).start()

    def load_started(a, leg):
        @pl.when(is_live(leg))
        def _():
            load(a, owner_of(leg)).start()

    def parts(a, owner_z, is_upper, quarter):
        size = (0, upper(a)) if is_upper else (upper(a), lower(a))
        at = (rows_at(a, owner_z, *size), quarter_at(a, quarter))
        return (whole[a].at[at], loaded[a].at[at])

    def pair_up(a, owner_z, is_upper, quarter):
        both = parts(a, owner_z, is_upper, quarter)
        add_blocks(upper(a) if is_upper else lower(a), [(both[0], both)])

    def paired(a, leg):
        @pl.when(is_live(leg))
        def _():
            owner_z = owner_of(leg)
            load(a, owner_z).wait()
            give(a, owner_z).wait_recv()
            for quarter in (xy_quarter, x_quarter):
                pair_up(a, owner_z, True, quarter)
            for quarter in (xy_quarter, y_quarter):
                pair_up(a, owner_z, False, quarter)
            for which in (1, 0):
                first_near(a, owner_z, which).start()
                first_far(a, owner_z, which).start()


    def from_near(a, owner_z, which):
        start = pl.multiple_of((owner_z * 2 + which) * upper(a), 16)
        return near_one[a].at[pl.ds(start, upper(a)), :]

    def from_far(a, owner_z, which):
        start = pl.multiple_of((owner_z * 2 + which) * lower(a), 16)
        return far_one[a].at[pl.ds(start, lower(a)), :]

    def halved(a, leg):
        @pl.when(is_live(leg))
        def _():
            owner_z = owner_of(leg)
            first_near(a, owner_z, 1).wait_recv()
            both = parts(a, owner_z, True, y_quarter)
            add_blocks(upper(a), [(both[0], both + (from_near(a, owner_z, 1),))])
            second_far(a, owner_z).start()
            first_far(a, owner_z, 1).wait_recv()
            both = parts(a, owner_z, False, x_quarter)
            add_blocks(lower(a), [(both[0], both + (from_far(a, owner_z, 1),))])
            second_near(a, owner_z).start()

    def quartered(a, leg):
        k, upward = legs[leg]

        @pl.when(is_live(leg))
        def _():
            owner_z = owner_of(leg)
            own = quarter_at(a, section)
            first_near(a, owner_z, 0).wait_recv()
            second_far(a, owner_z).wait_recv()
            start = pl.multiple_of(owner_z * upper(a), 16)
            terms = parts(a, owner_z, True, section) + (
                from_near(a, owner_z, 0), far_two[a].at[pl.ds(start, upper(a)), :]
            )
            add_blocks(upper(a), [(held[a].at[pl.ds(0, upper(a)), :], terms)])
            first_far(a, owner_z, 0).wait_recv()
            second_near(a, owner_z).wait_recv()
            start = pl.multiple_of(owner_z * lower(a), 16)
            terms = parts(a, owner_z, False, section) + (
                from_far(a, owner_z, 0), near_two[a].at[pl.ds(start, lower(a)), :]
            )
            add_blocks(lower(a), [(held[a].at[pl.ds(upper(a), lower(a)), :], terms)])
            target = held[a]

            def join(upward_from, slot):
                onward(a, owner_z, upward_from, slot is not owner_z or k == 0).wait_recv()
                add_blocks(sizes[a], [(target, (target, along[a].at[rows_at(a, slot), :]))])

            if k > 0:

                @pl.when(z > 0 if upward else z < zn - 1)
                def _():
                    join(upward, owner_z)

                add_blocks(sizes[a], [(whole[a].at[rows_at(a, owner_z), own], (target,))])
                onward(a, owner_z, upward, k == 1).start()
            else:

                @pl.when(z > 0)
                def _():
                    join(True, owner_z)

                @pl.when(z < zn - 1)
                def _():
                    join(False, zn)

                def settle(i, carried_through):
                    at = pl.ds(pl.multiple_of(i * 16, 16), 16)
                    values = target[at, :]
                    done[a][at, :] = values.astype(done[a].dtype)
                    squares = values * values
                    squares = squares[:8] + squares[8:]
                    carried = total_ref[0:8, :]
                    for column in range(0, widths[a], 128):
                        carried = carried + squares[:, column : column + 128]
                    total_ref[0:8, :] = carried
                    return carried_through

                lax.fori_loop(0, sizes[a] // 16, settle, 0)
                keep(a).start()
                finished(a, 0).start()
                finished(a, 1).start()

    total_ref[0:8, :] = jnp.zeros((8, 128), jnp.float32)
    tally_copy = pltpu.make_async_copy(tally, total_ref.at[8:, :], load_sem.at[count * zn])
    tally_copy.start()
    for a, leg in items:
        started(a, leg)
        load_started(a, leg)
    lag = 5
    for i in range(len(items) + 2 * lag):
        if i < len(items):
            paired(*items[i])
        if 0 <= i - lag < len(items):
            halved(*items[i - lag])
        if 0 <= i - 2 * lag < len(items):
            quartered(*items[i - 2 * lag])

    tally_copy.wait()

    def exchanged(stage, device):
        return pltpu.make_async_remote_copy(
            src_ref=total_ref,
            dst_ref=side_ref.at[pl.ds(stage * tally_rows, tally_rows), :],
            send_sem=side_send.at[stage],
            recv_sem=side_recv.at[stage],
            device_id=device,
            device_id_type=MESH,
        )

    for stage, device in enumerate((mate, near, far)):
        swap = exchanged(stage, device)
        swap.start()
        swap.wait()
        total_ref[...] += side_ref[stage * tally_rows : (stage + 1) * tally_rows, :]

    def told(from_z, to_z, j):
        index = from_z * zn + to_z
        return pltpu.make_async_remote_copy(
            src_ref=total_ref,
            dst_ref=line_ref.at[pl.ds(pl.multiple_of(from_z * tally_rows, 8), tally_rows), :],
            send_sem=line_send.at[index],
            recv_sem=line_recv.at[index],
            device_id={"dp": to_z * 2 + core},
            device_id_type=MESH,
        )

    for j in range(1, zn):
        told(z, (z + j) % zn, j).start()
    line_ref[pl.ds(pl.multiple_of(z * tally_rows, 8), tally_rows), :] = total_ref[...]
    for j in range(1, zn):
        told((z + j) % zn, z, j).wait_recv()
    grand = line_ref[0:tally_rows, :]
    for j in range(1, zn):
        grand = grand + line_ref[j * tally_rows : (j + 1) * tally_rows, :]
    for j in range(1, zn):
        told(z, (z + j) % zn, j).wait_send()
    total_ref[...] = grand
    show = pltpu.make_async_copy(total_ref, out_total, load_sem.at[count * zn])
    show.start()

    for a in range(count):
        finished(a, 0).wait_recv()
        finished(a, 2).start()
        finished(a, 1).wait_recv()
        finished(a, 3).start()
    for a in range(count):
        keep(a).wait()
        finished(a, 2).wait_recv()
        finished(a, 3).wait_recv()
        for kind in range(4):
            finished(a, kind).wait_send()
    for a, leg in items:
        k, upward = legs[leg]

        @pl.when(is_live(leg))
        def _(a=a, leg=leg, k=k, upward=upward):
            owner_z = owner_of(leg)
            give(a, owner_z).wait_send()
            for which in (0, 1):
                first_near(a, owner_z, which).wait_send()
                first_far(a, owner_z, which).wait_send()
            second_near(a, owner_z).wait_send()
            second_far(a, owner_z).wait_send()
            if k > 0:
                onward(a, owner_z, upward, k == 1).wait_send()

    show.wait()


def reduce_blocks(blocks, tally, result_types):
    count = len(blocks)
    dp_size = lax.axis_size("dp")
    zn = dp_size // 2
    tally_rows = 8 + tally.shape[0]
    shapes = [(member.shape[0] // dp_size, member.shape[1]) for member in blocks]
    vmem = lambda rows, columns, dtype=jnp.bfloat16: pltpu.VMEM((rows, columns), dtype)
    anywhere = pl.BlockSpec(memory_space=pl.ANY)
    moves = 12 * count * (zn + 1)
    return pl.pallas_call(
        functools.partial(reduce_kernel, count, zn),
        in_specs=[anywhere] * (count + 1),
        out_specs=[anywhere] * (count + 1),
        out_shape=[jax.ShapeDtypeStruct(shape, kind) for shape, kind in zip(shapes, result_types)]
        + [jax.ShapeDtypeStruct((tally_rows, 128), jnp.float32)],
        scratch_shapes=[vmem(zn * r, w) for r, w in shapes]
        + [vmem(zn * 2 * upper_rows(r), w // 4) for r, w in shapes]
        + [vmem(zn * 2 * (r - upper_rows(r)), w // 4) for r, w in shapes]
        + [vmem(zn * upper_rows(r), w // 4) for r, w in shapes]
        + [vmem(zn * (r - upper_rows(r)), w // 4) for r, w in shapes]
        + [vmem((zn + 1) * r, w // 4) for r, w in shapes]
        + [vmem(zn * r, w) for r, w in shapes]
        + [vmem(r, w // 4, jnp.float32) for r, w in shapes]
        + [vmem(r, w // 4, kind) for (r, w), kind in zip(shapes, result_types)]
        + [
            vmem(tally_rows, 128, jnp.float32),
            vmem(3 * tally_rows, 128, jnp.float32),
            vmem(zn * tally_rows, 128, jnp.float32),
            pltpu.SemaphoreType.DMA((count * zn + 1,)),
            pltpu.SemaphoreType.DMA((moves,)),
            pltpu.SemaphoreType.DMA((moves,)),
            pltpu.SemaphoreType.DMA((3,)),
            pltpu.SemaphoreType.DMA((3,)),
            pltpu.SemaphoreType.DMA((zn * zn,)),
            pltpu.SemaphoreType.DMA((zn * zn,)),
        ],
        compiler_params=pltpu.CompilerParams(
            collective_id=1, has_side_effects=True, vmem_limit_bytes=60 * 1024 * 1024
        ),
    )(*blocks, tally)


def adamw_step(weight, grad_now, first, second, decay, rate):
    first = BETA_ONE * first + (1.0 - BETA_ONE) * grad_now
    second = BETA_TWO * second + (1.0 - BETA_TWO) * grad_now * grad_now
    ratio = first / (1.0 - BETA_ONE**STEP) / (jnp.sqrt(second / (1.0 - BETA_TWO**STEP)) + EPSILON)
    return (weight - rate * (ratio + decay * weight), first, second)


def local(
    pixels,
    token_order,
    visible,
    wide_weight,
    tall_weight,
    pred_weight,
    pred_down,
    enc_gains,
    pred_gains,
    wide_first,
    tall_first,
    pred_first,
    pred_down_first,
    enc_gains_first,
    pred_gains_first,
    wide_second,
    tall_second,
    pred_second,
    pred_down_second,
    enc_gains_second,
    pred_gains_second,
    teacher_wide,
    teacher_tall,
    teacher_gains,
):
    masters = (wide_weight, tall_weight, pred_weight, pred_down, enc_gains, pred_gains)
    section_idx = lax.axis_index("section")
    section_count = lax.axis_size("section")
    core = lax.axis_index("dp") % 2
    clips_here = pixels.shape[0]
    assert section_count == 2 * clips_here

    owner = section_idx // clips_here
    clip = section_idx % clips_here
    holds = core == owner
    counts_own = lax.dynamic_index_in_dim(visible, clip, 0)
    order_own = lax.dynamic_index_in_dim(token_order, clip, 0, keepdims=False)
    clip_facts = jnp.concatenate([order_own, counts_own])
    clip_facts = jnp.where(holds, clip_facts, swapped(clip_facts))
    seen = clip_facts[L]
    order_pairs = clip_facts[:L].reshape(HALF, 2)
    order = jnp.where(core == 0, order_pairs[:, 0], order_pairs[:, 1])
    pairs_own = order_own.reshape(HALF, 2)
    order_here = jnp.where(core == 0, pairs_own[:, 0], pairs_own[:, 1])
    order_there = jnp.where(core == 0, pairs_own[:, 1], pairs_own[:, 0])
    pixel_rows = lax.dynamic_index_in_dim(pixels, clip, 0, keepdims=False)
    for_here = picked_rows(pixel_rows, order_here)
    for_there = picked_rows(pixel_rows, order_there)
    chosen = jnp.where(holds, for_here, swapped(for_there))
    seen_near = (seen - core + 1) // 2
    seen_far = (seen + core) // 2
    kept = jnp.stack([seen_near, seen_far])
    visible_high, visible_low = visible // LANES, visible % LANES
    dp_size = lax.axis_size("dp")
    row_count = wide_weight.shape[0]
    small = jnp.concatenate(
        [
            wide_weight[:, 4 * D + FF :],
            enc_gains,
            teacher_gains,
            jnp.pad(pred_gains, ((0, row_count - pred_gains.shape[0]), (0, 0))),
            jnp.zeros((row_count, LANES - 10 - 2 * clips_here), jnp.float32),
            jnp.broadcast_to(
                jnp.concatenate([visible_high, visible_low]).astype(jnp.float32)[None, :],
                (row_count, 2 * clips_here),
            ),
        ],
        axis=1,
    )
    pred_block = pred_weight.shape if pred_weight.shape[0] % 16 == 0 else (-1, D)
    pred_form = (PD, pred_weight.shape[1]) if pred_weight.shape[0] % 16 == 0 else (-1, D)
    blocks = (
        teacher_wide,
        teacher_tall,
        wide_weight[:, : 4 * D + FF],
        tall_weight,
        pred_weight.reshape(pred_block),
        small,
        jnp.pad(pred_down, ((0, 0), (0, LANES))),
    )
    teach_wide, teach_tall, w_wide, w_tall, w_pred, w_small, w_down = gather_blocks(
        tuple(member.astype(jnp.bfloat16) for member in blocks)
    )
    w_pred = w_pred.reshape(PD, -1)
    w_down = w_down[:, :PD]
    pred_embed = w_small[:, :PD]
    enc_copy = w_small[:, PD : PD + 3]
    teach_copy = w_small[:, PD + 3 : PD + 6]
    pred_copy = w_small[:, PD + 6 : PD + 10].reshape(dp_size, row_count, 4)
    pred_copy = pred_copy[:, : pred_gains.shape[0]].reshape(PD, 4)
    counts = w_small[::row_count, PD + LANES - 2 * clips_here :].astype(jnp.float32)
    counts = counts[:, :clips_here] * LANES + counts[:, clips_here:]
    target_total = jnp.sum(L - counts)
    enc_gain = enc_copy.astype(jnp.float32)
    pred_gain = pred_copy.astype(jnp.float32)
    teach_gain = teach_copy.astype(jnp.float32)
    enc_attn = (w_wide[:, : 3 * D], w_wide[:, 3 * D : 4 * D])
    enc_feed = (w_wide[:, 4 * D : 4 * D + FF], w_tall[PATCH:])
    pred_attn = (w_pred[:, : 3 * PD], w_pred[:, 3 * PD : 4 * PD])
    pred_feed = (w_pred[:, 4 * PD : 4 * PD + PF], w_down)
    pred_head = w_pred[:, 4 * PD + PF :]

    table = position_table(order, D)
    pred_table = position_table(order, PD)
    row_ids = lax.iota(jnp.int32, HALF)
    context = (row_ids < seen_near)[:, None]

    teach_stream = matmul(chosen, teach_tall[:PATCH]) + table
    teach_stream, discarded_value = attend_fwd(
        teach_stream, teach_gain[:, 0], teach_wide[:, : 3 * D], teach_wide[:, 3 * D : 4 * D],
        HE, None, SKIP, 336,
    )
    teach_stream = teach_stream.astype(jnp.bfloat16).astype(jnp.float32)
    teach_stream, discarded_value = feed_fwd(
        teach_stream, teach_gain[:, 1], teach_wide[:, 4 * D :], teach_tall[PATCH:]
    )
    goal = normed(scaled(teach_stream, teach_gain[:, 2])).astype(jnp.bfloat16).astype(jnp.float32)

    enc_chosen = chosen[:SEEN]
    stream_a = matmul(enc_chosen, w_tall[:PATCH]) + table[:SEEN]
    stream_b, stored_a = attend_fwd(
        stream_a, enc_gain[:, 0], enc_attn[0], enc_attn[1], HE, kept, 0, SEEN
    )
    stream_b = stream_b.astype(jnp.bfloat16).astype(jnp.float32)
    stream_c, stored_b = feed_fwd(stream_b, enc_gain[:, 1], enc_feed[0], enc_feed[1])
    encoded = scaled(stream_c, enc_gain[:, 2]).astype(jnp.bfloat16)

    projected = padded_rows(matmul(encoded, pred_embed), 0, HALF - SEEN)
    stream_d = jnp.where(context, projected, pred_gain[:, 3][None, :]) + pred_table
    stream_e, stored_d = attend_fwd(
        stream_d, pred_gain[:, 0], pred_attn[0], pred_attn[1], PH, None, SKIP, 336
    )
    stream_e = stream_e.astype(jnp.bfloat16).astype(jnp.float32)
    stream_f, stored_e = feed_fwd(stream_e, pred_gain[:, 1], pred_feed[0], pred_feed[1])
    final = scaled(stream_f, pred_gain[:, 2]).astype(jnp.bfloat16)
    residual = matmul(final, pred_head) - goal
    smooth_err = jnp.sqrt(residual * residual + 1.0)
    target_mask = jnp.logical_not(context[SKIP:])
    loss_part = jnp.sum(jnp.where(target_mask, smooth_err - 1.0, 0.0))
    grad_guess = (jnp.where(target_mask, residual / smooth_err, 0.0) / target_total).astype(
        jnp.bfloat16
    )

    grad_head = inner_rows(final, grad_guess)
    grad_final = outer_rows(grad_guess, pred_head).astype(jnp.bfloat16).astype(jnp.float32)
    grad_stream, grad_pg2 = scaled_back(stream_f, pred_gain[:, 2], grad_final)
    grad_stream, grad_pup, branch_grad, grad_pg1 = feed_back(
        stream_e, pred_gain[:, 1], pred_feed[0], pred_feed[1], stored_e, grad_stream
    )
    grad_down = inner_rows(stored_e[2], branch_grad)
    grad_stream = grad_stream.astype(jnp.bfloat16).astype(jnp.float32)
    grad_stream, grad_pin, grad_pout, grad_pg0 = attend_back(
        stream_d, pred_gain[:, 0], pred_attn[0], pred_attn[1], PH, None, SKIP, 336, stored_d, grad_stream
    )
    grad_token = jnp.sum(jnp.where(context, 0.0, grad_stream), axis=0)
    grad_projected = jnp.where(context, grad_stream, 0.0)[:SEEN].astype(jnp.bfloat16)
    grad_embed = inner_rows(encoded, grad_projected)
    grad_encoded = outer_rows(grad_projected, pred_embed).astype(jnp.bfloat16).astype(jnp.float32)
    grad_stream, grad_eg2 = scaled_back(stream_c, enc_gain[:, 2], grad_encoded)
    grad_stream, grad_eup, branch_grad, grad_eg1 = feed_back(
        stream_b, enc_gain[:, 1], enc_feed[0], enc_feed[1], stored_b, grad_stream
    )
    grad_stream = grad_stream.astype(jnp.bfloat16).astype(jnp.float32)
    grad_stream, grad_ein, grad_eout, grad_eg0 = attend_back(
        stream_a, enc_gain[:, 0], enc_attn[0], enc_attn[1], HE, kept, 0, SEEN, stored_a, grad_stream
    )
    grad_tall = tall_grad(
        chosen[:SEEN], grad_stream.astype(jnp.bfloat16), stored_b[2], branch_grad
    )

    gain_grads = jnp.concatenate(
        [
            jnp.stack([grad_eg0, grad_eg1, grad_eg2], axis=1).reshape(-1, LANES),
            jnp.stack([grad_pg0, grad_pg1, grad_pg2, grad_token], axis=1).reshape(-1, LANES),
        ],
        axis=0,
    )
    gain_rows = 3 * D // LANES
    loss_tile = jnp.zeros((8, LANES), jnp.float32).at[0, 0].set(loss_part)
    tally = jnp.concatenate(
        [loss_tile, gain_grads, jnp.zeros((4, LANES), jnp.float32)], axis=0
    )
    blocks = shortened(
        (
            grad_ein,
            grad_eout,
            grad_eup,
            jnp.pad(grad_embed, ((0, 0), (0, LANES))),
            grad_tall,
            jnp.concatenate(shortened([grad_pin, grad_pout, grad_pup, grad_head]), axis=1).reshape(pred_form),
            jnp.pad(grad_down, ((0, 0), (0, LANES))),
        )
    )
    *summed, tally = reduce_blocks(
        blocks, tally, [jnp.bfloat16] * 5 + [jnp.float32] * 2
    )
    wide_parts = [summed[0], summed[1], summed[2], summed[3][:, :PD]]
    place = lax.axis_index("dp")
    gains_all = tally[16 : 16 + gain_rows].reshape(D, 3)
    pred_gains_all = tally[16 + gain_rows : 16 + gain_rows + 4 * PD // LANES].reshape(PD, 4)
    shares = (
        jnp.concatenate(wide_parts, axis=1).astype(jnp.float32),
        summed[4].astype(jnp.float32),
        summed[5].reshape(pred_weight.shape).astype(jnp.float32),
        summed[6][:, :PD].astype(jnp.float32),
        lax.dynamic_slice_in_dim(gains_all, place * enc_gains.shape[0], enc_gains.shape[0], 0),
        lax.dynamic_slice_in_dim(pred_gains_all, place * pred_gains.shape[0], pred_gains.shape[0], 0),
    )
    loss_sum = tally[8, 0]
    square_total = jnp.sum(tally[:8]) + jnp.sum(jnp.square(tally[16:]))
    grad_norm = jnp.sqrt(square_total)
    factor = jnp.minimum(1.0, CLIP_AT / (grad_norm + 1e-06))
    firsts = (
        wide_first,
        tall_first,
        pred_first,
        pred_down_first,
        enc_gains_first,
        pred_gains_first,
    )
    seconds = (
        wide_second,
        tall_second,
        pred_second,
        pred_down_second,
        enc_gains_second,
        pred_gains_second,
    )
    decays = (DECAY, DECAY, DECAY, DECAY, 0.0, 0.0)
    rates = (RATE, RATE, RATE, RATE, GAIN_RATE, GAIN_RATE)
    results = [
        adamw_step(
            masters[group_idx],
            shares[group_idx] * factor,
            firsts[group_idx],
            seconds[group_idx],
            decays[group_idx],
            rates[group_idx],
        )
        for group_idx in range(6)
    ]
    news = [entry[0] for entry in results]
    teacher_wide_new = KEEP_RATE * teacher_wide + (1.0 - KEEP_RATE) * news[0][:, : 4 * D + FF]
    teacher_tall_new = KEEP_RATE * teacher_tall + (1.0 - KEEP_RATE) * news[1]
    teacher_gains_new = KEEP_RATE * teacher_gains + (1.0 - KEEP_RATE) * news[4]
    return (
        loss_sum,
        target_total,
        grad_norm,
        news[0],
        news[1],
        news[2],
        news[3],
        news[4],
        news[5],
        results[0][1],
        results[1][1],
        results[2][1],
        results[3][1],
        results[4][1],
        results[5][1],
        results[0][2],
        results[1][2],
        results[2][2],
        results[3][2],
        results[4][2],
        results[5][2],
        news[0].astype(jnp.bfloat16),
        news[1].astype(jnp.bfloat16),
        news[2].astype(jnp.bfloat16),
        news[3].astype(jnp.bfloat16),
        news[4].astype(jnp.bfloat16),
        news[5].astype(jnp.bfloat16),
        teacher_wide_new,
        teacher_tall_new,
        teacher_gains_new,
    )


def solution(mesh):
    return jax.shard_map(
        local,
        mesh=mesh,
        in_specs=(
            P("dp", None, None),
            P("dp", None),
            P("dp"),
            P("dp", None),
            P("dp", None),
            P("dp", None),
            P("dp", None),
            P("dp", None),
            P("dp", None),
            P("dp", None),
            P("dp", None),
            P("dp", None),
            P("dp", None),
            P("dp", None),
            P("dp", None),
            P("dp", None),
            P("dp", None),
            P("dp", None),
            P("dp", None),
            P("dp", None),
            P("dp", None),
            P("dp", None),
            P("dp", None),
            P("dp", None),
        ),
        out_specs=(
            P(),
            P(),
            P(),
            P("dp", None),
            P("dp", None),
            P("dp", None),
            P("dp", None),
            P("dp", None),
            P("dp", None),
            P("dp", None),
            P("dp", None),
            P("dp", None),
            P("dp", None),
            P("dp", None),
            P("dp", None),
            P("dp", None),
            P("dp", None),
            P("dp", None),
            P("dp", None),
            P("dp", None),
            P("dp", None),
            P("dp", None),
            P("dp", None),
            P("dp", None),
            P("dp", None),
            P("dp", None),
            P("dp", None),
            P("dp", None),
            P("dp", None),
            P("dp", None),
        ),
        check_vma=False,
    )
```

```python
import functools
import math

import jax
import jax.numpy as jnp
from jax import lax
from jax.experimental import pallas as pl
from jax.experimental.pallas import tpu as pltpu
from jax.sharding import PartitionSpec as P

D = 1024
HE = 16
FF = 4096
PD = 384
PH = 12
PF = 1536
PATCH = 1536
L = 1536
STEP = 10
VIS = 576
VIS_LO = 192
HALF = L // 2
SEEN = VIS // 2
SKIP = VIS_LO // 2
LANES = 128
VMEM_LIMIT = 50 * 1024 * 1024


BETA_ONE = 0.9
BETA_TWO = 0.999
EPSILON = 1e-08
RATE = 0.02
GAIN_RATE = 0.5
DECAY = 0.05
CLIP_AT = 0.05
KEEP_RATE = 0.8
NEGATIVE = -1e30


def shortened(x):
    return jax.tree.map(lambda a: a.astype(jnp.bfloat16) if a.dtype == jnp.float32 else a, x)


def normed(stream):
    centred = stream - jnp.mean(stream, axis=-1, keepdims=True)
    return centred * lax.rsqrt(jnp.mean(centred * centred, axis=-1, keepdims=True) + 1e-06)


def scaled(stream, gain_vec):
    return normed(stream) * gain_vec


def position_table(positions, feature_width):
    frequency = jnp.exp(
        jnp.arange(feature_width // 2, dtype=jnp.float32)
        * (-2.0 * math.log(10000.0) / feature_width)
    )
    angles = positions.astype(jnp.float32)[:, None] * frequency[None, :]
    return jnp.concatenate([jnp.sin(angles), jnp.cos(angles)], axis=1)


def matmul(left, right):
    return jnp.dot(left, right, preferred_element_type=jnp.float32)


def inner_rows(left, right):
    return lax.dot_general(
        left, right, (((0,), (0,)), ((), ())), preferred_element_type=jnp.float32
    )


def outer_rows(left, right):
    return lax.dot_general(
        left, right, (((1,), (1,)), ((), ())), preferred_element_type=jnp.float32
    )


def head_scores(queries, key_heads, kept):
    logits = outer_rows(queries, key_heads)
    if kept is None:
        return logits
    key_ids = lax.broadcasted_iota(jnp.int32, logits.shape, 1)
    return jnp.where(key_ids < kept, logits, NEGATIVE)


def attend_kernel(head_size, masked, kept_ref, q_ref, k0_ref, v0_ref, k1_ref, v1_ref, o_ref, l_ref):
    exponent = head_size ** (-0.5) * math.log2(math.e)
    lane_head = lax.broadcasted_iota(jnp.int32, (1, LANES), 1) // head_size
    kept = (kept_ref[0], kept_ref[1]) if masked else (None, None)
    queries = q_ref[...]
    merged = jnp.zeros(o_ref.shape, jnp.float32)
    log_totals = jnp.zeros(o_ref.shape, jnp.float32)
    for head in range(LANES // head_size):
        chosen = lane_head == head
        head_queries = jnp.where(chosen, queries, jnp.zeros_like(queries))
        near = head_scores(head_queries, k0_ref[...], kept[0])
        far = head_scores(head_queries, k1_ref[...], kept[1])
        row_max = exponent * jnp.maximum(
            jnp.max(near, axis=1, keepdims=True), jnp.max(far, axis=1, keepdims=True)
        )
        near = jnp.exp2(near * exponent - row_max)
        far = jnp.exp2(far * exponent - row_max)
        row_total = jnp.sum(near, axis=1, keepdims=True) + jnp.sum(far, axis=1, keepdims=True)
        outcome = matmul(near.astype(jnp.bfloat16), v0_ref[...]) + matmul(
            far.astype(jnp.bfloat16), v1_ref[...]
        )
        merged = jnp.where(chosen, outcome / row_total, merged)
        log_totals = jnp.where(chosen, row_max + jnp.log2(row_total), log_totals)
    o_ref[...] = merged.astype(o_ref.dtype)
    if l_ref is not None:
        l_ref[...] = log_totals


def attend_rows(queries, kv_near, kv_far, kept, num_heads, block_rows):
    row_count, width = queries.shape
    keys = kv_near.shape[0]
    groups = width // LANES
    masked = kept is not None
    if not masked:
        kept = jnp.zeros((2,), jnp.int32)
    row_spec = pl.BlockSpec((block_rows, LANES), lambda g, b, kept: (b, g))
    k_spec = pl.BlockSpec((keys, LANES), lambda g, b, kept: (0, g))
    v_spec = pl.BlockSpec((keys, LANES), lambda g, b, kept: (0, g + groups))
    return pl.pallas_call(
        functools.partial(attend_kernel, width // num_heads, masked),
        grid_spec=pltpu.PrefetchScalarGridSpec(
            num_scalar_prefetch=1,
            grid=(groups, row_count // block_rows),
            in_specs=[row_spec, k_spec, v_spec, k_spec, v_spec],
            out_specs=[row_spec, row_spec],
        ),
        out_shape=[
            jax.ShapeDtypeStruct((row_count, width), jnp.bfloat16),
            jax.ShapeDtypeStruct((row_count, width), jnp.float32),
        ],
        compiler_params=pltpu.CompilerParams(vmem_limit_bytes=VMEM_LIMIT),
        cost_estimate=pl.CostEstimate(
            flops=8 * row_count * keys * width,
            bytes_accessed=8 * (row_count + keys) * width,
            transcendentals=2 * row_count * keys * num_heads,
        ),
    )(kept, queries, kv_near, kv_near, kv_far, kv_far)


def attend_back_kernel(
    head_size, masked, kept_ref, q_ref, g_ref, l_ref, k0_ref, v0_ref, k1_ref, v1_ref,
    dq_ref, dk0_ref, dv0_ref, dk1_ref, dv1_ref,
):
    scaling = head_size ** (-0.5)
    exponent = scaling * math.log2(math.e)
    lane_head = lax.broadcasted_iota(jnp.int32, (1, LANES), 1) // head_size
    kept = (kept_ref[0], kept_ref[1]) if masked else (None, None)

    @pl.when(pl.program_id(1) == 0)
    def _():
        for ref in (dk0_ref, dv0_ref, dk1_ref, dv1_ref):
            ref[...] = jnp.zeros_like(ref)

    queries, grads, log_totals = q_ref[...], g_ref[...], l_ref[...]
    grad_queries = jnp.zeros(dq_ref.shape, jnp.float32)
    for head in range(LANES // head_size):
        chosen = lane_head == head
        head_queries = jnp.where(chosen, queries, jnp.zeros_like(queries))
        head_grads = jnp.where(chosen, grads, jnp.zeros_like(grads))
        log_total = log_totals[:, head * head_size : head * head_size + 1]
        probs, steps, totals = [], [], 0.0
        for k_ref, v_ref, count in ((k0_ref, v0_ref, kept[0]), (k1_ref, v1_ref, kept[1])):
            attn = jnp.exp2(head_scores(head_queries, k_ref[...], count) * exponent - log_total)
            step = outer_rows(head_grads, v_ref[...]) * attn
            totals = totals + jnp.sum(step, axis=1, keepdims=True)
            probs.append(attn)
            steps.append(step)
        outcome = 0.0
        for attn, step, k_ref, dk_ref, dv_ref in zip(
            probs, steps, (k0_ref, k1_ref), (dk0_ref, dk1_ref), (dv0_ref, dv1_ref)
        ):
            grad_logits = (step - attn * totals).astype(jnp.bfloat16)
            dv_ref[...] += inner_rows(attn.astype(jnp.bfloat16), head_grads)
            dk_ref[...] += inner_rows(grad_logits, head_queries) * scaling
            outcome = outcome + matmul(grad_logits, k_ref[...])
        grad_queries = jnp.where(chosen, outcome * scaling, grad_queries)
    dq_ref[...] = grad_queries.astype(dq_ref.dtype)


def attend_rows_back(queries, grads, log_totals, kv_near, kv_far, kept, num_heads, block_rows):
    row_count, width = queries.shape
    keys = kv_near.shape[0]
    groups = width // LANES
    masked = kept is not None
    if not masked:
        kept = jnp.zeros((2,), jnp.int32)
    row_spec = pl.BlockSpec((block_rows, LANES), lambda g, b, kept: (b, g))
    k_spec = pl.BlockSpec((keys, LANES), lambda g, b, kept: (0, g))
    v_spec = pl.BlockSpec((keys, LANES), lambda g, b, kept: (0, g + groups))
    key_shape = jax.ShapeDtypeStruct((keys, width), jnp.float32)
    return pl.pallas_call(
        functools.partial(attend_back_kernel, width // num_heads, masked),
        grid_spec=pltpu.PrefetchScalarGridSpec(
            num_scalar_prefetch=1,
            grid=(groups, row_count // block_rows),
            in_specs=[row_spec, row_spec, row_spec, k_spec, v_spec, k_spec, v_spec],
            out_specs=[row_spec, k_spec, k_spec, k_spec, k_spec],
        ),
        out_shape=[jax.ShapeDtypeStruct((row_count, width), jnp.bfloat16)] + [key_shape] * 4,
        compiler_params=pltpu.CompilerParams(vmem_limit_bytes=VMEM_LIMIT),
        cost_estimate=pl.CostEstimate(
            flops=20 * row_count * keys * width,
            bytes_accessed=8 * (row_count + 4 * keys) * width,
            transcendentals=2 * row_count * keys * num_heads,
        ),
    )(kept, queries, grads, log_totals, kv_near, kv_near, kv_far, kv_far)


def padded_rows(block, before, after):
    return jnp.pad(block, ((before, after), (0, 0)))


def scaled_back(stream, gain_vec, grad_out):
    discarded_value, backward_fn = jax.vjp(scaled, stream, gain_vec)
    return backward_fn(grad_out)


def gelu_erf(raised):
    return 0.5 * raised * (1.0 + lax.erf(raised * 0.5**0.5))


def gelu_slope(raised):
    bell = jnp.exp(-0.5 * raised * raised) * (2.0 * math.pi) ** (-0.5)
    return 0.5 * (1.0 + lax.erf(raised * 0.5**0.5)) + raised * bell


def feed_fwd(stream, gain_vec, w_up, w_down):
    normal_in = scaled(stream, gain_vec).astype(jnp.bfloat16)
    raised = matmul(normal_in, w_up)
    hidden = gelu_erf(raised).astype(jnp.bfloat16)
    return (stream + matmul(hidden, w_down), (normal_in, raised, hidden))


def feed_back(stream, gain_vec, w_up, w_down, stored, grad_out):
    normal_in, raised, hidden = stored
    branch_grad = grad_out.astype(jnp.bfloat16)
    grad_hidden = outer_rows(branch_grad, w_down).astype(jnp.bfloat16).astype(jnp.float32)
    grad_raised = (grad_hidden * gelu_slope(raised)).astype(jnp.bfloat16)
    grad_wup = inner_rows(normal_in, grad_raised)
    grad_normal = outer_rows(grad_raised, w_up).astype(jnp.bfloat16).astype(jnp.float32)
    grad_stream, grad_gain = scaled_back(stream, gain_vec, grad_normal)
    return (grad_out + grad_stream, grad_wup, branch_grad, grad_gain)


def picked_rows(table, row_ids):
    choice = row_ids[:, None] == lax.iota(jnp.int32, table.shape[0])[None, :]
    return matmul(choice.astype(table.dtype), table).astype(table.dtype)


def swapped(block):
    devices = range(lax.axis_size("dp"))
    return lax.ppermute(block, "dp", [(i, i ^ 1) for i in devices])


def attend_fwd(stream, gain_vec, w_in, w_out, num_heads, kept, skip, block_rows):
    width = stream.shape[1]
    normal_in = scaled(stream, gain_vec).astype(jnp.bfloat16)
    kv_near = matmul(normal_in, w_in[:, width:]).astype(jnp.bfloat16)
    kv_far = swapped(kv_near)
    queries = matmul(normal_in[skip:], w_in[:, :width]).astype(jnp.bfloat16)
    merged, log_totals = attend_rows(queries, kv_near, kv_far, kept, num_heads, block_rows)
    outcome = stream[skip:] + matmul(merged, w_out)
    return (outcome, (normal_in, queries, kv_near, kv_far, merged, log_totals))


def attend_back(stream, gain_vec, w_in, w_out, num_heads, kept, skip, block_rows, stored, grad_out):
    normal_in, queries, kv_near, kv_far, merged, log_totals = stored
    branch_grad = grad_out.astype(jnp.bfloat16)
    grad_wout = inner_rows(merged, branch_grad)
    grad_merged = outer_rows(branch_grad, w_out).astype(jnp.bfloat16)
    dq, dk_near, dv_near, dk_far, dv_far = attend_rows_back(
        queries, grad_merged, log_totals, kv_near, kv_far, kept, num_heads, block_rows
    )
    dk = (dk_near + swapped(dk_far)).astype(jnp.bfloat16)
    dv = (dv_near + swapped(dv_far)).astype(jnp.bfloat16)
    grad_packed = jnp.concatenate([padded_rows(dq, skip, 0), dk, dv], axis=1)
    grad_win = inner_rows(normal_in, grad_packed)
    grad_normal = outer_rows(grad_packed, w_in).astype(jnp.bfloat16).astype(jnp.float32)
    grad_stream, grad_gain = scaled_back(stream, gain_vec, grad_normal)
    return (padded_rows(grad_out, skip, 0) + grad_stream, grad_win, grad_wout, grad_gain)


def tall_grad_kernel(first_blocks, x_ref, gx_ref, h_ref, gh_ref, out_ref):
    @pl.when(pl.program_id(0) < first_blocks)
    def _():
        out_ref[...] = inner_rows(x_ref[...], gx_ref[...]).astype(out_ref.dtype)

    @pl.when(pl.program_id(0) >= first_blocks)
    def _():
        out_ref[...] = inner_rows(h_ref[...], gh_ref[...]).astype(out_ref.dtype)


def tall_grad(chosen, grad_stream, hidden, branch_grad):
    rows, width = grad_stream.shape
    block = 512
    first_blocks, blocks = PATCH // block, (PATCH + FF) // block
    return pl.pallas_call(
        functools.partial(tall_grad_kernel, first_blocks),
        grid=(blocks,),
        in_specs=[
            pl.BlockSpec((rows, block), lambda i: (0, jnp.minimum(i, first_blocks - 1))),
            pl.BlockSpec((rows, width), lambda i: (0, 0)),
            pl.BlockSpec((rows, block), lambda i: (0, jnp.maximum(i - first_blocks, 0))),
            pl.BlockSpec((rows, width), lambda i: (0, 0)),
        ],
        out_specs=pl.BlockSpec((block, width), lambda i: (i, 0)),
        out_shape=jax.ShapeDtypeStruct((PATCH + FF, width), jnp.bfloat16),
        compiler_params=pltpu.CompilerParams(vmem_limit_bytes=VMEM_LIMIT),
        cost_estimate=pl.CostEstimate(
            flops=2 * rows * width * (PATCH + FF),
            bytes_accessed=2 * (PATCH + FF) * (rows + width),
            transcendentals=0,
        ),
    )(chosen, grad_stream, hidden, branch_grad)


MESH = pl.DeviceIdType.MESH


def normed_rows(source, target, rows, gain_row, chunk, twice=False):
    def step(i, carried_through):
        at = pl.ds(pl.multiple_of(i * chunk, 16), chunk)
        values = normed(source[at, :]) * gain_row
        if twice:
            values = normed(values)
        target[at, :] = values.astype(target.dtype)
        return carried_through

    lax.fori_loop(0, rows // chunk, step, 0)


def gather_kernel(count, zn, *refs):
    ins, refs = refs[:count], refs[count:]
    chosen_ref, table_ref, *refs = refs
    outs, goal_ref, refs = refs[:count], refs[count], refs[count + 1 :]
    stages, refs = refs[:count], refs[count:]
    facts_ref, t0_ref, a_ref, near_ref, far_ref, q_ref, o_ref, h_ref, sum_ref, embed_buf, qkv_buf, up_buf, down_buf, *refs = refs
    local_sem, z_send, z_recv, p_send, p_recv, w_sem, kv_sem = refs
    section, place = lax.axis_index("section"), lax.axis_index("dp")
    z, core = place // 2, place % 2
    near = {"section": section + 1 - 2 * (section % 2)}
    far = {"section": (section + 2) % 4}
    mate = {"dp": place + 1 - 2 * core}
    ahead = {"dp": place + 2}
    behind = {"dp": place - 2}

    barrier = pltpu.get_barrier_semaphore()
    line = [{"dp": (z + j) % zn * 2 + core} for j in range(1, zn)]
    for other in [near, far, mate] + line:
        pl.semaphore_signal(barrier, inc=1, device_id=other, device_id_type=MESH)
    pl.semaphore_wait(barrier, 3 + len(line))

    def block(ref, a, owner_z, quarter=None, rows=None, owner_core=core):
        size = ins[a].shape[0]
        start, length = (0, size) if rows is None else rows
        offset = pl.multiple_of((owner_z * 2 + owner_core) * size + start, 16)
        if quarter is None:
            return ref.at[pl.ds(offset, length), :]
        width = ins[a].shape[1] // 4
        return ref.at[pl.ds(offset, length), pl.ds(pl.multiple_of(quarter * width, 128), width)]

    def own_quarter(a):
        width = ins[a].shape[1] // 4
        return ins[a].at[:, pl.ds(pl.multiple_of(section * width, 128), width)]

    def copy(src, dst, sends, recvs, index, device):
        return pltpu.make_async_remote_copy(
            src_ref=src,
            dst_ref=dst,
            send_sem=sends.at[index],
            recv_sem=recvs.at[index],
            device_id=device,
            device_id_type=MESH,
        )

    def along(a, step, upward):
        device = ahead if upward else behind
        source_z = z - (step - 1) if upward else z + (step - 1)
        src = own_quarter(a) if step == 1 else block(outs[a], a, source_z, section)
        index = (a * (zn - 1) + step - 1) * 2 + (0 if upward else 1)
        return copy(src, block(outs[a], a, source_z, section), z_send, z_recv, index, device)

    def sends_along(step, upward):
        if upward:
            return (z - (step - 1) >= 0) & (z < zn - 1)
        return (z + (step - 1) <= zn - 1) & (z > 0)

    def first_half(a):
        size = ins[a].shape[0]
        return (0, (size + 31) // 32 * 16)

    def second_half(a):
        size = ins[a].shape[0]
        start = (size + 31) // 32 * 16
        return (start, size - start)

    def in_plane(a, step, upward, kind):
        owner_z = z - step if upward else z + step
        index = ((a * (zn - 1) + step - 1) * 2 + (0 if upward else 1)) * 5 + kind
        x_quarter, y_quarter = near["section"], far["section"]
        part = [
            lambda: block(outs[a], a, owner_z, section),
            lambda: block(outs[a], a, owner_z, section),
            lambda: block(outs[a], a, owner_z, x_quarter, first_half(a)),
            lambda: block(outs[a], a, owner_z, y_quarter, second_half(a)),
            lambda: block(outs[a], a, owner_z),
        ][kind]()
        return copy(part, part, p_send, p_recv, index, (near, far, far, near, mate)[kind])

    own = []
    def offered(a):
        for upward in (True, False):

            @pl.when(sends_along(1, upward))
            def _(upward=upward):
                along(a, 1, upward).start()

    for a in range(2):
        offered(a)

    settled = []
    for a in range(count):
        take = pltpu.make_async_copy(ins[a], stages[a], local_sem.at[a])
        take.start()
        base = count * (zn - 1) * 10
        give = copy(ins[a], block(outs[a], a, z), p_send, p_recv, base + a, mate)
        give.start()
        keep = pltpu.make_async_copy(stages[a], block(outs[a], a, z), local_sem.at[a])
        own.append((take, keep, give))

    for take, keep, give in own:
        take.wait()
        keep.start()

    items = [
        (a, step, upward)
        for a in range(count)
        for step in range(1, zn)
        for upward in (True, False)
    ]

    def arrives(step, upward):
        return z - step >= 0 if upward else z + step <= zn - 1

    def received(a, step, upward):
        @pl.when(arrives(step, upward))
        def _():
            along(a, step, upward).wait_recv()
            in_plane(a, step, upward, 0).start()
            in_plane(a, step, upward, 1).start()

        if step < zn - 1:

            @pl.when(arrives(step, upward) & sends_along(step + 1, upward))
            def _():
                along(a, step + 1, upward).start()

    def passed_on(a, step, upward):
        @pl.when(arrives(step, upward))
        def _():
            in_plane(a, step, upward, 0).wait_recv()
            in_plane(a, step, upward, 2).start()
            in_plane(a, step, upward, 1).wait_recv()
            in_plane(a, step, upward, 3).start()

    def completed(a, step, upward):
        @pl.when(arrives(step, upward))
        def _():
            in_plane(a, step, upward, 2).wait_recv()
            in_plane(a, step, upward, 3).wait_recv()
            in_plane(a, step, upward, 4).start()

    lag = 3
    group = 2 * (zn - 1)

    def advance(i):
        if i % group == 0 and 2 <= i // group + 1 < count:
            offered(i // group + 1)
        if 0 <= i - 2 * lag < len(items):
            completed(*items[i - 2 * lag])
        if 0 <= i - lag < len(items):
            passed_on(*items[i - lag])
        if i < len(items):
            received(*items[i])

    def settle(a):
        take, keep, give = own[a]
        keep.wait()
        give.wait_recv()
        for b, step, upward in items:
            if b == a:

                @pl.when(arrives(step, upward))
                def _(step=step, upward=upward):
                    in_plane(a, step, upward, 4).wait_recv()

        settled.append(a)

    def run_loop(length, body, steps):
        def step(i, carried_through):
            body(i)
            for at, move in enumerate(steps):
                pl.when(i == at * length // len(steps))(functools.partial(advance, move))
            return carried_through

        lax.fori_loop(0, length, step, 0)

    def streamed(length, fetches, body, steps):
        for fetch in fetches:
            fetch(0).start()

        def with_blocks(i):
            @pl.when(i + 1 < length)
            def _():
                for fetch in fetches:
                    fetch(i + 1).start()

            for fetch in fetches:
                fetch(i).wait()
            body(i, i % 2)

        run_loop(length, with_blocks, steps)

    def column_fetch(a, rows, first, width, buffer, sem):
        def fetch(i):
            columns = pl.ds(pl.multiple_of(first + i * width, 128), width)
            return pltpu.make_async_copy(
                outs[a].at[rows, columns], buffer.at[i % 2], w_sem.at[sem * 2 + i % 2]
            )

        return fetch

    ends = [group * (a + 1) + 2 * lag for a in range(count)]
    last = len(items) + 2 * lag
    SMALL, TALL, WIDE = 0, 1, 2
    for i in range(min(ends[TALL], last)):
        advance(i)
    settle(SMALL)
    settle(TALL)
    facts = pltpu.make_async_copy(outs[SMALL].at[:, PD : PD + LANES], facts_ref, local_sem.at[SMALL])
    facts.start()

    def embed(i, slot):
        at = pl.ds(pl.multiple_of(i * 256, 128), 256)
        t0_ref[:, at] = matmul(chosen_ref[...], embed_buf[slot]) + table_ref[:, at]

    waiting = list(range(ends[TALL], min(ends[WIDE], last)))
    streamed(4, [column_fetch(TALL, pl.ds(0, PATCH), 0, 256, embed_buf, 0)], embed, waiting[:2])
    facts.wait()
    gain_rows = jnp.transpose(facts_ref[...].astype(jnp.float32))
    normed_rows(t0_ref, a_ref, HALF, gain_rows[3:4, :], 96)
    for i in waiting[2:]:
        advance(i)
    settle(WIDE)

    rest = list(range(ends[WIDE], last))
    cuts = [len(rest) * part // 80 for part in (0, 8, 12, 48, 54, 80)]
    rest = [rest[cuts[i] : cuts[i + 1]] for i in range(5)]
    whole_rows = pl.ds(0, D)

    def keys_values(i, slot):
        at = pl.ds(pl.multiple_of(i * 256, 128), 256)
        near_ref[:, at] = matmul(a_ref[...], qkv_buf[slot]).astype(jnp.bfloat16)

    def queries(i, slot):
        at = pl.ds(pl.multiple_of(i * 256, 128), 256)
        q_ref[:, at] = matmul(a_ref[SKIP:, :], qkv_buf[slot]).astype(jnp.bfloat16)

    streamed(8, [column_fetch(WIDE, whole_rows, D, 256, qkv_buf, 1)], keys_values, rest[0])
    share = pltpu.make_async_remote_copy(
        src_ref=near_ref,
        dst_ref=far_ref,
        send_sem=kv_sem.at[0],
        recv_sem=kv_sem.at[1],
        device_id=mate,
        device_id_type=MESH,
    )
    share.start()
    streamed(4, [column_fetch(WIDE, whole_rows, 0, 256, qkv_buf, 1)], queries, rest[1])
    share.wait()
    block_rows = (HALF - SKIP) // 2

    def attention(i):
        lanes = pl.ds(pl.multiple_of(i // 2 * LANES, LANES), LANES)
        values = pl.ds(pl.multiple_of(D + i // 2 * LANES, LANES), LANES)
        rows = pl.ds(pl.multiple_of(i % 2 * block_rows, 16), block_rows)
        attend_kernel(
            D // HE, False, None, q_ref.at[rows, lanes], near_ref.at[:, lanes],
            near_ref.at[:, values], far_ref.at[:, lanes], far_ref.at[:, values],
            o_ref.at[rows, lanes], None,
        )

    run_loop(2 * D // LANES, attention, rest[2])

    def merge(i, slot):
        at = pl.ds(pl.multiple_of(i * 256, 128), 256)
        stream = t0_ref[SKIP:, at] + matmul(o_ref[...], qkv_buf[slot])
        sum_ref[:, at] = stream.astype(jnp.bfloat16).astype(jnp.float32)

    streamed(4, [column_fetch(WIDE, whole_rows, 3 * D, 256, qkv_buf, 1)], merge, rest[3])

    row_count = HALF - SKIP
    normed_rows(sum_ref, a_ref, row_count, gain_rows[4:5, :], 96)

    def down_fetch(i):
        rows = pl.ds(pl.multiple_of(PATCH + i * 512, 16), 512)
        return pltpu.make_async_copy(outs[TALL].at[rows, :], down_buf.at[i % 2], w_sem.at[6 + i % 2])

    def feed(i, slot):
        for part in range(2):
            rows = pl.ds(part * block_rows, block_rows)
            h_ref[...] = gelu_erf(matmul(a_ref[rows, :], up_buf[slot])).astype(jnp.bfloat16)
            sum_ref[rows, :] += matmul(h_ref[...], down_buf[slot])

    streamed(
        8,
        [column_fetch(WIDE, whole_rows, 4 * D, 512, up_buf, 2), down_fetch],
        feed,
        rest[4],
    )
    normed_rows(sum_ref, goal_ref, row_count, gain_rows[5:6, :], 96, twice=True)

    for a in range(count):
        if a not in settled:
            settle(a)
    for take, keep, give in own:
        give.wait_send()
    for a, step, upward in items:

        @pl.when(sends_along(step, upward))
        def _(a=a, step=step, upward=upward):
            along(a, step, upward).wait_send()

        @pl.when(arrives(step, upward))
        def _(a=a, step=step, upward=upward):
            for kind in range(5):
                in_plane(a, step, upward, kind).wait_send()


def gather_and_teach(blocks, chosen, table):
    count = len(blocks)
    dp_size = lax.axis_size("dp")
    zn = dp_size // 2
    return pl.pallas_call(
        functools.partial(gather_kernel, count, zn),
        in_specs=[pl.BlockSpec(memory_space=pl.ANY)] * count
        + [pl.BlockSpec(memory_space=pltpu.VMEM)] * 2,
        out_specs=[pl.BlockSpec(memory_space=pl.ANY)] * count
        + [pl.BlockSpec(memory_space=pltpu.VMEM)],
        out_shape=[
            jax.ShapeDtypeStruct((member.shape[0] * dp_size, member.shape[1]), member.dtype)
            for member in blocks
        ]
        + [jax.ShapeDtypeStruct((HALF - SKIP, D), jnp.bfloat16)],
        scratch_shapes=[pltpu.VMEM(member.shape, member.dtype) for member in blocks]
        + [
            pltpu.VMEM((D, LANES), jnp.bfloat16),
            pltpu.VMEM((HALF, D), jnp.float32),
            pltpu.VMEM((HALF, D), jnp.bfloat16),
            pltpu.VMEM((HALF, 2 * D), jnp.bfloat16),
            pltpu.VMEM((HALF, 2 * D), jnp.bfloat16),
            pltpu.VMEM((HALF - SKIP, D), jnp.bfloat16),
            pltpu.VMEM((HALF - SKIP, D), jnp.bfloat16),
            pltpu.VMEM(((HALF - SKIP) // 2, 512), jnp.bfloat16),
            pltpu.VMEM((HALF - SKIP, D), jnp.float32),
            pltpu.VMEM((2, PATCH, 256), jnp.bfloat16),
            pltpu.VMEM((2, D, 256), jnp.bfloat16),
            pltpu.VMEM((2, D, 512), jnp.bfloat16),
            pltpu.VMEM((2, 512, D), jnp.bfloat16),
        ]
        + [
            pltpu.SemaphoreType.DMA((count,)),
            pltpu.SemaphoreType.DMA((count * (zn - 1) * 2,)),
            pltpu.SemaphoreType.DMA((count * (zn - 1) * 2,)),
            pltpu.SemaphoreType.DMA((count * ((zn - 1) * 10 + 1),)),
            pltpu.SemaphoreType.DMA((count * ((zn - 1) * 10 + 1),)),
            pltpu.SemaphoreType.DMA((8,)),
            pltpu.SemaphoreType.DMA((2,)),
        ],
        compiler_params=pltpu.CompilerParams(
            collective_id=0, has_side_effects=True, vmem_limit_bytes=VMEM_LIMIT
        ),
    )(*blocks, chosen, table)


def upper_rows(size):
    return (size + 31) // 32 * 16


def add_blocks(rows, targets):
    def step(i, carried_through):
        at = pl.ds(pl.multiple_of(i * 16, 16), 16)
        for out, terms in targets:
            out[at, :] = sum(term[at, :].astype(jnp.float32) for term in terms).astype(out.dtype)
        return carried_through

    lax.fori_loop(0, rows // 16, step, 0)


def reduce_kernel(count, zn, *refs):
    ins, refs = refs[: count + 1], refs[count + 1 :]
    outs, refs = refs[: count + 1], refs[count + 1 :]
    whole, refs = refs[:count], refs[count:]
    near_one, refs = refs[:count], refs[count:]
    far_one, refs = refs[:count], refs[count:]
    far_two, refs = refs[:count], refs[count:]
    near_two, refs = refs[:count], refs[count:]
    along, refs = refs[:count], refs[count:]
    loaded, refs = refs[:count], refs[count:]
    held, refs = refs[:count], refs[count:]
    done, refs = refs[:count], refs[count:]
    total_ref, side_ref, line_ref, load_sem, move_send, move_recv, side_send, side_recv, line_send, line_recv = refs
    tally, out_total = ins[count], outs[count]
    tally_rows = out_total.shape[0]

    section, place = lax.axis_index("section"), lax.axis_index("dp")
    z, core = place // 2, place % 2
    x_quarter = section + 1 - 2 * (section % 2)
    y_quarter = (section + 2) % 4
    xy_quarter = (x_quarter + 2) % 4
    near, far = {"section": x_quarter}, {"section": y_quarter}
    mate = {"dp": place + 1 - 2 * core}
    sizes = [out.shape[0] for out in outs[:count]]
    widths = [out.shape[1] // 4 for out in outs[:count]]

    barrier = pltpu.get_barrier_semaphore()
    line = [{"dp": (z + j) % zn * 2 + core} for j in range(1, zn)]
    for other in [near, far, mate] + line:
        pl.semaphore_signal(barrier, inc=1, device_id=other, device_id_type=MESH)
    pl.semaphore_wait(barrier, 3 + len(line))

    def rows_at(a, slot, start=0, length=None):
        return pl.ds(pl.multiple_of(slot * sizes[a] + start, 16), sizes[a] if length is None else length)

    def quarter_at(a, quarter):
        return pl.ds(pl.multiple_of(quarter * widths[a], 128), widths[a])

    def upper(a):
        return upper_rows(sizes[a])

    def lower(a):
        return sizes[a] - upper_rows(sizes[a])

    def sent(src, dst, kind, a, slot, device):
        index = (kind * count + a) * (zn + 1) + slot
        return pltpu.make_async_remote_copy(
            src_ref=src,
            dst_ref=dst,
            send_sem=move_send.at[index],
            recv_sem=move_recv.at[index],
            device_id=device,
            device_id_type=MESH,
        )

    def load(a, owner_z):
        source = pl.ds(pl.multiple_of((owner_z * 2 + core) * sizes[a], 16), sizes[a])
        return pltpu.make_async_copy(
            ins[a].at[source, :], loaded[a].at[rows_at(a, owner_z), :], load_sem.at[a * zn + owner_z]
        )

    def give(a, owner_z):
        source = pl.ds(pl.multiple_of((owner_z * 2 + 1 - core) * sizes[a], 16), sizes[a])
        return sent(ins[a].at[source, :], whole[a].at[rows_at(a, owner_z), :], 0, a, owner_z, mate)

    def first_near(a, owner_z, which):
        quarter = (x_quarter, xy_quarter)[which]
        return sent(
            whole[a].at[rows_at(a, owner_z, 0, upper(a)), quarter_at(a, quarter)],
            near_one[a].at[pl.ds(pl.multiple_of((owner_z * 2 + which) * upper(a), 16), upper(a)), :],
            1 + which, a, owner_z, near,
        )

    def first_far(a, owner_z, which):
        quarter = (y_quarter, xy_quarter)[which]
        return sent(
            whole[a].at[rows_at(a, owner_z, upper(a), lower(a)), quarter_at(a, quarter)],
            far_one[a].at[pl.ds(pl.multiple_of((owner_z * 2 + which) * lower(a), 16), lower(a)), :],
            3 + which, a, owner_z, far,
        )

    def second_far(a, owner_z):
        return sent(
            whole[a].at[rows_at(a, owner_z, 0, upper(a)), quarter_at(a, y_quarter)],
            far_two[a].at[pl.ds(pl.multiple_of(owner_z * upper(a), 16), upper(a)), :],
            5, a, owner_z, far,
        )

    def second_near(a, owner_z):
        return sent(
            whole[a].at[rows_at(a, owner_z, upper(a), lower(a)), quarter_at(a, x_quarter)],
            near_two[a].at[pl.ds(pl.multiple_of(owner_z * lower(a), 16), lower(a)), :],
            6, a, owner_z, near,
        )

    def onward(a, owner_z, upward, last):
        slot = zn if last and not upward else owner_z
        return sent(
            whole[a].at[rows_at(a, owner_z), quarter_at(a, section)],
            along[a].at[rows_at(a, slot), :],
            7, a, slot, {"dp": place + 2 if upward else place - 2},
        )

    def finished(a, kind):
        quarter = (section, section, x_quarter, y_quarter)[kind]
        columns = quarter_at(a, quarter)
        part = (
            pl.ds(0, sizes[a]), pl.ds(0, sizes[a]), pl.ds(0, upper(a)), pl.ds(upper(a), lower(a))
        )[kind]
        src = done[a] if kind < 2 else outs[a].at[part, columns]
        return sent(src, outs[a].at[part, columns], 8 + kind, a, 0, (near, far, far, near)[kind])

    def keep(a):
        return pltpu.make_async_copy(
            done[a], outs[a].at[:, quarter_at(a, section)], load_sem.at[a * zn]
        )

    legs = [(k, upward) for k in range(zn - 1, 0, -1) for upward in (True, False)] + [(0, True)]
    items = [(a, leg) for leg in range(len(legs)) for a in range(count)]

    def owner_of(leg):
        k, upward = legs[leg]
        return z + k if upward else z - k

    def is_live(leg):
        k, upward = legs[leg]
        return (z + k <= zn - 1) if upward else (z - k >= 0)

    def started(a, leg):
        @pl.when(is_live(leg))
        def _():
            give(a, owner_of(leg)).start()

    def load_started(a, leg):
        @pl.when(is_live(leg))
        def _():
            load(a, owner_of(leg)).start()

    def parts(a, owner_z, is_upper, quarter):
        size = (0, upper(a)) if is_upper else (upper(a), lower(a))
        at = (rows_at(a, owner_z, *size), quarter_at(a, quarter))
        return (whole[a].at[at], loaded[a].at[at])

    def pair_up(a, owner_z, is_upper, quarter):
        both = parts(a, owner_z, is_upper, quarter)
        add_blocks(upper(a) if is_upper else lower(a), [(both[0], both)])

    def paired(a, leg):
        @pl.when(is_live(leg))
        def _():
            owner_z = owner_of(leg)
            load(a, owner_z).wait()
            give(a, owner_z).wait_recv()
            for quarter in (xy_quarter, x_quarter):
                pair_up(a, owner_z, True, quarter)
            for quarter in (xy_quarter, y_quarter):
                pair_up(a, owner_z, False, quarter)
            for which in (1, 0):
                first_near(a, owner_z, which).start()
                first_far(a, owner_z, which).start()


    def from_near(a, owner_z, which):
        start = pl.multiple_of((owner_z * 2 + which) * upper(a), 16)
        return near_one[a].at[pl.ds(start, upper(a)), :]

    def from_far(a, owner_z, which):
        start = pl.multiple_of((owner_z * 2 + which) * lower(a), 16)
        return far_one[a].at[pl.ds(start, lower(a)), :]

    def halved(a, leg):
        @pl.when(is_live(leg))
        def _():
            owner_z = owner_of(leg)
            first_near(a, owner_z, 1).wait_recv()
            both = parts(a, owner_z, True, y_quarter)
            add_blocks(upper(a), [(both[0], both + (from_near(a, owner_z, 1),))])
            second_far(a, owner_z).start()
            first_far(a, owner_z, 1).wait_recv()
            both = parts(a, owner_z, False, x_quarter)
            add_blocks(lower(a), [(both[0], both + (from_far(a, owner_z, 1),))])
            second_near(a, owner_z).start()

    def quartered(a, leg):
        k, upward = legs[leg]

        @pl.when(is_live(leg))
        def _():
            owner_z = owner_of(leg)
            own = quarter_at(a, section)
            first_near(a, owner_z, 0).wait_recv()
            second_far(a, owner_z).wait_recv()
            start = pl.multiple_of(owner_z * upper(a), 16)
            terms = parts(a, owner_z, True, section) + (
                from_near(a, owner_z, 0), far_two[a].at[pl.ds(start, upper(a)), :]
            )
            add_blocks(upper(a), [(held[a].at[pl.ds(0, upper(a)), :], terms)])
            first_far(a, owner_z, 0).wait_recv()
            second_near(a, owner_z).wait_recv()
            start = pl.multiple_of(owner_z * lower(a), 16)
            terms = parts(a, owner_z, False, section) + (
                from_far(a, owner_z, 0), near_two[a].at[pl.ds(start, lower(a)), :]
            )
            add_blocks(lower(a), [(held[a].at[pl.ds(upper(a), lower(a)), :], terms)])
            target = held[a]

            def join(upward_from, slot):
                onward(a, owner_z, upward_from, slot is not owner_z or k == 0).wait_recv()
                add_blocks(sizes[a], [(target, (target, along[a].at[rows_at(a, slot), :]))])

            if k > 0:

                @pl.when(z > 0 if upward else z < zn - 1)
                def _():
                    join(upward, owner_z)

                add_blocks(sizes[a], [(whole[a].at[rows_at(a, owner_z), own], (target,))])
                onward(a, owner_z, upward, k == 1).start()
            else:

                @pl.when(z > 0)
                def _():
                    join(True, owner_z)

                @pl.when(z < zn - 1)
                def _():
                    join(False, zn)

                def settle(i, carried_through):
                    at = pl.ds(pl.multiple_of(i * 16, 16), 16)
                    values = target[at, :]
                    done[a][at, :] = values.astype(done[a].dtype)
                    squares = values * values
                    squares = squares[:8] + squares[8:]
                    carried = total_ref[0:8, :]
                    for column in range(0, widths[a], 128):
                        carried = carried + squares[:, column : column + 128]
                    total_ref[0:8, :] = carried
                    return carried_through

                lax.fori_loop(0, sizes[a] // 16, settle, 0)
                keep(a).start()
                finished(a, 0).start()
                finished(a, 1).start()

    total_ref[0:8, :] = jnp.zeros((8, 128), jnp.float32)
    tally_copy = pltpu.make_async_copy(tally, total_ref.at[8:, :], load_sem.at[count * zn])
    tally_copy.start()
    for a, leg in items:
        started(a, leg)
        load_started(a, leg)
    lag = 5
    for i in range(len(items) + 2 * lag):
        if i < len(items):
            paired(*items[i])
        if 0 <= i - lag < len(items):
            halved(*items[i - lag])
        if 0 <= i - 2 * lag < len(items):
            quartered(*items[i - 2 * lag])

    tally_copy.wait()

    def exchanged(stage, device):
        return pltpu.make_async_remote_copy(
            src_ref=total_ref,
            dst_ref=side_ref.at[pl.ds(stage * tally_rows, tally_rows), :],
            send_sem=side_send.at[stage],
            recv_sem=side_recv.at[stage],
            device_id=device,
            device_id_type=MESH,
        )

    for stage, device in enumerate((mate, near, far)):
        swap = exchanged(stage, device)
        swap.start()
        swap.wait()
        total_ref[...] += side_ref[stage * tally_rows : (stage + 1) * tally_rows, :]

    def told(from_z, to_z, j):
        index = from_z * zn + to_z
        return pltpu.make_async_remote_copy(
            src_ref=total_ref,
            dst_ref=line_ref.at[pl.ds(pl.multiple_of(from_z * tally_rows, 8), tally_rows), :],
            send_sem=line_send.at[index],
            recv_sem=line_recv.at[index],
            device_id={"dp": to_z * 2 + core},
            device_id_type=MESH,
        )

    for j in range(1, zn):
        told(z, (z + j) % zn, j).start()
    line_ref[pl.ds(pl.multiple_of(z * tally_rows, 8), tally_rows), :] = total_ref[...]
    for j in range(1, zn):
        told((z + j) % zn, z, j).wait_recv()
    grand = line_ref[0:tally_rows, :]
    for j in range(1, zn):
        grand = grand + line_ref[j * tally_rows : (j + 1) * tally_rows, :]
    for j in range(1, zn):
        told(z, (z + j) % zn, j).wait_send()
    total_ref[...] = grand
    show = pltpu.make_async_copy(total_ref, out_total, load_sem.at[count * zn])
    show.start()

    for a in range(count):
        finished(a, 0).wait_recv()
        finished(a, 2).start()
        finished(a, 1).wait_recv()
        finished(a, 3).start()
    for a in range(count):
        keep(a).wait()
        finished(a, 2).wait_recv()
        finished(a, 3).wait_recv()
        for kind in range(4):
            finished(a, kind).wait_send()
    for a, leg in items:
        k, upward = legs[leg]

        @pl.when(is_live(leg))
        def _(a=a, leg=leg, k=k, upward=upward):
            owner_z = owner_of(leg)
            give(a, owner_z).wait_send()
            for which in (0, 1):
                first_near(a, owner_z, which).wait_send()
                first_far(a, owner_z, which).wait_send()
            second_near(a, owner_z).wait_send()
            second_far(a, owner_z).wait_send()
            if k > 0:
                onward(a, owner_z, upward, k == 1).wait_send()

    show.wait()


def reduce_blocks(blocks, tally, result_types):
    count = len(blocks)
    dp_size = lax.axis_size("dp")
    zn = dp_size // 2
    tally_rows = 8 + tally.shape[0]
    shapes = [(member.shape[0] // dp_size, member.shape[1]) for member in blocks]
    vmem = lambda rows, columns, dtype=jnp.bfloat16: pltpu.VMEM((rows, columns), dtype)
    anywhere = pl.BlockSpec(memory_space=pl.ANY)
    moves = 12 * count * (zn + 1)
    return pl.pallas_call(
        functools.partial(reduce_kernel, count, zn),
        in_specs=[anywhere] * (count + 1),
        out_specs=[anywhere] * (count + 1),
        out_shape=[jax.ShapeDtypeStruct(shape, kind) for shape, kind in zip(shapes, result_types)]
        + [jax.ShapeDtypeStruct((tally_rows, 128), jnp.float32)],
        scratch_shapes=[vmem(zn * r, w) for r, w in shapes]
        + [vmem(zn * 2 * upper_rows(r), w // 4) for r, w in shapes]
        + [vmem(zn * 2 * (r - upper_rows(r)), w // 4) for r, w in shapes]
        + [vmem(zn * upper_rows(r), w // 4) for r, w in shapes]
        + [vmem(zn * (r - upper_rows(r)), w // 4) for r, w in shapes]
        + [vmem((zn + 1) * r, w // 4) for r, w in shapes]
        + [vmem(zn * r, w) for r, w in shapes]
        + [vmem(r, w // 4, jnp.float32) for r, w in shapes]
        + [vmem(r, w // 4, kind) for (r, w), kind in zip(shapes, result_types)]
        + [
            vmem(tally_rows, 128, jnp.float32),
            vmem(3 * tally_rows, 128, jnp.float32),
            vmem(zn * tally_rows, 128, jnp.float32),
            pltpu.SemaphoreType.DMA((count * zn + 1,)),
            pltpu.SemaphoreType.DMA((moves,)),
            pltpu.SemaphoreType.DMA((moves,)),
            pltpu.SemaphoreType.DMA((3,)),
            pltpu.SemaphoreType.DMA((3,)),
            pltpu.SemaphoreType.DMA((zn * zn,)),
            pltpu.SemaphoreType.DMA((zn * zn,)),
        ],
        compiler_params=pltpu.CompilerParams(
            collective_id=1, has_side_effects=True, vmem_limit_bytes=60 * 1024 * 1024
        ),
    )(*blocks, tally)


def adamw_step(weight, grad_now, first, second, decay, rate):
    first = BETA_ONE * first + (1.0 - BETA_ONE) * grad_now
    second = BETA_TWO * second + (1.0 - BETA_TWO) * grad_now * grad_now
    ratio = first / (1.0 - BETA_ONE**STEP) / (jnp.sqrt(second / (1.0 - BETA_TWO**STEP)) + EPSILON)
    return (weight - rate * (ratio + decay * weight), first, second)


def local(
    pixels,
    token_order,
    visible,
    wide_weight,
    tall_weight,
    pred_weight,
    pred_down,
    enc_gains,
    pred_gains,
    wide_first,
    tall_first,
    pred_first,
    pred_down_first,
    enc_gains_first,
    pred_gains_first,
    wide_second,
    tall_second,
    pred_second,
    pred_down_second,
    enc_gains_second,
    pred_gains_second,
    teacher_wide,
    teacher_tall,
    teacher_gains,
):
    masters = (wide_weight, tall_weight, pred_weight, pred_down, enc_gains, pred_gains)
    section_idx = lax.axis_index("section")
    section_count = lax.axis_size("section")
    core = lax.axis_index("dp") % 2
    clips_here = pixels.shape[0]
    assert section_count == 2 * clips_here

    owner = section_idx // clips_here
    clip = section_idx % clips_here
    holds = core == owner
    counts_own = lax.dynamic_index_in_dim(visible, clip, 0)
    order_own = lax.dynamic_index_in_dim(token_order, clip, 0, keepdims=False)
    clip_facts = jnp.concatenate([order_own, counts_own])
    clip_facts = jnp.where(holds, clip_facts, swapped(clip_facts))
    seen = clip_facts[L]
    order_pairs = clip_facts[:L].reshape(HALF, 2)
    order = jnp.where(core == 0, order_pairs[:, 0], order_pairs[:, 1])
    pairs_own = order_own.reshape(HALF, 2)
    order_here = jnp.where(core == 0, pairs_own[:, 0], pairs_own[:, 1])
    order_there = jnp.where(core == 0, pairs_own[:, 1], pairs_own[:, 0])
    pixel_rows = lax.dynamic_index_in_dim(pixels, clip, 0, keepdims=False)
    for_here = picked_rows(pixel_rows, order_here)
    for_there = picked_rows(pixel_rows, order_there)
    chosen = jnp.where(holds, for_here, swapped(for_there))
    seen_near = (seen - core + 1) // 2
    seen_far = (seen + core) // 2
    kept = jnp.stack([seen_near, seen_far])
    visible_high, visible_low = visible // LANES, visible % LANES
    dp_size = lax.axis_size("dp")
    row_count = wide_weight.shape[0]
    small = jnp.concatenate(
        [
            wide_weight[:, 4 * D + FF :],
            enc_gains,
            teacher_gains,
            jnp.pad(pred_gains, ((0, row_count - pred_gains.shape[0]), (0, 0))),
            jnp.zeros((row_count, LANES - 10 - 2 * clips_here), jnp.float32),
            jnp.broadcast_to(
                jnp.concatenate([visible_high, visible_low]).astype(jnp.float32)[None, :],
                (row_count, 2 * clips_here),
            ),
        ],
        axis=1,
    )
    pred_block = pred_weight.shape if pred_weight.shape[0] % 16 == 0 else (-1, D)
    pred_form = (PD, pred_weight.shape[1]) if pred_weight.shape[0] % 16 == 0 else (-1, D)
    blocks = (
        small,
        teacher_tall,
        teacher_wide,
        tall_weight,
        wide_weight[:, : 4 * D + FF],
        pred_weight.reshape(pred_block),
        jnp.pad(pred_down, ((0, 0), (0, LANES))),
    )
    table = position_table(order, D)
    w_small, teach_tall, teach_wide, w_tall, w_wide, w_pred, w_down, goal = gather_and_teach(
        tuple(member.astype(jnp.bfloat16) for member in blocks), chosen, table
    )
    goal = goal.astype(jnp.float32)
    w_pred = w_pred.reshape(PD, -1)
    w_down = w_down[:, :PD]
    pred_embed = w_small[:, :PD]
    enc_copy = w_small[:, PD : PD + 3]
    pred_copy = w_small[:, PD + 6 : PD + 10].reshape(dp_size, row_count, 4)
    pred_copy = pred_copy[:, : pred_gains.shape[0]].reshape(PD, 4)
    counts = w_small[::row_count, PD + LANES - 2 * clips_here :].astype(jnp.float32)
    counts = counts[:, :clips_here] * LANES + counts[:, clips_here:]
    target_total = jnp.sum(L - counts)
    enc_gain = enc_copy.astype(jnp.float32)
    pred_gain = pred_copy.astype(jnp.float32)
    enc_attn = (w_wide[:, : 3 * D], w_wide[:, 3 * D : 4 * D])
    enc_feed = (w_wide[:, 4 * D : 4 * D + FF], w_tall[PATCH:])
    pred_attn = (w_pred[:, : 3 * PD], w_pred[:, 3 * PD : 4 * PD])
    pred_feed = (w_pred[:, 4 * PD : 4 * PD + PF], w_down)
    pred_head = w_pred[:, 4 * PD + PF :]

    pred_table = position_table(order, PD)
    row_ids = lax.iota(jnp.int32, HALF)
    context = (row_ids < seen_near)[:, None]

    enc_chosen = chosen[:SEEN]
    stream_a = matmul(enc_chosen, w_tall[:PATCH]) + table[:SEEN]
    stream_b, stored_a = attend_fwd(
        stream_a, enc_gain[:, 0], enc_attn[0], enc_attn[1], HE, kept, 0, SEEN
    )
    stream_b = stream_b.astype(jnp.bfloat16).astype(jnp.float32)
    stream_c, stored_b = feed_fwd(stream_b, enc_gain[:, 1], enc_feed[0], enc_feed[1])
    encoded = scaled(stream_c, enc_gain[:, 2]).astype(jnp.bfloat16)

    projected = padded_rows(matmul(encoded, pred_embed), 0, HALF - SEEN)
    stream_d = jnp.where(context, projected, pred_gain[:, 3][None, :]) + pred_table
    stream_e, stored_d = attend_fwd(
        stream_d, pred_gain[:, 0], pred_attn[0], pred_attn[1], PH, None, SKIP, 336
    )
    stream_e = stream_e.astype(jnp.bfloat16).astype(jnp.float32)
    stream_f, stored_e = feed_fwd(stream_e, pred_gain[:, 1], pred_feed[0], pred_feed[1])
    final = scaled(stream_f, pred_gain[:, 2]).astype(jnp.bfloat16)
    residual = matmul(final, pred_head) - goal
    smooth_err = jnp.sqrt(residual * residual + 1.0)
    target_mask = jnp.logical_not(context[SKIP:])
    loss_part = jnp.sum(jnp.where(target_mask, smooth_err - 1.0, 0.0))
    grad_guess = (jnp.where(target_mask, residual / smooth_err, 0.0) / target_total).astype(
        jnp.bfloat16
    )

    grad_head = inner_rows(final, grad_guess)
    grad_final = outer_rows(grad_guess, pred_head).astype(jnp.bfloat16).astype(jnp.float32)
    grad_stream, grad_pg2 = scaled_back(stream_f, pred_gain[:, 2], grad_final)
    grad_stream, grad_pup, branch_grad, grad_pg1 = feed_back(
        stream_e, pred_gain[:, 1], pred_feed[0], pred_feed[1], stored_e, grad_stream
    )
    grad_down = inner_rows(stored_e[2], branch_grad)
    grad_stream = grad_stream.astype(jnp.bfloat16).astype(jnp.float32)
    grad_stream, grad_pin, grad_pout, grad_pg0 = attend_back(
        stream_d, pred_gain[:, 0], pred_attn[0], pred_attn[1], PH, None, SKIP, 336, stored_d, grad_stream
    )
    grad_token = jnp.sum(jnp.where(context, 0.0, grad_stream), axis=0)
    grad_projected = jnp.where(context, grad_stream, 0.0)[:SEEN].astype(jnp.bfloat16)
    grad_embed = inner_rows(encoded, grad_projected)
    grad_encoded = outer_rows(grad_projected, pred_embed).astype(jnp.bfloat16).astype(jnp.float32)
    grad_stream, grad_eg2 = scaled_back(stream_c, enc_gain[:, 2], grad_encoded)
    grad_stream, grad_eup, branch_grad, grad_eg1 = feed_back(
        stream_b, enc_gain[:, 1], enc_feed[0], enc_feed[1], stored_b, grad_stream
    )
    grad_stream = grad_stream.astype(jnp.bfloat16).astype(jnp.float32)
    grad_stream, grad_ein, grad_eout, grad_eg0 = attend_back(
        stream_a, enc_gain[:, 0], enc_attn[0], enc_attn[1], HE, kept, 0, SEEN, stored_a, grad_stream
    )
    grad_tall = tall_grad(
        chosen[:SEEN], grad_stream.astype(jnp.bfloat16), stored_b[2], branch_grad
    )

    gain_grads = jnp.concatenate(
        [
            jnp.stack([grad_eg0, grad_eg1, grad_eg2], axis=1).reshape(-1, LANES),
            jnp.stack([grad_pg0, grad_pg1, grad_pg2, grad_token], axis=1).reshape(-1, LANES),
        ],
        axis=0,
    )
    gain_rows = 3 * D // LANES
    loss_tile = jnp.zeros((8, LANES), jnp.float32).at[0, 0].set(loss_part)
    tally = jnp.concatenate(
        [loss_tile, gain_grads, jnp.zeros((4, LANES), jnp.float32)], axis=0
    )
    blocks = shortened(
        (
            grad_ein,
            grad_eout,
            grad_eup,
            jnp.pad(grad_embed, ((0, 0), (0, LANES))),
            grad_tall,
            jnp.concatenate(shortened([grad_pin, grad_pout, grad_pup, grad_head]), axis=1).reshape(pred_form),
            jnp.pad(grad_down, ((0, 0), (0, LANES))),
        )
    )
    *summed, tally = reduce_blocks(
        blocks, tally, [jnp.bfloat16] * 5 + [jnp.float32] * 2
    )
    wide_parts = [summed[0], summed[1], summed[2], summed[3][:, :PD]]
    place = lax.axis_index("dp")
    gains_all = tally[16 : 16 + gain_rows].reshape(D, 3)
    pred_gains_all = tally[16 + gain_rows : 16 + gain_rows + 4 * PD // LANES].reshape(PD, 4)
    shares = (
        jnp.concatenate(wide_parts, axis=1).astype(jnp.float32),
        summed[4].astype(jnp.float32),
        summed[5].reshape(pred_weight.shape).astype(jnp.float32),
        summed[6][:, :PD].astype(jnp.float32),
        lax.dynamic_slice_in_dim(gains_all, place * enc_gains.shape[0], enc_gains.shape[0], 0),
        lax.dynamic_slice_in_dim(pred_gains_all, place * pred_gains.shape[0], pred_gains.shape[0], 0),
    )
    loss_sum = tally[8, 0]
    square_total = jnp.sum(tally[:8]) + jnp.sum(jnp.square(tally[16:]))
    grad_norm = jnp.sqrt(square_total)
    factor = jnp.minimum(1.0, CLIP_AT / (grad_norm + 1e-06))
    firsts = (
        wide_first,
        tall_first,
        pred_first,
        pred_down_first,
        enc_gains_first,
        pred_gains_first,
    )
    seconds = (
        wide_second,
        tall_second,
        pred_second,
        pred_down_second,
        enc_gains_second,
        pred_gains_second,
    )
    decays = (DECAY, DECAY, DECAY, DECAY, 0.0, 0.0)
    rates = (RATE, RATE, RATE, RATE, GAIN_RATE, GAIN_RATE)
    results = [
        adamw_step(
            masters[group_idx],
            shares[group_idx] * factor,
            firsts[group_idx],
            seconds[group_idx],
            decays[group_idx],
            rates[group_idx],
        )
        for group_idx in range(6)
    ]
    news = [entry[0] for entry in results]
    teacher_wide_new = KEEP_RATE * teacher_wide + (1.0 - KEEP_RATE) * news[0][:, : 4 * D + FF]
    teacher_tall_new = KEEP_RATE * teacher_tall + (1.0 - KEEP_RATE) * news[1]
    teacher_gains_new = KEEP_RATE * teacher_gains + (1.0 - KEEP_RATE) * news[4]
    return (
        loss_sum,
        target_total,
        grad_norm,
        news[0],
        news[1],
        news[2],
        news[3],
        news[4],
        news[5],
        results[0][1],
        results[1][1],
        results[2][1],
        results[3][1],
        results[4][1],
        results[5][1],
        results[0][2],
        results[1][2],
        results[2][2],
        results[3][2],
        results[4][2],
        results[5][2],
        news[0].astype(jnp.bfloat16),
        news[1].astype(jnp.bfloat16),
        news[2].astype(jnp.bfloat16),
        news[3].astype(jnp.bfloat16),
        news[4].astype(jnp.bfloat16),
        news[5].astype(jnp.bfloat16),
        teacher_wide_new,
        teacher_tall_new,
        teacher_gains_new,
    )


def solution(mesh):
    return jax.shard_map(
        local,
        mesh=mesh,
        in_specs=(
            P("dp", None, None),
            P("dp", None),
            P("dp"),
            P("dp", None),
            P("dp", None),
            P("dp", None),
            P("dp", None),
            P("dp", None),
            P("dp", None),
            P("dp", None),
            P("dp", None),
            P("dp", None),
            P("dp", None),
            P("dp", None),
            P("dp", None),
            P("dp", None),
            P("dp", None),
            P("dp", None),
            P("dp", None),
            P("dp", None),
            P("dp", None),
            P("dp", None),
            P("dp", None),
            P("dp", None),
        ),
        out_specs=(
            P(),
            P(),
            P(),
            P("dp", None),
            P("dp", None),
            P("dp", None),
            P("dp", None),
            P("dp", None),
            P("dp", None),
            P("dp", None),
            P("dp", None),
            P("dp", None),
            P("dp", None),
            P("dp", None),
            P("dp", None),
            P("dp", None),
            P("dp", None),
            P("dp", None),
            P("dp", None),
            P("dp", None),
            P("dp", None),
            P("dp", None),
            P("dp", None),
            P("dp", None),
            P("dp", None),
            P("dp", None),
            P("dp", None),
            P("dp", None),
            P("dp", None),
            P("dp", None),
        ),
        check_vma=False,
    )
```

```python
import functools
import math

import jax
import jax.numpy as jnp
from jax import lax
from jax.experimental import pallas as pl
from jax.experimental.pallas import tpu as pltpu
from jax.sharding import PartitionSpec as P

D = 1024
HE = 16
FF = 4096
PD = 384
PH = 12
PF = 1536
PATCH = 1536
L = 1536
STEP = 10
VIS = 576
VIS_LO = 192
HALF = L // 2
SEEN = VIS // 2
SKIP = VIS_LO // 2
LANES = 128
VMEM_LIMIT = 50 * 1024 * 1024


BETA_ONE = 0.9
BETA_TWO = 0.999
EPSILON = 1e-08
RATE = 0.02
GAIN_RATE = 0.5
DECAY = 0.05
CLIP_AT = 0.05
KEEP_RATE = 0.8
NEGATIVE = -1e30


def shortened(x):
    return jax.tree.map(lambda a: a.astype(jnp.bfloat16) if a.dtype == jnp.float32 else a, x)


def normed(stream):
    centred = stream - jnp.mean(stream, axis=-1, keepdims=True)
    return centred * lax.rsqrt(jnp.mean(centred * centred, axis=-1, keepdims=True) + 1e-06)


def scaled(stream, gain_vec):
    return normed(stream) * gain_vec


def position_table(positions, feature_width):
    frequency = jnp.exp(
        jnp.arange(feature_width // 2, dtype=jnp.float32)
        * (-2.0 * math.log(10000.0) / feature_width)
    )
    angles = positions.astype(jnp.float32)[:, None] * frequency[None, :]
    return jnp.concatenate([jnp.sin(angles), jnp.cos(angles)], axis=1)


def matmul(left, right):
    return jnp.dot(left, right, preferred_element_type=jnp.float32)


def inner_rows(left, right):
    return lax.dot_general(
        left, right, (((0,), (0,)), ((), ())), preferred_element_type=jnp.float32
    )


def outer_rows(left, right):
    return lax.dot_general(
        left, right, (((1,), (1,)), ((), ())), preferred_element_type=jnp.float32
    )


def head_scores(queries, key_heads, kept):
    logits = outer_rows(queries, key_heads)
    if kept is None:
        return logits
    key_ids = lax.broadcasted_iota(jnp.int32, logits.shape, 1)
    return jnp.where(key_ids < kept, logits, NEGATIVE)


def attend_kernel(head_size, masked, kept_ref, q_ref, k0_ref, v0_ref, k1_ref, v1_ref, o_ref, l_ref):
    exponent = head_size ** (-0.5) * math.log2(math.e)
    lane_head = lax.broadcasted_iota(jnp.int32, (1, LANES), 1) // head_size
    kept = (kept_ref[0], kept_ref[1]) if masked else (None, None)
    queries = q_ref[...]
    merged = jnp.zeros(o_ref.shape, jnp.float32)
    log_totals = jnp.zeros(o_ref.shape, jnp.float32)
    for head in range(LANES // head_size):
        chosen = lane_head == head
        head_queries = jnp.where(chosen, queries, jnp.zeros_like(queries))
        near = head_scores(head_queries, k0_ref[...], kept[0])
        far = head_scores(head_queries, k1_ref[...], kept[1])
        row_max = exponent * jnp.maximum(
            jnp.max(near, axis=1, keepdims=True), jnp.max(far, axis=1, keepdims=True)
        )
        near = jnp.exp2(near * exponent - row_max)
        far = jnp.exp2(far * exponent - row_max)
        row_total = jnp.sum(near, axis=1, keepdims=True) + jnp.sum(far, axis=1, keepdims=True)
        outcome = matmul(near.astype(jnp.bfloat16), v0_ref[...]) + matmul(
            far.astype(jnp.bfloat16), v1_ref[...]
        )
        merged = jnp.where(chosen, outcome / row_total, merged)
        log_totals = jnp.where(chosen, row_max + jnp.log2(row_total), log_totals)
    o_ref[...] = merged.astype(o_ref.dtype)
    if l_ref is not None:
        l_ref[...] = log_totals


def attend_rows(queries, kv_near, kv_far, kept, num_heads, block_rows):
    row_count, width = queries.shape
    keys = kv_near.shape[0]
    groups = width // LANES
    masked = kept is not None
    if not masked:
        kept = jnp.zeros((2,), jnp.int32)
    row_spec = pl.BlockSpec((block_rows, LANES), lambda g, b, kept: (b, g))
    k_spec = pl.BlockSpec((keys, LANES), lambda g, b, kept: (0, g))
    v_spec = pl.BlockSpec((keys, LANES), lambda g, b, kept: (0, g + groups))
    return pl.pallas_call(
        functools.partial(attend_kernel, width // num_heads, masked),
        grid_spec=pltpu.PrefetchScalarGridSpec(
            num_scalar_prefetch=1,
            grid=(groups, row_count // block_rows),
            in_specs=[row_spec, k_spec, v_spec, k_spec, v_spec],
            out_specs=[row_spec, row_spec],
        ),
        out_shape=[
            jax.ShapeDtypeStruct((row_count, width), jnp.bfloat16),
            jax.ShapeDtypeStruct((row_count, width), jnp.float32),
        ],
        compiler_params=pltpu.CompilerParams(vmem_limit_bytes=VMEM_LIMIT),
        cost_estimate=pl.CostEstimate(
            flops=8 * row_count * keys * width,
            bytes_accessed=8 * (row_count + keys) * width,
            transcendentals=2 * row_count * keys * num_heads,
        ),
    )(kept, queries, kv_near, kv_near, kv_far, kv_far)


def attend_back_kernel(
    head_size, masked, kept_ref, q_ref, g_ref, l_ref, k0_ref, v0_ref, k1_ref, v1_ref,
    dq_ref, dk0_ref, dv0_ref, dk1_ref, dv1_ref,
):
    scaling = head_size ** (-0.5)
    exponent = scaling * math.log2(math.e)
    lane_head = lax.broadcasted_iota(jnp.int32, (1, LANES), 1) // head_size
    kept = (kept_ref[0], kept_ref[1]) if masked else (None, None)

    @pl.when(pl.program_id(1) == 0)
    def _():
        for ref in (dk0_ref, dv0_ref, dk1_ref, dv1_ref):
            ref[...] = jnp.zeros_like(ref)

    queries, grads, log_totals = q_ref[...], g_ref[...], l_ref[...]
    grad_queries = jnp.zeros(dq_ref.shape, jnp.float32)
    for head in range(LANES // head_size):
        chosen = lane_head == head
        head_queries = jnp.where(chosen, queries, jnp.zeros_like(queries))
        head_grads = jnp.where(chosen, grads, jnp.zeros_like(grads))
        log_total = log_totals[:, head * head_size : head * head_size + 1]
        probs, steps, totals = [], [], 0.0
        for k_ref, v_ref, count in ((k0_ref, v0_ref, kept[0]), (k1_ref, v1_ref, kept[1])):
            attn = jnp.exp2(head_scores(head_queries, k_ref[...], count) * exponent - log_total)
            step = outer_rows(head_grads, v_ref[...]) * attn
            totals = totals + jnp.sum(step, axis=1, keepdims=True)
            probs.append(attn)
            steps.append(step)
        outcome = 0.0
        for attn, step, k_ref, dk_ref, dv_ref in zip(
            probs, steps, (k0_ref, k1_ref), (dk0_ref, dk1_ref), (dv0_ref, dv1_ref)
        ):
            grad_logits = (step - attn * totals).astype(jnp.bfloat16)
            dv_ref[...] += inner_rows(attn.astype(jnp.bfloat16), head_grads)
            dk_ref[...] += inner_rows(grad_logits, head_queries) * scaling
            outcome = outcome + matmul(grad_logits, k_ref[...])
        grad_queries = jnp.where(chosen, outcome * scaling, grad_queries)
    dq_ref[...] = grad_queries.astype(dq_ref.dtype)


def attend_rows_back(queries, grads, log_totals, kv_near, kv_far, kept, num_heads, block_rows):
    row_count, width = queries.shape
    keys = kv_near.shape[0]
    groups = width // LANES
    masked = kept is not None
    if not masked:
        kept = jnp.zeros((2,), jnp.int32)
    row_spec = pl.BlockSpec((block_rows, LANES), lambda g, b, kept: (b, g))
    k_spec = pl.BlockSpec((keys, LANES), lambda g, b, kept: (0, g))
    v_spec = pl.BlockSpec((keys, LANES), lambda g, b, kept: (0, g + groups))
    key_shape = jax.ShapeDtypeStruct((keys, width), jnp.float32)
    return pl.pallas_call(
        functools.partial(attend_back_kernel, width // num_heads, masked),
        grid_spec=pltpu.PrefetchScalarGridSpec(
            num_scalar_prefetch=1,
            grid=(groups, row_count // block_rows),
            in_specs=[row_spec, row_spec, row_spec, k_spec, v_spec, k_spec, v_spec],
            out_specs=[row_spec, k_spec, k_spec, k_spec, k_spec],
        ),
        out_shape=[jax.ShapeDtypeStruct((row_count, width), jnp.bfloat16)] + [key_shape] * 4,
        compiler_params=pltpu.CompilerParams(vmem_limit_bytes=VMEM_LIMIT),
        cost_estimate=pl.CostEstimate(
            flops=20 * row_count * keys * width,
            bytes_accessed=8 * (row_count + 4 * keys) * width,
            transcendentals=2 * row_count * keys * num_heads,
        ),
    )(kept, queries, grads, log_totals, kv_near, kv_near, kv_far, kv_far)


def padded_rows(block, before, after):
    return jnp.pad(block, ((before, after), (0, 0)))


def scaled_back(stream, gain_vec, grad_out):
    discarded_value, backward_fn = jax.vjp(scaled, stream, gain_vec)
    return backward_fn(grad_out)


def gelu_erf(raised):
    return 0.5 * raised * (1.0 + lax.erf(raised * 0.5**0.5))


def gelu_slope(raised):
    bell = jnp.exp(-0.5 * raised * raised) * (2.0 * math.pi) ** (-0.5)
    return 0.5 * (1.0 + lax.erf(raised * 0.5**0.5)) + raised * bell


def feed_fwd(stream, gain_vec, w_up, w_down):
    normal_in = scaled(stream, gain_vec).astype(jnp.bfloat16)
    raised = matmul(normal_in, w_up)
    hidden = gelu_erf(raised).astype(jnp.bfloat16)
    return (stream + matmul(hidden, w_down), (normal_in, raised, hidden))


def feed_back(stream, gain_vec, w_up, w_down, stored, grad_out):
    normal_in, raised, hidden = stored
    branch_grad = grad_out.astype(jnp.bfloat16)
    grad_hidden = outer_rows(branch_grad, w_down).astype(jnp.bfloat16).astype(jnp.float32)
    grad_raised = (grad_hidden * gelu_slope(raised)).astype(jnp.bfloat16)
    grad_wup = inner_rows(normal_in, grad_raised)
    grad_normal = outer_rows(grad_raised, w_up).astype(jnp.bfloat16).astype(jnp.float32)
    grad_stream, grad_gain = scaled_back(stream, gain_vec, grad_normal)
    return (grad_out + grad_stream, grad_wup, branch_grad, grad_gain)


def swapped(block):
    devices = range(lax.axis_size("dp"))
    return lax.ppermute(block, "dp", [(i, i ^ 1) for i in devices])


def attend_fwd(stream, gain_vec, w_in, w_out, num_heads, kept, skip, block_rows):
    width = stream.shape[1]
    normal_in = scaled(stream, gain_vec).astype(jnp.bfloat16)
    kv_near = matmul(normal_in, w_in[:, width:]).astype(jnp.bfloat16)
    kv_far = swapped(kv_near)
    queries = matmul(normal_in[skip:], w_in[:, :width]).astype(jnp.bfloat16)
    merged, log_totals = attend_rows(queries, kv_near, kv_far, kept, num_heads, block_rows)
    outcome = stream[skip:] + matmul(merged, w_out)
    return (outcome, (normal_in, queries, kv_near, kv_far, merged, log_totals))


def attend_back(stream, gain_vec, w_in, w_out, num_heads, kept, skip, block_rows, stored, grad_out):
    normal_in, queries, kv_near, kv_far, merged, log_totals = stored
    branch_grad = grad_out.astype(jnp.bfloat16)
    grad_wout = inner_rows(merged, branch_grad)
    grad_merged = outer_rows(branch_grad, w_out).astype(jnp.bfloat16)
    dq, dk_near, dv_near, dk_far, dv_far = attend_rows_back(
        queries, grad_merged, log_totals, kv_near, kv_far, kept, num_heads, block_rows
    )
    dk = (dk_near + swapped(dk_far)).astype(jnp.bfloat16)
    dv = (dv_near + swapped(dv_far)).astype(jnp.bfloat16)
    grad_packed = jnp.concatenate([padded_rows(dq, skip, 0), dk, dv], axis=1)
    grad_win = inner_rows(normal_in, grad_packed)
    grad_normal = outer_rows(grad_packed, w_in).astype(jnp.bfloat16).astype(jnp.float32)
    grad_stream, grad_gain = scaled_back(stream, gain_vec, grad_normal)
    return (padded_rows(grad_out, skip, 0) + grad_stream, grad_win, grad_wout, grad_gain)


def tall_grad_kernel(first_blocks, x_ref, gx_ref, h_ref, gh_ref, out_ref):
    @pl.when(pl.program_id(0) < first_blocks)
    def _():
        out_ref[...] = inner_rows(x_ref[...], gx_ref[...]).astype(out_ref.dtype)

    @pl.when(pl.program_id(0) >= first_blocks)
    def _():
        out_ref[...] = inner_rows(h_ref[...], gh_ref[...]).astype(out_ref.dtype)


def tall_grad(chosen, grad_stream, hidden, branch_grad):
    rows, width = grad_stream.shape
    block = 512
    first_blocks, blocks = PATCH // block, (PATCH + FF) // block
    return pl.pallas_call(
        functools.partial(tall_grad_kernel, first_blocks),
        grid=(blocks,),
        in_specs=[
            pl.BlockSpec((rows, block), lambda i: (0, jnp.minimum(i, first_blocks - 1))),
            pl.BlockSpec((rows, width), lambda i: (0, 0)),
            pl.BlockSpec((rows, block), lambda i: (0, jnp.maximum(i - first_blocks, 0))),
            pl.BlockSpec((rows, width), lambda i: (0, 0)),
        ],
        out_specs=pl.BlockSpec((block, width), lambda i: (i, 0)),
        out_shape=jax.ShapeDtypeStruct((PATCH + FF, width), jnp.bfloat16),
        compiler_params=pltpu.CompilerParams(vmem_limit_bytes=VMEM_LIMIT),
        cost_estimate=pl.CostEstimate(
            flops=2 * rows * width * (PATCH + FF),
            bytes_accessed=2 * (PATCH + FF) * (rows + width),
            transcendentals=0,
        ),
    )(chosen, grad_stream, hidden, branch_grad)


MESH = pl.DeviceIdType.MESH


def normed_rows(source, target, rows, gain_row, chunk, twice=False):
    def step(i, carried_through):
        at = pl.ds(pl.multiple_of(i * chunk, 16), chunk)
        values = normed(source[at, :]) * gain_row
        if twice:
            values = normed(values)
        target[at, :] = values.astype(target.dtype)
        return carried_through

    lax.fori_loop(0, rows // chunk, step, 0)


def gather_kernel(count, zn, *refs):
    ins, refs = refs[:count], refs[count:]
    pixels_ref, here_ref, there_ref, order_ref, high_ref, low_ref, *refs = refs
    outs, refs = refs[:count], refs[count:]
    goal_ref, picked_ref, table_ref, *refs = refs
    stages, refs = refs[:count], refs[count:]
    facts_ref, t0_ref, a_ref, near_ref, far_ref, q_ref, o_ref, h_ref, sum_ref, embed_buf, qkv_buf, up_buf, down_buf, *refs = refs
    pixel_buf, other_ref, chosen_ref, *refs = refs
    local_sem, z_send, z_recv, p_send, p_recv, w_sem, kv_sem = refs
    section, place = lax.axis_index("section"), lax.axis_index("dp")
    z, core = place // 2, place % 2
    near = {"section": section + 1 - 2 * (section % 2)}
    far = {"section": (section + 2) % 4}
    mate = {"dp": place + 1 - 2 * core}
    ahead = {"dp": place + 2}
    behind = {"dp": place - 2}

    barrier = pltpu.get_barrier_semaphore()
    line = [{"dp": (z + j) % zn * 2 + core} for j in range(1, zn)]
    for other in [near, far, mate] + line:
        pl.semaphore_signal(barrier, inc=1, device_id=other, device_id_type=MESH)
    pl.semaphore_wait(barrier, 3 + len(line))

    def block(ref, a, owner_z, quarter=None, rows=None, owner_core=core):
        size = ins[a].shape[0]
        start, length = (0, size) if rows is None else rows
        offset = pl.multiple_of((owner_z * 2 + owner_core) * size + start, 16)
        if quarter is None:
            return ref.at[pl.ds(offset, length), :]
        width = ins[a].shape[1] // 4
        return ref.at[pl.ds(offset, length), pl.ds(pl.multiple_of(quarter * width, 128), width)]

    def own_quarter(a):
        width = ins[a].shape[1] // 4
        return ins[a].at[:, pl.ds(pl.multiple_of(section * width, 128), width)]

    def copy(src, dst, sends, recvs, index, device):
        return pltpu.make_async_remote_copy(
            src_ref=src,
            dst_ref=dst,
            send_sem=sends.at[index],
            recv_sem=recvs.at[index],
            device_id=device,
            device_id_type=MESH,
        )

    def along(a, step, upward):
        device = ahead if upward else behind
        source_z = z - (step - 1) if upward else z + (step - 1)
        src = own_quarter(a) if step == 1 else block(outs[a], a, source_z, section)
        index = (a * (zn - 1) + step - 1) * 2 + (0 if upward else 1)
        return copy(src, block(outs[a], a, source_z, section), z_send, z_recv, index, device)

    def sends_along(step, upward):
        if upward:
            return (z - (step - 1) >= 0) & (z < zn - 1)
        return (z + (step - 1) <= zn - 1) & (z > 0)

    def first_half(a):
        size = ins[a].shape[0]
        return (0, (size + 31) // 32 * 16)

    def second_half(a):
        size = ins[a].shape[0]
        start = (size + 31) // 32 * 16
        return (start, size - start)

    def in_plane(a, step, upward, kind):
        owner_z = z - step if upward else z + step
        index = ((a * (zn - 1) + step - 1) * 2 + (0 if upward else 1)) * 5 + kind
        x_quarter, y_quarter = near["section"], far["section"]
        part = [
            lambda: block(outs[a], a, owner_z, section),
            lambda: block(outs[a], a, owner_z, section),
            lambda: block(outs[a], a, owner_z, x_quarter, first_half(a)),
            lambda: block(outs[a], a, owner_z, y_quarter, second_half(a)),
            lambda: block(outs[a], a, owner_z),
        ][kind]()
        return copy(part, part, p_send, p_recv, index, (near, far, far, near, mate)[kind])

    own = []
    def offered(a):
        for upward in (True, False):

            @pl.when(sends_along(1, upward))
            def _(upward=upward):
                along(a, 1, upward).start()

    for a in range(2):
        offered(a)

    settled = []
    for a in range(count):
        take = pltpu.make_async_copy(ins[a], stages[a], local_sem.at[a])
        take.start()
        base = count * (zn - 1) * 10
        give = copy(ins[a], block(outs[a], a, z), p_send, p_recv, base + a, mate)
        give.start()
        keep = pltpu.make_async_copy(stages[a], block(outs[a], a, z), local_sem.at[a])
        own.append((take, keep, give))

    for take, keep, give in own:
        take.wait()
        keep.start()

    items = [
        (a, step, upward)
        for a in range(count)
        for step in range(1, zn)
        for upward in (True, False)
    ]

    def arrives(step, upward):
        return z - step >= 0 if upward else z + step <= zn - 1

    def received(a, step, upward):
        @pl.when(arrives(step, upward))
        def _():
            along(a, step, upward).wait_recv()
            in_plane(a, step, upward, 0).start()
            in_plane(a, step, upward, 1).start()

        if step < zn - 1:

            @pl.when(arrives(step, upward) & sends_along(step + 1, upward))
            def _():
                along(a, step + 1, upward).start()

    def passed_on(a, step, upward):
        @pl.when(arrives(step, upward))
        def _():
            in_plane(a, step, upward, 0).wait_recv()
            in_plane(a, step, upward, 2).start()
            in_plane(a, step, upward, 1).wait_recv()
            in_plane(a, step, upward, 3).start()

    def completed(a, step, upward):
        @pl.when(arrives(step, upward))
        def _():
            in_plane(a, step, upward, 2).wait_recv()
            in_plane(a, step, upward, 3).wait_recv()
            in_plane(a, step, upward, 4).start()

    lag = 3
    group = 2 * (zn - 1)

    def advance(i):
        if i % group == 0 and 2 <= i // group + 1 < count:
            offered(i // group + 1)
        if 0 <= i - 2 * lag < len(items):
            completed(*items[i - 2 * lag])
        if 0 <= i - lag < len(items):
            passed_on(*items[i - lag])
        if i < len(items):
            received(*items[i])

    def settle(a):
        take, keep, give = own[a]
        keep.wait()
        give.wait_recv()
        for b, step, upward in items:
            if b == a:

                @pl.when(arrives(step, upward))
                def _(step=step, upward=upward):
                    in_plane(a, step, upward, 4).wait_recv()

        settled.append(a)

    def run_loop(length, body, steps):
        def step(i, carried_through):
            body(i)
            for at, move in enumerate(steps):
                pl.when(i == at * length // len(steps))(functools.partial(advance, move))
            return carried_through

        lax.fori_loop(0, length, step, 0)

    def streamed(length, fetches, body, steps):
        for fetch in fetches:
            fetch(0).start()

        def with_blocks(i):
            @pl.when(i + 1 < length)
            def _():
                for fetch in fetches:
                    fetch(i + 1).start()

            for fetch in fetches:
                fetch(i).wait()
            body(i, i % 2)

        run_loop(length, with_blocks, steps)

    def column_fetch(a, rows, first, width, buffer, sem):
        def fetch(i):
            columns = pl.ds(pl.multiple_of(first + i * width, 128), width)
            return pltpu.make_async_copy(
                outs[a].at[rows, columns], buffer.at[i % 2], w_sem.at[sem * 2 + i % 2]
            )

        return fetch

    ends = [group * (a + 1) + 2 * lag for a in range(count)]
    last = len(items) + 2 * lag
    SMALL, TALL, WIDE = 0, 1, 2
    clips_here = pixels_ref.shape[0]
    holds = core == section // clips_here
    first = list(range(min(ends[TALL], last)))
    pixel_copy = pltpu.make_async_copy(pixels_ref.at[section % clips_here], pixel_buf, kv_sem.at[2])
    handed = pltpu.make_async_remote_copy(
        src_ref=other_ref,
        dst_ref=chosen_ref,
        send_sem=kv_sem.at[3],
        recv_sem=kv_sem.at[4],
        device_id=mate,
        device_id_type=MESH,
    )

    @pl.when(holds)
    def _():
        pixel_copy.start()

    def tabulate(i):
        rows = pl.ds(pl.multiple_of(i * 96, 16), 96)
        order = order_ref[rows, :]

        def wave(table, index):
            choice = lax.broadcasted_iota(jnp.int32, (96, table.shape[0]), 1) == index
            return jnp.dot(
                choice.astype(jnp.float32), table[...],
                precision=lax.Precision.HIGHEST, preferred_element_type=jnp.float32,
            )

        high, low = wave(high_ref, order // 32), wave(low_ref, order % 32)
        sin_high, cos_high = high[:, : D // 2], high[:, D // 2 :]
        sin_low, cos_low = low[:, : D // 2], low[:, D // 2 :]
        t0_ref[rows, : D // 2] = sin_high * cos_low + cos_high * sin_low
        t0_ref[rows, D // 2 :] = cos_high * cos_low - sin_high * sin_low

    run_loop(HALF // 96, tabulate, first[:2])
    table_ref[...] = t0_ref[:SEEN, :]

    @pl.when(holds)
    def _():
        pixel_copy.wait()

    def pick(source, target):
        def rows_picked(i):
            @pl.when(holds)
            def _():
                rows = pl.ds(pl.multiple_of(i * 96, 16), 96)
                choice = lax.broadcasted_iota(jnp.int32, (96, L), 1) == source[rows, :]
                target[rows, :] = matmul(choice.astype(jnp.bfloat16), pixel_buf[...]).astype(jnp.bfloat16)

        return rows_picked

    run_loop(HALF // 96, pick(there_ref, other_ref), first[2:5])

    @pl.when(holds)
    def _():
        handed.start()

    run_loop(HALF // 96, pick(here_ref, chosen_ref), first[5:8])
    for i in first[8:]:
        advance(i)

    @pl.when(holds)
    def _():
        handed.wait_send()

    @pl.when(jnp.logical_not(holds))
    def _():
        handed.wait_recv()

    picked_ref[...] = chosen_ref[:SEEN, :]
    settle(SMALL)
    settle(TALL)
    facts = pltpu.make_async_copy(outs[SMALL].at[:, PD : PD + LANES], facts_ref, local_sem.at[SMALL])
    facts.start()

    def embed(i, slot):
        at = pl.ds(pl.multiple_of(i * 256, 128), 256)
        t0_ref[:, at] += matmul(chosen_ref[...], embed_buf[slot])

    waiting = list(range(ends[TALL], min(ends[WIDE], last)))
    streamed(4, [column_fetch(TALL, pl.ds(0, PATCH), 0, 256, embed_buf, 0)], embed, waiting[:2])
    facts.wait()
    gain_rows = jnp.transpose(facts_ref[...].astype(jnp.float32))
    normed_rows(t0_ref, a_ref, HALF, gain_rows[3:4, :], 96)
    for i in waiting[2:]:
        advance(i)
    settle(WIDE)

    rest = list(range(ends[WIDE], last))
    cuts = [len(rest) * part // 80 for part in (0, 8, 12, 48, 54, 80)]
    rest = [rest[cuts[i] : cuts[i + 1]] for i in range(5)]
    whole_rows = pl.ds(0, D)

    def keys_values(i, slot):
        at = pl.ds(pl.multiple_of(i * 256, 128), 256)
        near_ref[:, at] = matmul(a_ref[...], qkv_buf[slot]).astype(jnp.bfloat16)

    def queries(i, slot):
        at = pl.ds(pl.multiple_of(i * 256, 128), 256)
        q_ref[:, at] = matmul(a_ref[SKIP:, :], qkv_buf[slot]).astype(jnp.bfloat16)

    streamed(8, [column_fetch(WIDE, whole_rows, D, 256, qkv_buf, 1)], keys_values, rest[0])
    share = pltpu.make_async_remote_copy(
        src_ref=near_ref,
        dst_ref=far_ref,
        send_sem=kv_sem.at[0],
        recv_sem=kv_sem.at[1],
        device_id=mate,
        device_id_type=MESH,
    )
    share.start()
    streamed(4, [column_fetch(WIDE, whole_rows, 0, 256, qkv_buf, 1)], queries, rest[1])
    share.wait()
    block_rows = (HALF - SKIP) // 2

    def attention(i):
        lanes = pl.ds(pl.multiple_of(i // 2 * LANES, LANES), LANES)
        values = pl.ds(pl.multiple_of(D + i // 2 * LANES, LANES), LANES)
        rows = pl.ds(pl.multiple_of(i % 2 * block_rows, 16), block_rows)
        attend_kernel(
            D // HE, False, None, q_ref.at[rows, lanes], near_ref.at[:, lanes],
            near_ref.at[:, values], far_ref.at[:, lanes], far_ref.at[:, values],
            o_ref.at[rows, lanes], None,
        )

    run_loop(2 * D // LANES, attention, rest[2])

    def merge(i, slot):
        at = pl.ds(pl.multiple_of(i * 256, 128), 256)
        stream = t0_ref[SKIP:, at] + matmul(o_ref[...], qkv_buf[slot])
        sum_ref[:, at] = stream.astype(jnp.bfloat16).astype(jnp.float32)

    streamed(4, [column_fetch(WIDE, whole_rows, 3 * D, 256, qkv_buf, 1)], merge, rest[3])

    row_count = HALF - SKIP
    normed_rows(sum_ref, a_ref, row_count, gain_rows[4:5, :], 96)

    def down_fetch(i):
        rows = pl.ds(pl.multiple_of(PATCH + i * 512, 16), 512)
        return pltpu.make_async_copy(outs[TALL].at[rows, :], down_buf.at[i % 2], w_sem.at[6 + i % 2])

    def feed(i, slot):
        for part in range(2):
            rows = pl.ds(part * block_rows, block_rows)
            h_ref[...] = gelu_erf(matmul(a_ref[rows, :], up_buf[slot])).astype(jnp.bfloat16)
            sum_ref[rows, :] += matmul(h_ref[...], down_buf[slot])

    streamed(
        8,
        [column_fetch(WIDE, whole_rows, 4 * D, 512, up_buf, 2), down_fetch],
        feed,
        rest[4],
    )
    normed_rows(sum_ref, goal_ref, row_count, gain_rows[5:6, :], 96, twice=True)

    for a in range(count):
        if a not in settled:
            settle(a)
    for take, keep, give in own:
        give.wait_send()
    for a, step, upward in items:

        @pl.when(sends_along(step, upward))
        def _(a=a, step=step, upward=upward):
            along(a, step, upward).wait_send()

        @pl.when(arrives(step, upward))
        def _(a=a, step=step, upward=upward):
            for kind in range(5):
                in_plane(a, step, upward, kind).wait_send()


def gather_and_teach(blocks, pixels, order_here, order_there, order):
    count = len(blocks)
    dp_size = lax.axis_size("dp")
    zn = dp_size // 2
    return pl.pallas_call(
        functools.partial(gather_kernel, count, zn),
        in_specs=[pl.BlockSpec(memory_space=pl.ANY)] * count
        + [pl.BlockSpec(memory_space=pl.ANY)]
        + [pl.BlockSpec(memory_space=pltpu.VMEM)] * 5,
        out_specs=[pl.BlockSpec(memory_space=pl.ANY)] * count
        + [pl.BlockSpec(memory_space=pltpu.VMEM)] * 3,
        out_shape=[
            jax.ShapeDtypeStruct((member.shape[0] * dp_size, member.shape[1]), member.dtype)
            for member in blocks
        ]
        + [
            jax.ShapeDtypeStruct((HALF - SKIP, D), jnp.bfloat16),
            jax.ShapeDtypeStruct((SEEN, PATCH), jnp.bfloat16),
            jax.ShapeDtypeStruct((SEEN, D), jnp.float32),
        ],
        scratch_shapes=[pltpu.VMEM(member.shape, member.dtype) for member in blocks]
        + [
            pltpu.VMEM((D, LANES), jnp.bfloat16),
            pltpu.VMEM((HALF, D), jnp.float32),
            pltpu.VMEM((HALF, D), jnp.bfloat16),
            pltpu.VMEM((HALF, 2 * D), jnp.bfloat16),
            pltpu.VMEM((HALF, 2 * D), jnp.bfloat16),
            pltpu.VMEM((HALF - SKIP, D), jnp.bfloat16),
            pltpu.VMEM((HALF - SKIP, D), jnp.bfloat16),
            pltpu.VMEM(((HALF - SKIP) // 2, 512), jnp.bfloat16),
            pltpu.VMEM((HALF - SKIP, D), jnp.float32),
            pltpu.VMEM((2, PATCH, 256), jnp.bfloat16),
            pltpu.VMEM((2, D, 256), jnp.bfloat16),
            pltpu.VMEM((2, D, 512), jnp.bfloat16),
            pltpu.VMEM((2, 512, D), jnp.bfloat16),
            pltpu.VMEM((L, PATCH), jnp.bfloat16),
            pltpu.VMEM((HALF, PATCH), jnp.bfloat16),
            pltpu.VMEM((HALF, PATCH), jnp.bfloat16),
        ]
        + [
            pltpu.SemaphoreType.DMA((count,)),
            pltpu.SemaphoreType.DMA((count * (zn - 1) * 2,)),
            pltpu.SemaphoreType.DMA((count * (zn - 1) * 2,)),
            pltpu.SemaphoreType.DMA((count * ((zn - 1) * 10 + 1),)),
            pltpu.SemaphoreType.DMA((count * ((zn - 1) * 10 + 1),)),
            pltpu.SemaphoreType.DMA((8,)),
            pltpu.SemaphoreType.DMA((5,)),
        ],
        compiler_params=pltpu.CompilerParams(
            collective_id=0, has_side_effects=True, vmem_limit_bytes=58 * 1024 * 1024
        ),
    )(
        *blocks,
        pixels,
        order_here[:, None],
        order_there[:, None],
        order[:, None],
        position_table(32 * lax.iota(jnp.int32, L // 32), D),
        position_table(lax.iota(jnp.int32, 32), D),
    )


def upper_rows(size):
    return (size + 31) // 32 * 16


def add_blocks(rows, targets):
    def step(i, carried_through):
        at = pl.ds(pl.multiple_of(i * 16, 16), 16)
        for out, terms in targets:
            out[at, :] = sum(term[at, :].astype(jnp.float32) for term in terms).astype(out.dtype)
        return carried_through

    lax.fori_loop(0, rows // 16, step, 0)


def reduce_kernel(count, zn, *refs):
    ins, refs = refs[: count + 1], refs[count + 1 :]
    outs, refs = refs[: count + 1], refs[count + 1 :]
    whole, refs = refs[:count], refs[count:]
    near_one, refs = refs[:count], refs[count:]
    far_one, refs = refs[:count], refs[count:]
    far_two, refs = refs[:count], refs[count:]
    near_two, refs = refs[:count], refs[count:]
    along, refs = refs[:count], refs[count:]
    loaded, refs = refs[:count], refs[count:]
    held, refs = refs[:count], refs[count:]
    done, refs = refs[:count], refs[count:]
    total_ref, side_ref, line_ref, load_sem, move_send, move_recv, side_send, side_recv, line_send, line_recv = refs
    tally, out_total = ins[count], outs[count]
    tally_rows = out_total.shape[0]

    section, place = lax.axis_index("section"), lax.axis_index("dp")
    z, core = place // 2, place % 2
    x_quarter = section + 1 - 2 * (section % 2)
    y_quarter = (section + 2) % 4
    xy_quarter = (x_quarter + 2) % 4
    near, far = {"section": x_quarter}, {"section": y_quarter}
    mate = {"dp": place + 1 - 2 * core}
    sizes = [out.shape[0] for out in outs[:count]]
    widths = [out.shape[1] // 4 for out in outs[:count]]

    barrier = pltpu.get_barrier_semaphore()
    line = [{"dp": (z + j) % zn * 2 + core} for j in range(1, zn)]
    for other in [near, far, mate] + line:
        pl.semaphore_signal(barrier, inc=1, device_id=other, device_id_type=MESH)
    pl.semaphore_wait(barrier, 3 + len(line))

    def rows_at(a, slot, start=0, length=None):
        return pl.ds(pl.multiple_of(slot * sizes[a] + start, 16), sizes[a] if length is None else length)

    def quarter_at(a, quarter):
        return pl.ds(pl.multiple_of(quarter * widths[a], 128), widths[a])

    def upper(a):
        return upper_rows(sizes[a])

    def lower(a):
        return sizes[a] - upper_rows(sizes[a])

    def sent(src, dst, kind, a, slot, device):
        index = (kind * count + a) * (zn + 1) + slot
        return pltpu.make_async_remote_copy(
            src_ref=src,
            dst_ref=dst,
            send_sem=move_send.at[index],
            recv_sem=move_recv.at[index],
            device_id=device,
            device_id_type=MESH,
        )

    def load(a, owner_z):
        source = pl.ds(pl.multiple_of((owner_z * 2 + core) * sizes[a], 16), sizes[a])
        return pltpu.make_async_copy(
            ins[a].at[source, :], loaded[a].at[rows_at(a, owner_z), :], load_sem.at[a * zn + owner_z]
        )

    def give(a, owner_z):
        source = pl.ds(pl.multiple_of((owner_z * 2 + 1 - core) * sizes[a], 16), sizes[a])
        return sent(ins[a].at[source, :], whole[a].at[rows_at(a, owner_z), :], 0, a, owner_z, mate)

    def first_near(a, owner_z, which):
        quarter = (x_quarter, xy_quarter)[which]
        return sent(
            whole[a].at[rows_at(a, owner_z, 0, upper(a)), quarter_at(a, quarter)],
            near_one[a].at[pl.ds(pl.multiple_of((owner_z * 2 + which) * upper(a), 16), upper(a)), :],
            1 + which, a, owner_z, near,
        )

    def first_far(a, owner_z, which):
        quarter = (y_quarter, xy_quarter)[which]
        return sent(
            whole[a].at[rows_at(a, owner_z, upper(a), lower(a)), quarter_at(a, quarter)],
            far_one[a].at[pl.ds(pl.multiple_of((owner_z * 2 + which) * lower(a), 16), lower(a)), :],
            3 + which, a, owner_z, far,
        )

    def second_far(a, owner_z):
        return sent(
            whole[a].at[rows_at(a, owner_z, 0, upper(a)), quarter_at(a, y_quarter)],
            far_two[a].at[pl.ds(pl.multiple_of(owner_z * upper(a), 16), upper(a)), :],
            5, a, owner_z, far,
        )

    def second_near(a, owner_z):
        return sent(
            whole[a].at[rows_at(a, owner_z, upper(a), lower(a)), quarter_at(a, x_quarter)],
            near_two[a].at[pl.ds(pl.multiple_of(owner_z * lower(a), 16), lower(a)), :],
            6, a, owner_z, near,
        )

    def onward(a, owner_z, upward, last):
        slot = zn if last and not upward else owner_z
        return sent(
            whole[a].at[rows_at(a, owner_z), quarter_at(a, section)],
            along[a].at[rows_at(a, slot), :],
            7, a, slot, {"dp": place + 2 if upward else place - 2},
        )

    def finished(a, kind):
        quarter = (section, section, x_quarter, y_quarter)[kind]
        columns = quarter_at(a, quarter)
        part = (
            pl.ds(0, sizes[a]), pl.ds(0, sizes[a]), pl.ds(0, upper(a)), pl.ds(upper(a), lower(a))
        )[kind]
        src = done[a] if kind < 2 else outs[a].at[part, columns]
        return sent(src, outs[a].at[part, columns], 8 + kind, a, 0, (near, far, far, near)[kind])

    def keep(a):
        return pltpu.make_async_copy(
            done[a], outs[a].at[:, quarter_at(a, section)], load_sem.at[a * zn]
        )

    legs = [(k, upward) for k in range(zn - 1, 0, -1) for upward in (True, False)] + [(0, True)]
    items = [(a, leg) for leg in range(len(legs)) for a in range(count)]

    def owner_of(leg):
        k, upward = legs[leg]
        return z + k if upward else z - k

    def is_live(leg):
        k, upward = legs[leg]
        return (z + k <= zn - 1) if upward else (z - k >= 0)

    def started(a, leg):
        @pl.when(is_live(leg))
        def _():
            give(a, owner_of(leg)).start()

    def load_started(a, leg):
        @pl.when(is_live(leg))
        def _():
            load(a, owner_of(leg)).start()

    def parts(a, owner_z, is_upper, quarter):
        size = (0, upper(a)) if is_upper else (upper(a), lower(a))
        at = (rows_at(a, owner_z, *size), quarter_at(a, quarter))
        return (whole[a].at[at], loaded[a].at[at])

    def pair_up(a, owner_z, is_upper, quarter):
        both = parts(a, owner_z, is_upper, quarter)
        add_blocks(upper(a) if is_upper else lower(a), [(both[0], both)])

    def paired(a, leg):
        @pl.when(is_live(leg))
        def _():
            owner_z = owner_of(leg)
            load(a, owner_z).wait()
            give(a, owner_z).wait_recv()
            for quarter in (xy_quarter, x_quarter):
                pair_up(a, owner_z, True, quarter)
            for quarter in (xy_quarter, y_quarter):
                pair_up(a, owner_z, False, quarter)
            for which in (1, 0):
                first_near(a, owner_z, which).start()
                first_far(a, owner_z, which).start()


    def from_near(a, owner_z, which):
        start = pl.multiple_of((owner_z * 2 + which) * upper(a), 16)
        return near_one[a].at[pl.ds(start, upper(a)), :]

    def from_far(a, owner_z, which):
        start = pl.multiple_of((owner_z * 2 + which) * lower(a), 16)
        return far_one[a].at[pl.ds(start, lower(a)), :]

    def halved(a, leg):
        @pl.when(is_live(leg))
        def _():
            owner_z = owner_of(leg)
            first_near(a, owner_z, 1).wait_recv()
            both = parts(a, owner_z, True, y_quarter)
            add_blocks(upper(a), [(both[0], both + (from_near(a, owner_z, 1),))])
            second_far(a, owner_z).start()
            first_far(a, owner_z, 1).wait_recv()
            both = parts(a, owner_z, False, x_quarter)
            add_blocks(lower(a), [(both[0], both + (from_far(a, owner_z, 1),))])
            second_near(a, owner_z).start()

    def quartered(a, leg):
        k, upward = legs[leg]

        @pl.when(is_live(leg))
        def _():
            owner_z = owner_of(leg)
            own = quarter_at(a, section)
            first_near(a, owner_z, 0).wait_recv()
            second_far(a, owner_z).wait_recv()
            start = pl.multiple_of(owner_z * upper(a), 16)
            terms = parts(a, owner_z, True, section) + (
                from_near(a, owner_z, 0), far_two[a].at[pl.ds(start, upper(a)), :]
            )
            add_blocks(upper(a), [(held[a].at[pl.ds(0, upper(a)), :], terms)])
            first_far(a, owner_z, 0).wait_recv()
            second_near(a, owner_z).wait_recv()
            start = pl.multiple_of(owner_z * lower(a), 16)
            terms = parts(a, owner_z, False, section) + (
                from_far(a, owner_z, 0), near_two[a].at[pl.ds(start, lower(a)), :]
            )
            add_blocks(lower(a), [(held[a].at[pl.ds(upper(a), lower(a)), :], terms)])
            target = held[a]

            def join(upward_from, slot):
                onward(a, owner_z, upward_from, slot is not owner_z or k == 0).wait_recv()
                add_blocks(sizes[a], [(target, (target, along[a].at[rows_at(a, slot), :]))])

            if k > 0:

                @pl.when(z > 0 if upward else z < zn - 1)
                def _():
                    join(upward, owner_z)

                add_blocks(sizes[a], [(whole[a].at[rows_at(a, owner_z), own], (target,))])
                onward(a, owner_z, upward, k == 1).start()
            else:

                @pl.when(z > 0)
                def _():
                    join(True, owner_z)

                @pl.when(z < zn - 1)
                def _():
                    join(False, zn)

                def settle(i, carried_through):
                    at = pl.ds(pl.multiple_of(i * 16, 16), 16)
                    values = target[at, :]
                    done[a][at, :] = values.astype(done[a].dtype)
                    squares = values * values
                    squares = squares[:8] + squares[8:]
                    carried = total_ref[0:8, :]
                    for column in range(0, widths[a], 128):
                        carried = carried + squares[:, column : column + 128]
                    total_ref[0:8, :] = carried
                    return carried_through

                lax.fori_loop(0, sizes[a] // 16, settle, 0)
                keep(a).start()
                finished(a, 0).start()
                finished(a, 1).start()

    total_ref[0:8, :] = jnp.zeros((8, 128), jnp.float32)
    tally_copy = pltpu.make_async_copy(tally, total_ref.at[8:, :], load_sem.at[count * zn])
    tally_copy.start()
    for a, leg in items:
        started(a, leg)
        load_started(a, leg)
    lag = 5
    for i in range(len(items) + 2 * lag):
        if i < len(items):
            paired(*items[i])
        if 0 <= i - lag < len(items):
            halved(*items[i - lag])
        if 0 <= i - 2 * lag < len(items):
            quartered(*items[i - 2 * lag])

    tally_copy.wait()

    def exchanged(stage, device):
        return pltpu.make_async_remote_copy(
            src_ref=total_ref,
            dst_ref=side_ref.at[pl.ds(stage * tally_rows, tally_rows), :],
            send_sem=side_send.at[stage],
            recv_sem=side_recv.at[stage],
            device_id=device,
            device_id_type=MESH,
        )

    for stage, device in enumerate((mate, near, far)):
        swap = exchanged(stage, device)
        swap.start()
        swap.wait()
        total_ref[...] += side_ref[stage * tally_rows : (stage + 1) * tally_rows, :]

    def told(from_z, to_z, j):
        index = from_z * zn + to_z
        return pltpu.make_async_remote_copy(
            src_ref=total_ref,
            dst_ref=line_ref.at[pl.ds(pl.multiple_of(from_z * tally_rows, 8), tally_rows), :],
            send_sem=line_send.at[index],
            recv_sem=line_recv.at[index],
            device_id={"dp": to_z * 2 + core},
            device_id_type=MESH,
        )

    for j in range(1, zn):
        told(z, (z + j) % zn, j).start()
    line_ref[pl.ds(pl.multiple_of(z * tally_rows, 8), tally_rows), :] = total_ref[...]
    for j in range(1, zn):
        told((z + j) % zn, z, j).wait_recv()
    grand = line_ref[0:tally_rows, :]
    for j in range(1, zn):
        grand = grand + line_ref[j * tally_rows : (j + 1) * tally_rows, :]
    for j in range(1, zn):
        told(z, (z + j) % zn, j).wait_send()
    total_ref[...] = grand
    show = pltpu.make_async_copy(total_ref, out_total, load_sem.at[count * zn])
    show.start()

    for a in range(count):
        finished(a, 0).wait_recv()
        finished(a, 2).start()
        finished(a, 1).wait_recv()
        finished(a, 3).start()
    for a in range(count):
        keep(a).wait()
        finished(a, 2).wait_recv()
        finished(a, 3).wait_recv()
        for kind in range(4):
            finished(a, kind).wait_send()
    for a, leg in items:
        k, upward = legs[leg]

        @pl.when(is_live(leg))
        def _(a=a, leg=leg, k=k, upward=upward):
            owner_z = owner_of(leg)
            give(a, owner_z).wait_send()
            for which in (0, 1):
                first_near(a, owner_z, which).wait_send()
                first_far(a, owner_z, which).wait_send()
            second_near(a, owner_z).wait_send()
            second_far(a, owner_z).wait_send()
            if k > 0:
                onward(a, owner_z, upward, k == 1).wait_send()

    show.wait()


def reduce_blocks(blocks, tally, result_types):
    count = len(blocks)
    dp_size = lax.axis_size("dp")
    zn = dp_size // 2
    tally_rows = 8 + tally.shape[0]
    shapes = [(member.shape[0] // dp_size, member.shape[1]) for member in blocks]
    vmem = lambda rows, columns, dtype=jnp.bfloat16: pltpu.VMEM((rows, columns), dtype)
    anywhere = pl.BlockSpec(memory_space=pl.ANY)
    moves = 12 * count * (zn + 1)
    return pl.pallas_call(
        functools.partial(reduce_kernel, count, zn),
        in_specs=[anywhere] * (count + 1),
        out_specs=[anywhere] * (count + 1),
        out_shape=[jax.ShapeDtypeStruct(shape, kind) for shape, kind in zip(shapes, result_types)]
        + [jax.ShapeDtypeStruct((tally_rows, 128), jnp.float32)],
        scratch_shapes=[vmem(zn * r, w) for r, w in shapes]
        + [vmem(zn * 2 * upper_rows(r), w // 4) for r, w in shapes]
        + [vmem(zn * 2 * (r - upper_rows(r)), w // 4) for r, w in shapes]
        + [vmem(zn * upper_rows(r), w // 4) for r, w in shapes]
        + [vmem(zn * (r - upper_rows(r)), w // 4) for r, w in shapes]
        + [vmem((zn + 1) * r, w // 4) for r, w in shapes]
        + [vmem(zn * r, w) for r, w in shapes]
        + [vmem(r, w // 4, jnp.float32) for r, w in shapes]
        + [vmem(r, w // 4, kind) for (r, w), kind in zip(shapes, result_types)]
        + [
            vmem(tally_rows, 128, jnp.float32),
            vmem(3 * tally_rows, 128, jnp.float32),
            vmem(zn * tally_rows, 128, jnp.float32),
            pltpu.SemaphoreType.DMA((count * zn + 1,)),
            pltpu.SemaphoreType.DMA((moves,)),
            pltpu.SemaphoreType.DMA((moves,)),
            pltpu.SemaphoreType.DMA((3,)),
            pltpu.SemaphoreType.DMA((3,)),
            pltpu.SemaphoreType.DMA((zn * zn,)),
            pltpu.SemaphoreType.DMA((zn * zn,)),
        ],
        compiler_params=pltpu.CompilerParams(
            collective_id=1, has_side_effects=True, vmem_limit_bytes=60 * 1024 * 1024
        ),
    )(*blocks, tally)


def adamw_step(weight, grad_now, first, second, decay, rate):
    first = BETA_ONE * first + (1.0 - BETA_ONE) * grad_now
    second = BETA_TWO * second + (1.0 - BETA_TWO) * grad_now * grad_now
    ratio = first / (1.0 - BETA_ONE**STEP) / (jnp.sqrt(second / (1.0 - BETA_TWO**STEP)) + EPSILON)
    return (weight - rate * (ratio + decay * weight), first, second)


def local(
    pixels,
    token_order,
    visible,
    wide_weight,
    tall_weight,
    pred_weight,
    pred_down,
    enc_gains,
    pred_gains,
    wide_first,
    tall_first,
    pred_first,
    pred_down_first,
    enc_gains_first,
    pred_gains_first,
    wide_second,
    tall_second,
    pred_second,
    pred_down_second,
    enc_gains_second,
    pred_gains_second,
    teacher_wide,
    teacher_tall,
    teacher_gains,
):
    masters = (wide_weight, tall_weight, pred_weight, pred_down, enc_gains, pred_gains)
    section_idx = lax.axis_index("section")
    section_count = lax.axis_size("section")
    core = lax.axis_index("dp") % 2
    clips_here = pixels.shape[0]
    assert section_count == 2 * clips_here

    owner = section_idx // clips_here
    clip = section_idx % clips_here
    holds = core == owner
    counts_own = lax.dynamic_index_in_dim(visible, clip, 0)
    order_own = lax.dynamic_index_in_dim(token_order, clip, 0, keepdims=False)
    clip_facts = jnp.concatenate([order_own, counts_own])
    clip_facts = jnp.where(holds, clip_facts, swapped(clip_facts))
    seen = clip_facts[L]
    order_pairs = clip_facts[:L].reshape(HALF, 2)
    order = jnp.where(core == 0, order_pairs[:, 0], order_pairs[:, 1])
    pairs_own = order_own.reshape(HALF, 2)
    order_here = jnp.where(core == 0, pairs_own[:, 0], pairs_own[:, 1])
    order_there = jnp.where(core == 0, pairs_own[:, 1], pairs_own[:, 0])
    seen_near = (seen - core + 1) // 2
    seen_far = (seen + core) // 2
    kept = jnp.stack([seen_near, seen_far])
    visible_high, visible_low = visible // LANES, visible % LANES
    dp_size = lax.axis_size("dp")
    row_count = wide_weight.shape[0]
    small = jnp.concatenate(
        [
            wide_weight[:, 4 * D + FF :],
            enc_gains,
            teacher_gains,
            jnp.pad(pred_gains, ((0, row_count - pred_gains.shape[0]), (0, 0))),
            jnp.zeros((row_count, LANES - 10 - 2 * clips_here), jnp.float32),
            jnp.broadcast_to(
                jnp.concatenate([visible_high, visible_low]).astype(jnp.float32)[None, :],
                (row_count, 2 * clips_here),
            ),
        ],
        axis=1,
    )
    pred_block = pred_weight.shape if pred_weight.shape[0] % 16 == 0 else (-1, D)
    pred_form = (PD, pred_weight.shape[1]) if pred_weight.shape[0] % 16 == 0 else (-1, D)
    blocks = (
        small,
        teacher_tall,
        teacher_wide,
        tall_weight,
        wide_weight[:, : 4 * D + FF],
        pred_weight.reshape(pred_block),
        jnp.pad(pred_down, ((0, 0), (0, LANES))),
    )
    w_small, teach_tall, teach_wide, w_tall, w_wide, w_pred, w_down, goal, enc_chosen, table = gather_and_teach(
        tuple(member.astype(jnp.bfloat16) for member in blocks),
        pixels,
        order_here,
        order_there,
        order,
    )
    goal = goal.astype(jnp.float32)
    w_pred = w_pred.reshape(PD, -1)
    w_down = w_down[:, :PD]
    pred_embed = w_small[:, :PD]
    enc_copy = w_small[:, PD : PD + 3]
    pred_copy = w_small[:, PD + 6 : PD + 10].reshape(dp_size, row_count, 4)
    pred_copy = pred_copy[:, : pred_gains.shape[0]].reshape(PD, 4)
    counts = w_small[::row_count, PD + LANES - 2 * clips_here :].astype(jnp.float32)
    counts = counts[:, :clips_here] * LANES + counts[:, clips_here:]
    target_total = jnp.sum(L - counts)
    enc_gain = enc_copy.astype(jnp.float32)
    pred_gain = pred_copy.astype(jnp.float32)
    enc_attn = (w_wide[:, : 3 * D], w_wide[:, 3 * D : 4 * D])
    enc_feed = (w_wide[:, 4 * D : 4 * D + FF], w_tall[PATCH:])
    pred_attn = (w_pred[:, : 3 * PD], w_pred[:, 3 * PD : 4 * PD])
    pred_feed = (w_pred[:, 4 * PD : 4 * PD + PF], w_down)
    pred_head = w_pred[:, 4 * PD + PF :]

    pred_table = position_table(order, PD)
    row_ids = lax.iota(jnp.int32, HALF)
    context = (row_ids < seen_near)[:, None]

    stream_a = matmul(enc_chosen, w_tall[:PATCH]) + table
    stream_b, stored_a = attend_fwd(
        stream_a, enc_gain[:, 0], enc_attn[0], enc_attn[1], HE, kept, 0, SEEN
    )
    stream_b = stream_b.astype(jnp.bfloat16).astype(jnp.float32)
    stream_c, stored_b = feed_fwd(stream_b, enc_gain[:, 1], enc_feed[0], enc_feed[1])
    encoded = scaled(stream_c, enc_gain[:, 2]).astype(jnp.bfloat16)

    projected = padded_rows(matmul(encoded, pred_embed), 0, HALF - SEEN)
    stream_d = jnp.where(context, projected, pred_gain[:, 3][None, :]) + pred_table
    stream_e, stored_d = attend_fwd(
        stream_d, pred_gain[:, 0], pred_attn[0], pred_attn[1], PH, None, SKIP, 336
    )
    stream_e = stream_e.astype(jnp.bfloat16).astype(jnp.float32)
    stream_f, stored_e = feed_fwd(stream_e, pred_gain[:, 1], pred_feed[0], pred_feed[1])
    final = scaled(stream_f, pred_gain[:, 2]).astype(jnp.bfloat16)
    residual = matmul(final, pred_head) - goal
    smooth_err = jnp.sqrt(residual * residual + 1.0)
    target_mask = jnp.logical_not(context[SKIP:])
    loss_part = jnp.sum(jnp.where(target_mask, smooth_err - 1.0, 0.0))
    grad_guess = (jnp.where(target_mask, residual / smooth_err, 0.0) / target_total).astype(
        jnp.bfloat16
    )

    grad_head = inner_rows(final, grad_guess)
    grad_final = outer_rows(grad_guess, pred_head).astype(jnp.bfloat16).astype(jnp.float32)
    grad_stream, grad_pg2 = scaled_back(stream_f, pred_gain[:, 2], grad_final)
    grad_stream, grad_pup, branch_grad, grad_pg1 = feed_back(
        stream_e, pred_gain[:, 1], pred_feed[0], pred_feed[1], stored_e, grad_stream
    )
    grad_down = inner_rows(stored_e[2], branch_grad)
    grad_stream = grad_stream.astype(jnp.bfloat16).astype(jnp.float32)
    grad_stream, grad_pin, grad_pout, grad_pg0 = attend_back(
        stream_d, pred_gain[:, 0], pred_attn[0], pred_attn[1], PH, None, SKIP, 336, stored_d, grad_stream
    )
    grad_token = jnp.sum(jnp.where(context, 0.0, grad_stream), axis=0)
    grad_projected = jnp.where(context, grad_stream, 0.0)[:SEEN].astype(jnp.bfloat16)
    grad_embed = inner_rows(encoded, grad_projected)
    grad_encoded = outer_rows(grad_projected, pred_embed).astype(jnp.bfloat16).astype(jnp.float32)
    grad_stream, grad_eg2 = scaled_back(stream_c, enc_gain[:, 2], grad_encoded)
    grad_stream, grad_eup, branch_grad, grad_eg1 = feed_back(
        stream_b, enc_gain[:, 1], enc_feed[0], enc_feed[1], stored_b, grad_stream
    )
    grad_stream = grad_stream.astype(jnp.bfloat16).astype(jnp.float32)
    grad_stream, grad_ein, grad_eout, grad_eg0 = attend_back(
        stream_a, enc_gain[:, 0], enc_attn[0], enc_attn[1], HE, kept, 0, SEEN, stored_a, grad_stream
    )
    grad_tall = tall_grad(
        enc_chosen, grad_stream.astype(jnp.bfloat16), stored_b[2], branch_grad
    )

    gain_grads = jnp.concatenate(
        [
            jnp.stack([grad_eg0, grad_eg1, grad_eg2], axis=1).reshape(-1, LANES),
            jnp.stack([grad_pg0, grad_pg1, grad_pg2, grad_token], axis=1).reshape(-1, LANES),
        ],
        axis=0,
    )
    gain_rows = 3 * D // LANES
    loss_tile = jnp.zeros((8, LANES), jnp.float32).at[0, 0].set(loss_part)
    tally = jnp.concatenate(
        [loss_tile, gain_grads, jnp.zeros((4, LANES), jnp.float32)], axis=0
    )
    blocks = shortened(
        (
            grad_ein,
            grad_eout,
            grad_eup,
            jnp.pad(grad_embed, ((0, 0), (0, LANES))),
            grad_tall,
            jnp.concatenate(shortened([grad_pin, grad_pout, grad_pup, grad_head]), axis=1).reshape(pred_form),
            jnp.pad(grad_down, ((0, 0), (0, LANES))),
        )
    )
    *summed, tally = reduce_blocks(
        blocks, tally, [jnp.bfloat16] * 5 + [jnp.float32] * 2
    )
    wide_parts = [summed[0], summed[1], summed[2], summed[3][:, :PD]]
    place = lax.axis_index("dp")
    gains_all = tally[16 : 16 + gain_rows].reshape(D, 3)
    pred_gains_all = tally[16 + gain_rows : 16 + gain_rows + 4 * PD // LANES].reshape(PD, 4)
    shares = (
        jnp.concatenate(wide_parts, axis=1).astype(jnp.float32),
        summed[4].astype(jnp.float32),
        summed[5].reshape(pred_weight.shape).astype(jnp.float32),
        summed[6][:, :PD].astype(jnp.float32),
        lax.dynamic_slice_in_dim(gains_all, place * enc_gains.shape[0], enc_gains.shape[0], 0),
        lax.dynamic_slice_in_dim(pred_gains_all, place * pred_gains.shape[0], pred_gains.shape[0], 0),
    )
    loss_sum = tally[8, 0]
    square_total = jnp.sum(tally[:8]) + jnp.sum(jnp.square(tally[16:]))
    grad_norm = jnp.sqrt(square_total)
    factor = jnp.minimum(1.0, CLIP_AT / (grad_norm + 1e-06))
    firsts = (
        wide_first,
        tall_first,
        pred_first,
        pred_down_first,
        enc_gains_first,
        pred_gains_first,
    )
    seconds = (
        wide_second,
        tall_second,
        pred_second,
        pred_down_second,
        enc_gains_second,
        pred_gains_second,
    )
    decays = (DECAY, DECAY, DECAY, DECAY, 0.0, 0.0)
    rates = (RATE, RATE, RATE, RATE, GAIN_RATE, GAIN_RATE)
    results = [
        adamw_step(
            masters[group_idx],
            shares[group_idx] * factor,
            firsts[group_idx],
            seconds[group_idx],
            decays[group_idx],
            rates[group_idx],
        )
        for group_idx in range(6)
    ]
    news = [entry[0] for entry in results]
    teacher_wide_new = KEEP_RATE * teacher_wide + (1.0 - KEEP_RATE) * news[0][:, : 4 * D + FF]
    teacher_tall_new = KEEP_RATE * teacher_tall + (1.0 - KEEP_RATE) * news[1]
    teacher_gains_new = KEEP_RATE * teacher_gains + (1.0 - KEEP_RATE) * news[4]
    return (
        loss_sum,
        target_total,
        grad_norm,
        news[0],
        news[1],
        news[2],
        news[3],
        news[4],
        news[5],
        results[0][1],
        results[1][1],
        results[2][1],
        results[3][1],
        results[4][1],
        results[5][1],
        results[0][2],
        results[1][2],
        results[2][2],
        results[3][2],
        results[4][2],
        results[5][2],
        news[0].astype(jnp.bfloat16),
        news[1].astype(jnp.bfloat16),
        news[2].astype(jnp.bfloat16),
        news[3].astype(jnp.bfloat16),
        news[4].astype(jnp.bfloat16),
        news[5].astype(jnp.bfloat16),
        teacher_wide_new,
        teacher_tall_new,
        teacher_gains_new,
    )


def solution(mesh):
    return jax.shard_map(
        local,
        mesh=mesh,
        in_specs=(
            P("dp", None, None),
            P("dp", None),
            P("dp"),
            P("dp", None),
            P("dp", None),
            P("dp", None),
            P("dp", None),
            P("dp", None),
            P("dp", None),
            P("dp", None),
            P("dp", None),
            P("dp", None),
            P("dp", None),
            P("dp", None),
            P("dp", None),
            P("dp", None),
            P("dp", None),
            P("dp", None),
            P("dp", None),
            P("dp", None),
            P("dp", None),
            P("dp", None),
            P("dp", None),
            P("dp", None),
        ),
        out_specs=(
            P(),
            P(),
            P(),
            P("dp", None),
            P("dp", None),
            P("dp", None),
            P("dp", None),
            P("dp", None),
            P("dp", None),
            P("dp", None),
            P("dp", None),
            P("dp", None),
            P("dp", None),
            P("dp", None),
            P("dp", None),
            P("dp", None),
            P("dp", None),
            P("dp", None),
            P("dp", None),
            P("dp", None),
            P("dp", None),
            P("dp", None),
            P("dp", None),
            P("dp", None),
            P("dp", None),
            P("dp", None),
            P("dp", None),
            P("dp", None),
            P("dp", None),
            P("dp", None),
        ),
        check_vma=False,
    )
```

```python
import functools
import math

import jax
import jax.numpy as jnp
from jax import lax
from jax.experimental import pallas as pl
from jax.experimental.pallas import tpu as pltpu
from jax.sharding import PartitionSpec as P

D = 1024
HE = 16
FF = 4096
PD = 384
PH = 12
PF = 1536
PATCH = 1536
L = 1536
STEP = 10
VIS = 576
VIS_LO = 192
HALF = L // 2
SEEN = VIS // 2
SKIP = VIS_LO // 2
LANES = 128
VMEM_LIMIT = 50 * 1024 * 1024


BETA_ONE = 0.9
BETA_TWO = 0.999
EPSILON = 1e-08
RATE = 0.02
GAIN_RATE = 0.5
DECAY = 0.05
CLIP_AT = 0.05
KEEP_RATE = 0.8
NEGATIVE = -1e30


def shortened(x):
    return jax.tree.map(lambda a: a.astype(jnp.bfloat16) if a.dtype == jnp.float32 else a, x)


def normed(stream):
    centred = stream - jnp.mean(stream, axis=-1, keepdims=True)
    return centred * lax.rsqrt(jnp.mean(centred * centred, axis=-1, keepdims=True) + 1e-06)


def scaled(stream, gain_vec):
    return normed(stream) * gain_vec


def position_table(positions, feature_width):
    frequency = jnp.exp(
        jnp.arange(feature_width // 2, dtype=jnp.float32)
        * (-2.0 * math.log(10000.0) / feature_width)
    )
    angles = positions.astype(jnp.float32)[:, None] * frequency[None, :]
    return jnp.concatenate([jnp.sin(angles), jnp.cos(angles)], axis=1)


def matmul(left, right):
    return jnp.dot(left, right, preferred_element_type=jnp.float32)


def inner_rows(left, right):
    return lax.dot_general(
        left, right, (((0,), (0,)), ((), ())), preferred_element_type=jnp.float32
    )


def outer_rows(left, right):
    return lax.dot_general(
        left, right, (((1,), (1,)), ((), ())), preferred_element_type=jnp.float32
    )


def head_scores(queries, key_heads, kept):
    logits = outer_rows(queries, key_heads)
    if kept is None:
        return logits
    key_ids = lax.broadcasted_iota(jnp.int32, logits.shape, 1)
    return jnp.where(key_ids < kept, logits, NEGATIVE)


def attend_kernel(head_size, masked, kept_ref, q_ref, k0_ref, v0_ref, k1_ref, v1_ref, o_ref, l_ref):
    exponent = head_size ** (-0.5) * math.log2(math.e)
    lane_head = lax.broadcasted_iota(jnp.int32, (1, LANES), 1) // head_size
    kept = (kept_ref[0], kept_ref[1]) if masked else (None, None)
    queries = q_ref[...]
    merged = jnp.zeros(o_ref.shape, jnp.float32)
    log_totals = jnp.zeros(o_ref.shape, jnp.float32)
    for head in range(LANES // head_size):
        chosen = lane_head == head
        head_queries = jnp.where(chosen, queries, jnp.zeros_like(queries))
        near = head_scores(head_queries, k0_ref[...], kept[0])
        far = head_scores(head_queries, k1_ref[...], kept[1])
        row_max = exponent * jnp.maximum(
            jnp.max(near, axis=1, keepdims=True), jnp.max(far, axis=1, keepdims=True)
        )
        near = jnp.exp2(near * exponent - row_max)
        far = jnp.exp2(far * exponent - row_max)
        row_total = jnp.sum(near, axis=1, keepdims=True) + jnp.sum(far, axis=1, keepdims=True)
        outcome = matmul(near.astype(jnp.bfloat16), v0_ref[...]) + matmul(
            far.astype(jnp.bfloat16), v1_ref[...]
        )
        merged = jnp.where(chosen, outcome / row_total, merged)
        log_totals = jnp.where(chosen, row_max + jnp.log2(row_total), log_totals)
    o_ref[...] = merged.astype(o_ref.dtype)
    if l_ref is not None:
        l_ref[...] = log_totals


def attend_rows(queries, kv_near, kv_far, kept, num_heads, block_rows):
    row_count, width = queries.shape
    keys = kv_near.shape[0]
    groups = width // LANES
    masked = kept is not None
    if not masked:
        kept = jnp.zeros((2,), jnp.int32)
    row_spec = pl.BlockSpec((block_rows, LANES), lambda g, b, kept: (b, g))
    k_spec = pl.BlockSpec((keys, LANES), lambda g, b, kept: (0, g))
    v_spec = pl.BlockSpec((keys, LANES), lambda g, b, kept: (0, g + groups))
    return pl.pallas_call(
        functools.partial(attend_kernel, width // num_heads, masked),
        grid_spec=pltpu.PrefetchScalarGridSpec(
            num_scalar_prefetch=1,
            grid=(groups, row_count // block_rows),
            in_specs=[row_spec, k_spec, v_spec, k_spec, v_spec],
            out_specs=[row_spec, row_spec],
        ),
        out_shape=[
            jax.ShapeDtypeStruct((row_count, width), jnp.bfloat16),
            jax.ShapeDtypeStruct((row_count, width), jnp.float32),
        ],
        compiler_params=pltpu.CompilerParams(vmem_limit_bytes=VMEM_LIMIT),
        cost_estimate=pl.CostEstimate(
            flops=8 * row_count * keys * width,
            bytes_accessed=8 * (row_count + keys) * width,
            transcendentals=2 * row_count * keys * num_heads,
        ),
    )(kept, queries, kv_near, kv_near, kv_far, kv_far)


def attend_back_kernel(
    head_size, masked, kept_ref, q_ref, g_ref, l_ref, k0_ref, v0_ref, k1_ref, v1_ref,
    dq_ref, dk0_ref, dv0_ref, dk1_ref, dv1_ref,
):
    scaling = head_size ** (-0.5)
    exponent = scaling * math.log2(math.e)
    lane_head = lax.broadcasted_iota(jnp.int32, (1, LANES), 1) // head_size
    kept = (kept_ref[0], kept_ref[1]) if masked else (None, None)

    @pl.when(pl.program_id(1) == 0)
    def _():
        for ref in (dk0_ref, dv0_ref, dk1_ref, dv1_ref):
            ref[...] = jnp.zeros_like(ref)

    queries, grads, log_totals = q_ref[...], g_ref[...], l_ref[...]
    grad_queries = jnp.zeros(dq_ref.shape, jnp.float32)
    for head in range(LANES // head_size):
        chosen = lane_head == head
        head_queries = jnp.where(chosen, queries, jnp.zeros_like(queries))
        head_grads = jnp.where(chosen, grads, jnp.zeros_like(grads))
        log_total = log_totals[:, head * head_size : head * head_size + 1]
        probs, steps, totals = [], [], 0.0
        for k_ref, v_ref, count in ((k0_ref, v0_ref, kept[0]), (k1_ref, v1_ref, kept[1])):
            attn = jnp.exp2(head_scores(head_queries, k_ref[...], count) * exponent - log_total)
            step = outer_rows(head_grads, v_ref[...]) * attn
            totals = totals + jnp.sum(step, axis=1, keepdims=True)
            probs.append(attn)
            steps.append(step)
        outcome = 0.0
        for attn, step, k_ref, dk_ref, dv_ref in zip(
            probs, steps, (k0_ref, k1_ref), (dk0_ref, dk1_ref), (dv0_ref, dv1_ref)
        ):
            grad_logits = (step - attn * totals).astype(jnp.bfloat16)
            dv_ref[...] += jnp.transpose(inner_rows(head_grads, attn.astype(jnp.bfloat16)))
            dk_ref[...] += jnp.transpose(inner_rows(head_queries, grad_logits)) * scaling
            outcome = outcome + matmul(grad_logits, k_ref[...])
        grad_queries = jnp.where(chosen, outcome * scaling, grad_queries)
    dq_ref[...] = grad_queries.astype(dq_ref.dtype)


def attend_rows_back(queries, grads, log_totals, kv_near, kv_far, kept, num_heads, block_rows):
    row_count, width = queries.shape
    keys = kv_near.shape[0]
    groups = width // LANES
    masked = kept is not None
    if not masked:
        kept = jnp.zeros((2,), jnp.int32)
    row_spec = pl.BlockSpec((block_rows, LANES), lambda g, b, kept: (b, g))
    k_spec = pl.BlockSpec((keys, LANES), lambda g, b, kept: (0, g))
    v_spec = pl.BlockSpec((keys, LANES), lambda g, b, kept: (0, g + groups))
    key_shape = jax.ShapeDtypeStruct((keys, width), jnp.float32)
    return pl.pallas_call(
        functools.partial(attend_back_kernel, width // num_heads, masked),
        grid_spec=pltpu.PrefetchScalarGridSpec(
            num_scalar_prefetch=1,
            grid=(groups, row_count // block_rows),
            in_specs=[row_spec, row_spec, row_spec, k_spec, v_spec, k_spec, v_spec],
            out_specs=[row_spec, k_spec, k_spec, k_spec, k_spec],
        ),
        out_shape=[jax.ShapeDtypeStruct((row_count, width), jnp.bfloat16)] + [key_shape] * 4,
        compiler_params=pltpu.CompilerParams(vmem_limit_bytes=VMEM_LIMIT),
        cost_estimate=pl.CostEstimate(
            flops=20 * row_count * keys * width,
            bytes_accessed=8 * (row_count + 4 * keys) * width,
            transcendentals=2 * row_count * keys * num_heads,
        ),
    )(kept, queries, grads, log_totals, kv_near, kv_near, kv_far, kv_far)


def padded_rows(block, before, after):
    return jnp.pad(block, ((before, after), (0, 0)))


def scaled_back(stream, gain_vec, grad_out):
    discarded_value, backward_fn = jax.vjp(scaled, stream, gain_vec)
    return backward_fn(grad_out)


def gelu_erf(raised):
    return 0.5 * raised * (1.0 + lax.erf(raised * 0.5**0.5))


def gelu_slope(raised):
    bell = jnp.exp(-0.5 * raised * raised) * (2.0 * math.pi) ** (-0.5)
    return 0.5 * (1.0 + lax.erf(raised * 0.5**0.5)) + raised * bell


def feed_fwd(stream, gain_vec, w_up, w_down):
    normal_in = scaled(stream, gain_vec).astype(jnp.bfloat16)
    raised = matmul(normal_in, w_up)
    hidden = gelu_erf(raised).astype(jnp.bfloat16)
    return (stream + matmul(hidden, w_down), (normal_in, raised, hidden))


def feed_back(stream, gain_vec, w_up, w_down, stored, grad_out):
    normal_in, raised, hidden = stored
    branch_grad = grad_out.astype(jnp.bfloat16)
    grad_hidden = outer_rows(branch_grad, w_down).astype(jnp.bfloat16).astype(jnp.float32)
    grad_raised = (grad_hidden * gelu_slope(raised)).astype(jnp.bfloat16)
    grad_wup = inner_rows(normal_in, grad_raised)
    grad_normal = outer_rows(grad_raised, w_up).astype(jnp.bfloat16).astype(jnp.float32)
    grad_stream, grad_gain = scaled_back(stream, gain_vec, grad_normal)
    return (grad_out + grad_stream, grad_wup, branch_grad, grad_gain)


def swapped(block):
    devices = range(lax.axis_size("dp"))
    return lax.ppermute(block, "dp", [(i, i ^ 1) for i in devices])


def attend_fwd(stream, gain_vec, w_in, w_out, num_heads, kept, skip, block_rows):
    width = stream.shape[1]
    normal_in = scaled(stream, gain_vec).astype(jnp.bfloat16)
    kv_near = matmul(normal_in, w_in[:, width:]).astype(jnp.bfloat16)
    kv_far = swapped(kv_near)
    queries = matmul(normal_in[skip:], w_in[:, :width]).astype(jnp.bfloat16)
    merged, log_totals = attend_rows(queries, kv_near, kv_far, kept, num_heads, block_rows)
    outcome = stream[skip:] + matmul(merged, w_out)
    return (outcome, (normal_in, queries, kv_near, kv_far, merged, log_totals))


def attend_back(stream, gain_vec, w_in, w_out, num_heads, kept, skip, block_rows, stored, grad_out):
    normal_in, queries, kv_near, kv_far, merged, log_totals = stored
    branch_grad = grad_out.astype(jnp.bfloat16)
    grad_wout = inner_rows(merged, branch_grad)
    grad_merged = outer_rows(branch_grad, w_out).astype(jnp.bfloat16)
    dq, dk_near, dv_near, dk_far, dv_far = attend_rows_back(
        queries, grad_merged, log_totals, kv_near, kv_far, kept, num_heads, block_rows
    )
    dk = (dk_near + swapped(dk_far)).astype(jnp.bfloat16)
    dv = (dv_near + swapped(dv_far)).astype(jnp.bfloat16)
    grad_packed = jnp.concatenate([padded_rows(dq, skip, 0), dk, dv], axis=1)
    grad_win = inner_rows(normal_in, grad_packed)
    grad_normal = outer_rows(grad_packed, w_in).astype(jnp.bfloat16).astype(jnp.float32)
    grad_stream, grad_gain = scaled_back(stream, gain_vec, grad_normal)
    return (padded_rows(grad_out, skip, 0) + grad_stream, grad_win, grad_wout, grad_gain)


def tall_grad_kernel(first_blocks, x_ref, gx_ref, h_ref, gh_ref, out_ref):
    @pl.when(pl.program_id(0) < first_blocks)
    def _():
        out_ref[...] = inner_rows(x_ref[...], gx_ref[...]).astype(out_ref.dtype)

    @pl.when(pl.program_id(0) >= first_blocks)
    def _():
        out_ref[...] = inner_rows(h_ref[...], gh_ref[...]).astype(out_ref.dtype)


def tall_grad(chosen, grad_stream, hidden, branch_grad):
    rows, width = grad_stream.shape
    block = 512
    first_blocks, blocks = PATCH // block, (PATCH + FF) // block
    return pl.pallas_call(
        functools.partial(tall_grad_kernel, first_blocks),
        grid=(blocks,),
        in_specs=[
            pl.BlockSpec((rows, block), lambda i: (0, jnp.minimum(i, first_blocks - 1))),
            pl.BlockSpec((rows, width), lambda i: (0, 0)),
            pl.BlockSpec((rows, block), lambda i: (0, jnp.maximum(i - first_blocks, 0))),
            pl.BlockSpec((rows, width), lambda i: (0, 0)),
        ],
        out_specs=pl.BlockSpec((block, width), lambda i: (i, 0)),
        out_shape=jax.ShapeDtypeStruct((PATCH + FF, width), jnp.bfloat16),
        compiler_params=pltpu.CompilerParams(vmem_limit_bytes=VMEM_LIMIT),
        cost_estimate=pl.CostEstimate(
            flops=2 * rows * width * (PATCH + FF),
            bytes_accessed=2 * (PATCH + FF) * (rows + width),
            transcendentals=0,
        ),
    )(chosen, grad_stream, hidden, branch_grad)


MESH = pl.DeviceIdType.MESH


def normed_rows(source, target, rows, gain_row, chunk, twice=False):
    def step(i, carried_through):
        at = pl.ds(pl.multiple_of(i * chunk, 16), chunk)
        values = normed(source[at, :]) * gain_row
        if twice:
            values = normed(values)
        target[at, :] = values.astype(target.dtype)
        return carried_through

    lax.fori_loop(0, rows // chunk, step, 0)


def gather_kernel(count, zn, *refs):
    ins, refs = refs[:count], refs[count:]
    pixels_ref, here_ref, there_ref, order_ref, high_ref, low_ref, *refs = refs
    outs, refs = refs[:count], refs[count:]
    goal_ref, picked_ref, table_ref, *refs = refs
    stages, refs = refs[:count], refs[count:]
    facts_ref, t0_ref, a_ref, near_ref, far_ref, q_ref, o_ref, h_ref, sum_ref, embed_buf, qkv_buf, up_buf, down_buf, *refs = refs
    pixel_buf, other_ref, chosen_ref, wide_buf, pred_buf, *refs = refs
    local_sem, z_send, z_recv, p_send, p_recv, w_sem, kv_sem = refs
    section, place = lax.axis_index("section"), lax.axis_index("dp")
    z, core = place // 2, place % 2
    near = {"section": section + 1 - 2 * (section % 2)}
    far = {"section": (section + 2) % 4}
    mate = {"dp": place + 1 - 2 * core}
    ahead = {"dp": place + 2}
    behind = {"dp": place - 2}

    def landing(a):
        rows, columns = stages[a].shape
        if ins[a].dtype == stages[a].dtype:
            return stages[a]
        buffer = t0_ref if columns == D and rows > 48 else wide_buf if columns == 8 * D else pred_buf
        return buffer.at[pl.ds(0, rows), pl.ds(0, columns)]

    def fetched(a):
        source = ins[a].at[:, pl.ds(0, stages[a].shape[1])]
        return pltpu.make_async_copy(source, landing(a), local_sem.at[a])

    for a in FIRST_IN:
        fetched(a).start()

    barrier = pltpu.get_barrier_semaphore()
    line = [{"dp": (z + j) % zn * 2 + core} for j in range(1, zn)]
    for other in [near, far, mate] + line:
        pl.semaphore_signal(barrier, inc=1, device_id=other, device_id_type=MESH)
    pl.semaphore_wait(barrier, 3 + len(line))

    def block(ref, a, owner_z, quarter=None, rows=None, owner_core=core):
        size = stages[a].shape[0]
        start, length = (0, size) if rows is None else rows
        offset = pl.multiple_of((owner_z * 2 + owner_core) * size + start, 16)
        if quarter is None:
            return ref.at[pl.ds(offset, length), :]
        width = stages[a].shape[1] // 4
        return ref.at[pl.ds(offset, length), pl.ds(pl.multiple_of(quarter * width, 128), width)]

    def own_quarter(a):
        width = stages[a].shape[1] // 4
        return stages[a].at[:, pl.ds(pl.multiple_of(section * width, 128), width)]

    def copy(src, dst, sends, recvs, index, device):
        return pltpu.make_async_remote_copy(
            src_ref=src,
            dst_ref=dst,
            send_sem=sends.at[index],
            recv_sem=recvs.at[index],
            device_id=device,
            device_id_type=MESH,
        )

    def along(a, step, upward):
        device = ahead if upward else behind
        source_z = z - (step - 1) if upward else z + (step - 1)
        src = own_quarter(a) if step == 1 else block(outs[a], a, source_z, section)
        index = (a * (zn - 1) + step - 1) * 2 + (0 if upward else 1)
        return copy(src, block(outs[a], a, source_z, section), z_send, z_recv, index, device)

    def sends_along(step, upward):
        if upward:
            return (z - (step - 1) >= 0) & (z < zn - 1)
        return (z + (step - 1) <= zn - 1) & (z > 0)

    def first_half(a):
        size = stages[a].shape[0]
        return (0, (size + 31) // 32 * 16)

    def second_half(a):
        size = stages[a].shape[0]
        start = (size + 31) // 32 * 16
        return (start, size - start)

    def in_plane(a, step, upward, kind):
        owner_z = z - step if upward else z + step
        index = ((a * (zn - 1) + step - 1) * 2 + (0 if upward else 1)) * 5 + kind
        x_quarter, y_quarter = near["section"], far["section"]
        part = [
            lambda: block(outs[a], a, owner_z, section),
            lambda: block(outs[a], a, owner_z, section),
            lambda: block(outs[a], a, owner_z, x_quarter, first_half(a)),
            lambda: block(outs[a], a, owner_z, y_quarter, second_half(a)),
            lambda: block(outs[a], a, owner_z),
        ][kind]()
        return copy(part, part, p_send, p_recv, index, (near, far, far, near, mate)[kind])

    def offered(a):
        for upward in (True, False):

            @pl.when(sends_along(1, upward))
            def _(upward=upward):
                along(a, 1, upward).start()

    own = []
    settled = []
    base = count * (zn - 1) * 10
    for a in ARRIVAL:
        fetched(a).wait()
        if ins[a].dtype != stages[a].dtype:
            source = landing(a)

            def rounded(i, carried_through):
                at = pl.ds(pl.multiple_of(i * 16, 16), 16)
                stages[a][at, :] = source[at, :].astype(stages[a].dtype)
                return carried_through

            lax.fori_loop(0, stages[a].shape[0] // 16, rounded, 0)
        if a in NEXT_IN:
            fetched(NEXT_IN[a]).start()
        keep = pltpu.make_async_copy(stages[a], block(outs[a], a, z), local_sem.at[a])
        give = copy(stages[a], block(outs[a], a, z), p_send, p_recv, base + a, mate)
        if a < 2:
            offered(a)
        keep.start()
        give.start()
        own.append((a, keep, give))
    own = [(keep, give) for a, keep, give in sorted(own, key=lambda entry: entry[0])]

    items = [
        (a, step, upward)
        for a in range(count)
        for step in range(1, zn)
        for upward in (True, False)
    ]

    def arrives(step, upward):
        return z - step >= 0 if upward else z + step <= zn - 1

    def received(a, step, upward):
        @pl.when(arrives(step, upward))
        def _():
            along(a, step, upward).wait_recv()
            in_plane(a, step, upward, 0).start()
            in_plane(a, step, upward, 1).start()

        if step < zn - 1:

            @pl.when(arrives(step, upward) & sends_along(step + 1, upward))
            def _():
                along(a, step + 1, upward).start()

    def passed_on(a, step, upward):
        @pl.when(arrives(step, upward))
        def _():
            in_plane(a, step, upward, 0).wait_recv()
            in_plane(a, step, upward, 2).start()
            in_plane(a, step, upward, 1).wait_recv()
            in_plane(a, step, upward, 3).start()

    def completed(a, step, upward):
        @pl.when(arrives(step, upward))
        def _():
            in_plane(a, step, upward, 2).wait_recv()
            in_plane(a, step, upward, 3).wait_recv()
            in_plane(a, step, upward, 4).start()

    lag = 3
    group = 2 * (zn - 1)

    def advance(i):
        if i % group == 0 and 2 <= i // group + 1 < count:
            offered(i // group + 1)
        if 0 <= i - 2 * lag < len(items):
            completed(*items[i - 2 * lag])
        if 0 <= i - lag < len(items):
            passed_on(*items[i - lag])
        if i < len(items):
            received(*items[i])

    def settle(a):
        keep, give = own[a]
        keep.wait()
        give.wait_recv()
        for b, step, upward in items:
            if b == a:

                @pl.when(arrives(step, upward))
                def _(step=step, upward=upward):
                    in_plane(a, step, upward, 4).wait_recv()

        settled.append(a)

    def run_loop(length, body, steps):
        def step(i, carried_through):
            body(i)
            for at, move in enumerate(steps):
                pl.when(i == at * length // len(steps))(functools.partial(advance, move))
            return carried_through

        lax.fori_loop(0, length, step, 0)

    def streamed(length, fetches, body, steps):
        for fetch in fetches:
            fetch(0).start()

        def with_blocks(i):
            @pl.when(i + 1 < length)
            def _():
                for fetch in fetches:
                    fetch(i + 1).start()

            for fetch in fetches:
                fetch(i).wait()
            body(i, i % 2)

        run_loop(length, with_blocks, steps)

    def column_fetch(a, rows, first, width, buffer, sem):
        def fetch(i):
            columns = pl.ds(pl.multiple_of(first + i * width, 128), width)
            return pltpu.make_async_copy(
                outs[a].at[rows, columns], buffer.at[i % 2], w_sem.at[sem * 2 + i % 2]
            )

        return fetch

    ends = [group * (a + 1) + 2 * lag for a in range(count)]
    last = len(items) + 2 * lag
    SMALL, TALL, WIDE = 0, 1, 2
    clips_here = pixels_ref.shape[0]
    holds = core == section // clips_here
    first = list(range(min(ends[TALL], last)))
    pixel_copy = pltpu.make_async_copy(pixels_ref.at[section % clips_here], pixel_buf, kv_sem.at[2])
    handed = pltpu.make_async_remote_copy(
        src_ref=other_ref,
        dst_ref=chosen_ref,
        send_sem=kv_sem.at[3],
        recv_sem=kv_sem.at[4],
        device_id=mate,
        device_id_type=MESH,
    )

    @pl.when(holds)
    def _():
        pixel_copy.start()

    def tabulate(i):
        rows = pl.ds(pl.multiple_of(i * 96, 16), 96)
        order = order_ref[rows, :]

        def wave(table, index):
            choice = lax.broadcasted_iota(jnp.int32, (96, table.shape[0]), 1) == index
            return jnp.dot(
                choice.astype(jnp.float32), table[...],
                precision=lax.Precision.HIGHEST, preferred_element_type=jnp.float32,
            )

        high, low = wave(high_ref, order // 32), wave(low_ref, order % 32)
        sin_high, cos_high = high[:, : D // 2], high[:, D // 2 :]
        sin_low, cos_low = low[:, : D // 2], low[:, D // 2 :]
        t0_ref[rows, : D // 2] = sin_high * cos_low + cos_high * sin_low
        t0_ref[rows, D // 2 :] = cos_high * cos_low - sin_high * sin_low

    run_loop(HALF // 96, tabulate, first[:2])
    table_ref[...] = t0_ref[:SEEN, :]

    @pl.when(holds)
    def _():
        pixel_copy.wait()

    def pick(source, target):
        def rows_picked(i):
            @pl.when(holds)
            def _():
                rows = pl.ds(pl.multiple_of(i * 96, 16), 96)
                choice = lax.broadcasted_iota(jnp.int32, (96, L), 1) == source[rows, :]
                target[rows, :] = matmul(choice.astype(jnp.bfloat16), pixel_buf[...]).astype(jnp.bfloat16)

        return rows_picked

    run_loop(HALF // 96, pick(there_ref, other_ref), first[2:5])

    @pl.when(holds)
    def _():
        handed.start()

    run_loop(HALF // 96, pick(here_ref, chosen_ref), first[5:8])
    for i in first[8:]:
        advance(i)

    @pl.when(holds)
    def _():
        handed.wait_send()

    @pl.when(jnp.logical_not(holds))
    def _():
        handed.wait_recv()

    picked_ref[...] = chosen_ref[:SEEN, :]
    settle(SMALL)
    settle(TALL)
    facts = pltpu.make_async_copy(outs[SMALL].at[:, PD : PD + LANES], facts_ref, local_sem.at[SMALL])
    facts.start()

    def embed(i, slot):
        at = pl.ds(pl.multiple_of(i * 256, 128), 256)
        t0_ref[:, at] += matmul(chosen_ref[...], embed_buf[slot])

    waiting = list(range(ends[TALL], min(ends[WIDE], last)))
    streamed(4, [column_fetch(TALL, pl.ds(0, PATCH), 0, 256, embed_buf, 0)], embed, waiting[:2])
    facts.wait()
    gain_rows = jnp.transpose(facts_ref[...].astype(jnp.float32))
    normed_rows(t0_ref, a_ref, HALF, gain_rows[3:4, :], 96)
    for i in waiting[2:]:
        advance(i)
    settle(WIDE)

    rest = list(range(ends[WIDE], last))
    cuts = [len(rest) * part // 80 for part in (0, 8, 12, 48, 54, 80)]
    rest = [rest[cuts[i] : cuts[i + 1]] for i in range(5)]
    whole_rows = pl.ds(0, D)

    def keys_values(i, slot):
        at = pl.ds(pl.multiple_of(i * 256, 128), 256)
        near_ref[:, at] = matmul(a_ref[...], qkv_buf[slot]).astype(jnp.bfloat16)

    def queries(i, slot):
        at = pl.ds(pl.multiple_of(i * 256, 128), 256)
        q_ref[:, at] = matmul(a_ref[SKIP:, :], qkv_buf[slot]).astype(jnp.bfloat16)

    streamed(8, [column_fetch(WIDE, whole_rows, D, 256, qkv_buf, 1)], keys_values, rest[0])
    share = pltpu.make_async_remote_copy(
        src_ref=near_ref,
        dst_ref=far_ref,
        send_sem=kv_sem.at[0],
        recv_sem=kv_sem.at[1],
        device_id=mate,
        device_id_type=MESH,
    )
    share.start()
    streamed(4, [column_fetch(WIDE, whole_rows, 0, 256, qkv_buf, 1)], queries, rest[1])
    share.wait()
    block_rows = (HALF - SKIP) // 2

    def attention(i):
        lanes = pl.ds(pl.multiple_of(i // 2 * LANES, LANES), LANES)
        values = pl.ds(pl.multiple_of(D + i // 2 * LANES, LANES), LANES)
        rows = pl.ds(pl.multiple_of(i % 2 * block_rows, 16), block_rows)
        attend_kernel(
            D // HE, False, None, q_ref.at[rows, lanes], near_ref.at[:, lanes],
            near_ref.at[:, values], far_ref.at[:, lanes], far_ref.at[:, values],
            o_ref.at[rows, lanes], None,
        )

    run_loop(2 * D // LANES, attention, rest[2])

    def merge(i, slot):
        at = pl.ds(pl.multiple_of(i * 256, 128), 256)
        stream = t0_ref[SKIP:, at] + matmul(o_ref[...], qkv_buf[slot])
        sum_ref[:, at] = stream.astype(jnp.bfloat16).astype(jnp.float32)

    streamed(4, [column_fetch(WIDE, whole_rows, 3 * D, 256, qkv_buf, 1)], merge, rest[3])

    row_count = HALF - SKIP
    normed_rows(sum_ref, a_ref, row_count, gain_rows[4:5, :], 96)

    def down_fetch(i):
        rows = pl.ds(pl.multiple_of(PATCH + i * 512, 16), 512)
        return pltpu.make_async_copy(outs[TALL].at[rows, :], down_buf.at[i % 2], w_sem.at[6 + i % 2])

    def feed(i, slot):
        for part in range(2):
            rows = pl.ds(part * block_rows, block_rows)
            h_ref[...] = gelu_erf(matmul(a_ref[rows, :], up_buf[slot])).astype(jnp.bfloat16)
            sum_ref[rows, :] += matmul(h_ref[...], down_buf[slot])

    streamed(
        8,
        [column_fetch(WIDE, whole_rows, 4 * D, 512, up_buf, 2), down_fetch],
        feed,
        rest[4],
    )
    normed_rows(sum_ref, goal_ref, row_count, gain_rows[5:6, :], 96, twice=True)

    for a in range(count):
        if a not in settled:
            settle(a)
    for keep, give in own:
        give.wait_send()
    for a, step, upward in items:

        @pl.when(sends_along(step, upward))
        def _(a=a, step=step, upward=upward):
            along(a, step, upward).wait_send()

        @pl.when(arrives(step, upward))
        def _(a=a, step=step, upward=upward):
            for kind in range(5):
                in_plane(a, step, upward, kind).wait_send()


FIRST_IN = (0, 1, 2, 5, 6)
ARRIVAL = (0, 1, 2, 3, 4, 5, 6)
NEXT_IN = {1: 3, 2: 4}


def gather_and_teach(blocks, widths, pixels, order_here, order_there, order):
    count = len(blocks)
    dp_size = lax.axis_size("dp")
    zn = dp_size // 2
    return pl.pallas_call(
        functools.partial(gather_kernel, count, zn),
        in_specs=[pl.BlockSpec(memory_space=pl.ANY)] * count
        + [pl.BlockSpec(memory_space=pl.ANY)]
        + [pl.BlockSpec(memory_space=pltpu.VMEM)] * 5,
        out_specs=[pl.BlockSpec(memory_space=pl.ANY)] * count
        + [pl.BlockSpec(memory_space=pltpu.VMEM)] * 3,
        out_shape=[
            jax.ShapeDtypeStruct((member.shape[0] * dp_size, width), jnp.bfloat16)
            for member, width in zip(blocks, widths)
        ]
        + [
            jax.ShapeDtypeStruct((HALF - SKIP, D), jnp.bfloat16),
            jax.ShapeDtypeStruct((SEEN, PATCH), jnp.bfloat16),
            jax.ShapeDtypeStruct((SEEN, D), jnp.float32),
        ],
        scratch_shapes=[
            pltpu.VMEM((member.shape[0], width), jnp.bfloat16)
            for member, width in zip(blocks, widths)
        ]
        + [
            pltpu.VMEM((D, LANES), jnp.bfloat16),
            pltpu.VMEM((HALF, D), jnp.float32),
            pltpu.VMEM((HALF, D), jnp.bfloat16),
            pltpu.VMEM((HALF, 2 * D), jnp.bfloat16),
            pltpu.VMEM((HALF, 2 * D), jnp.bfloat16),
            pltpu.VMEM((HALF - SKIP, D), jnp.bfloat16),
            pltpu.VMEM((HALF - SKIP, D), jnp.bfloat16),
            pltpu.VMEM(((HALF - SKIP) // 2, 512), jnp.bfloat16),
            pltpu.VMEM((HALF - SKIP, D), jnp.float32),
            pltpu.VMEM((2, PATCH, 256), jnp.bfloat16),
            pltpu.VMEM((2, D, 256), jnp.bfloat16),
            pltpu.VMEM((2, D, 512), jnp.bfloat16),
            pltpu.VMEM((2, 512, D), jnp.bfloat16),
            pltpu.VMEM((L, PATCH), jnp.bfloat16),
            pltpu.VMEM((HALF, PATCH), jnp.bfloat16),
            pltpu.VMEM((HALF, PATCH), jnp.bfloat16),
            pltpu.VMEM((blocks[2].shape[0], 8 * D), jnp.float32),
            pltpu.VMEM(blocks[5].shape, jnp.float32),
        ]
        + [
            pltpu.SemaphoreType.DMA((count,)),
            pltpu.SemaphoreType.DMA((count * (zn - 1) * 2,)),
            pltpu.SemaphoreType.DMA((count * (zn - 1) * 2,)),
            pltpu.SemaphoreType.DMA((count * ((zn - 1) * 10 + 1),)),
            pltpu.SemaphoreType.DMA((count * ((zn - 1) * 10 + 1),)),
            pltpu.SemaphoreType.DMA((8,)),
            pltpu.SemaphoreType.DMA((5,)),
        ],
        compiler_params=pltpu.CompilerParams(
            collective_id=0, has_side_effects=True, vmem_limit_bytes=58 * 1024 * 1024
        ),
    )(
        *blocks,
        pixels,
        order_here[:, None],
        order_there[:, None],
        order[:, None],
        position_table(32 * lax.iota(jnp.int32, L // 32), D),
        position_table(lax.iota(jnp.int32, 32), D),
    )


def upper_rows(size):
    return (size + 31) // 32 * 16


def add_blocks(rows, targets):
    def step(i, carried_through):
        at = pl.ds(pl.multiple_of(i * 16, 16), 16)
        for out, terms in targets:
            out[at, :] = sum(term[at, :].astype(jnp.float32) for term in terms).astype(out.dtype)
        return carried_through

    lax.fori_loop(0, rows // 16, step, 0)


def reduce_kernel(count, zn, *refs):
    ins, refs = refs[: count + 1], refs[count + 1 :]
    outs, refs = refs[: count + 1], refs[count + 1 :]
    whole, refs = refs[:count], refs[count:]
    near_one, refs = refs[:count], refs[count:]
    far_one, refs = refs[:count], refs[count:]
    far_two, refs = refs[:count], refs[count:]
    near_two, refs = refs[:count], refs[count:]
    along, refs = refs[:count], refs[count:]
    loaded, refs = refs[:count], refs[count:]
    held, refs = refs[:count], refs[count:]
    done, refs = refs[:count], refs[count:]
    total_ref, side_ref, line_ref, load_sem, move_send, move_recv, side_send, side_recv, line_send, line_recv = refs
    tally, out_total = ins[count], outs[count]
    tally_rows = out_total.shape[0]

    section, place = lax.axis_index("section"), lax.axis_index("dp")
    z, core = place // 2, place % 2
    x_quarter = section + 1 - 2 * (section % 2)
    y_quarter = (section + 2) % 4
    xy_quarter = (x_quarter + 2) % 4
    near, far = {"section": x_quarter}, {"section": y_quarter}
    mate = {"dp": place + 1 - 2 * core}
    sizes = [out.shape[0] for out in outs[:count]]
    widths = [out.shape[1] // 4 for out in outs[:count]]

    barrier = pltpu.get_barrier_semaphore()
    line = [{"dp": (z + j) % zn * 2 + core} for j in range(1, zn)]
    for other in [near, far, mate] + line:
        pl.semaphore_signal(barrier, inc=1, device_id=other, device_id_type=MESH)
    pl.semaphore_wait(barrier, 3 + len(line))

    def rows_at(a, slot, start=0, length=None):
        return pl.ds(pl.multiple_of(slot * sizes[a] + start, 16), sizes[a] if length is None else length)

    def quarter_at(a, quarter):
        return pl.ds(pl.multiple_of(quarter * widths[a], 128), widths[a])

    def upper(a):
        return upper_rows(sizes[a])

    def lower(a):
        return sizes[a] - upper_rows(sizes[a])

    def sent(src, dst, kind, a, slot, device):
        index = (kind * count + a) * (zn + 1) + slot
        return pltpu.make_async_remote_copy(
            src_ref=src,
            dst_ref=dst,
            send_sem=move_send.at[index],
            recv_sem=move_recv.at[index],
            device_id=device,
            device_id_type=MESH,
        )

    def load(a, owner_z):
        source = pl.ds(pl.multiple_of((owner_z * 2 + core) * sizes[a], 16), sizes[a])
        return pltpu.make_async_copy(
            ins[a].at[source, :], loaded[a].at[rows_at(a, owner_z), :], load_sem.at[a * zn + owner_z]
        )

    def give(a, owner_z):
        source = pl.ds(pl.multiple_of((owner_z * 2 + 1 - core) * sizes[a], 16), sizes[a])
        return sent(ins[a].at[source, :], whole[a].at[rows_at(a, owner_z), :], 0, a, owner_z, mate)

    def first_near(a, owner_z, which):
        quarter = (x_quarter, xy_quarter)[which]
        return sent(
            whole[a].at[rows_at(a, owner_z, 0, upper(a)), quarter_at(a, quarter)],
            near_one[a].at[pl.ds(pl.multiple_of((owner_z * 2 + which) * upper(a), 16), upper(a)), :],
            1 + which, a, owner_z, near,
        )

    def first_far(a, owner_z, which):
        quarter = (y_quarter, xy_quarter)[which]
        return sent(
            whole[a].at[rows_at(a, owner_z, upper(a), lower(a)), quarter_at(a, quarter)],
            far_one[a].at[pl.ds(pl.multiple_of((owner_z * 2 + which) * lower(a), 16), lower(a)), :],
            3 + which, a, owner_z, far,
        )

    def second_far(a, owner_z):
        return sent(
            whole[a].at[rows_at(a, owner_z, 0, upper(a)), quarter_at(a, y_quarter)],
            far_two[a].at[pl.ds(pl.multiple_of(owner_z * upper(a), 16), upper(a)), :],
            5, a, owner_z, far,
        )

    def second_near(a, owner_z):
        return sent(
            whole[a].at[rows_at(a, owner_z, upper(a), lower(a)), quarter_at(a, x_quarter)],
            near_two[a].at[pl.ds(pl.multiple_of(owner_z * lower(a), 16), lower(a)), :],
            6, a, owner_z, near,
        )

    def onward(a, owner_z, upward, last):
        slot = zn if last and not upward else owner_z
        return sent(
            whole[a].at[rows_at(a, owner_z), quarter_at(a, section)],
            along[a].at[rows_at(a, slot), :],
            7, a, slot, {"dp": place + 2 if upward else place - 2},
        )

    def finished(a, kind):
        quarter = (section, section, x_quarter, y_quarter)[kind]
        columns = quarter_at(a, quarter)
        part = (
            pl.ds(0, sizes[a]), pl.ds(0, sizes[a]), pl.ds(0, upper(a)), pl.ds(upper(a), lower(a))
        )[kind]
        src = done[a] if kind < 2 else outs[a].at[part, columns]
        return sent(src, outs[a].at[part, columns], 8 + kind, a, 0, (near, far, far, near)[kind])

    def keep(a):
        return pltpu.make_async_copy(
            done[a], outs[a].at[:, quarter_at(a, section)], load_sem.at[a * zn]
        )

    legs = [(k, upward) for k in range(zn - 1, 0, -1) for upward in (True, False)] + [(0, True)]
    items = [(a, leg) for leg in range(len(legs)) for a in range(count)]

    def owner_of(leg):
        k, upward = legs[leg]
        return z + k if upward else z - k

    def is_live(leg):
        k, upward = legs[leg]
        return (z + k <= zn - 1) if upward else (z - k >= 0)

    def started(a, leg):
        @pl.when(is_live(leg))
        def _():
            give(a, owner_of(leg)).start()

    def load_started(a, leg):
        @pl.when(is_live(leg))
        def _():
            load(a, owner_of(leg)).start()

    def parts(a, owner_z, is_upper, quarter):
        size = (0, upper(a)) if is_upper else (upper(a), lower(a))
        at = (rows_at(a, owner_z, *size), quarter_at(a, quarter))
        return (whole[a].at[at], loaded[a].at[at])

    def pair_up(a, owner_z, is_upper, quarter):
        both = parts(a, owner_z, is_upper, quarter)
        add_blocks(upper(a) if is_upper else lower(a), [(both[0], both)])

    def paired(a, leg):
        @pl.when(is_live(leg))
        def _():
            owner_z = owner_of(leg)
            load(a, owner_z).wait()
            give(a, owner_z).wait_recv()
            for quarter in (xy_quarter, x_quarter):
                pair_up(a, owner_z, True, quarter)
            for quarter in (xy_quarter, y_quarter):
                pair_up(a, owner_z, False, quarter)
            for which in (1, 0):
                first_near(a, owner_z, which).start()
                first_far(a, owner_z, which).start()


    def from_near(a, owner_z, which):
        start = pl.multiple_of((owner_z * 2 + which) * upper(a), 16)
        return near_one[a].at[pl.ds(start, upper(a)), :]

    def from_far(a, owner_z, which):
        start = pl.multiple_of((owner_z * 2 + which) * lower(a), 16)
        return far_one[a].at[pl.ds(start, lower(a)), :]

    def halved(a, leg):
        @pl.when(is_live(leg))
        def _():
            owner_z = owner_of(leg)
            first_near(a, owner_z, 1).wait_recv()
            both = parts(a, owner_z, True, y_quarter)
            add_blocks(upper(a), [(both[0], both + (from_near(a, owner_z, 1),))])
            second_far(a, owner_z).start()
            first_far(a, owner_z, 1).wait_recv()
            both = parts(a, owner_z, False, x_quarter)
            add_blocks(lower(a), [(both[0], both + (from_far(a, owner_z, 1),))])
            second_near(a, owner_z).start()

    def quartered(a, leg):
        k, upward = legs[leg]

        @pl.when(is_live(leg))
        def _():
            owner_z = owner_of(leg)
            own = quarter_at(a, section)
            first_near(a, owner_z, 0).wait_recv()
            second_far(a, owner_z).wait_recv()
            start = pl.multiple_of(owner_z * upper(a), 16)
            terms = parts(a, owner_z, True, section) + (
                from_near(a, owner_z, 0), far_two[a].at[pl.ds(start, upper(a)), :]
            )
            add_blocks(upper(a), [(held[a].at[pl.ds(0, upper(a)), :], terms)])
            first_far(a, owner_z, 0).wait_recv()
            second_near(a, owner_z).wait_recv()
            start = pl.multiple_of(owner_z * lower(a), 16)
            terms = parts(a, owner_z, False, section) + (
                from_far(a, owner_z, 0), near_two[a].at[pl.ds(start, lower(a)), :]
            )
            add_blocks(lower(a), [(held[a].at[pl.ds(upper(a), lower(a)), :], terms)])
            target = held[a]

            def join(upward_from, slot):
                onward(a, owner_z, upward_from, slot is not owner_z or k == 0).wait_recv()
                add_blocks(sizes[a], [(target, (target, along[a].at[rows_at(a, slot), :]))])

            if k > 0:

                @pl.when(z > 0 if upward else z < zn - 1)
                def _():
                    join(upward, owner_z)

                add_blocks(sizes[a], [(whole[a].at[rows_at(a, owner_z), own], (target,))])
                onward(a, owner_z, upward, k == 1).start()
            else:

                @pl.when(z > 0)
                def _():
                    join(True, owner_z)

                @pl.when(z < zn - 1)
                def _():
                    join(False, zn)

                def settle(i, carried_through):
                    at = pl.ds(pl.multiple_of(i * 16, 16), 16)
                    values = target[at, :]
                    done[a][at, :] = values.astype(done[a].dtype)
                    squares = values * values
                    squares = squares[:8] + squares[8:]
                    carried = total_ref[0:8, :]
                    for column in range(0, widths[a], 128):
                        carried = carried + squares[:, column : column + 128]
                    total_ref[0:8, :] = carried
                    return carried_through

                lax.fori_loop(0, sizes[a] // 16, settle, 0)
                keep(a).start()
                finished(a, 0).start()
                finished(a, 1).start()

    total_ref[0:8, :] = jnp.zeros((8, 128), jnp.float32)
    tally_copy = pltpu.make_async_copy(tally, total_ref.at[8:, :], load_sem.at[count * zn])
    tally_copy.start()
    for a, leg in items:
        started(a, leg)
        load_started(a, leg)
    lag = 5
    for i in range(len(items) + 2 * lag):
        if i < len(items):
            paired(*items[i])
        if 0 <= i - lag < len(items):
            halved(*items[i - lag])
        if 0 <= i - 2 * lag < len(items):
            quartered(*items[i - 2 * lag])

    tally_copy.wait()

    def exchanged(stage, device):
        return pltpu.make_async_remote_copy(
            src_ref=total_ref,
            dst_ref=side_ref.at[pl.ds(stage * tally_rows, tally_rows), :],
            send_sem=side_send.at[stage],
            recv_sem=side_recv.at[stage],
            device_id=device,
            device_id_type=MESH,
        )

    for stage, device in enumerate((mate, near, far)):
        swap = exchanged(stage, device)
        swap.start()
        swap.wait()
        total_ref[...] += side_ref[stage * tally_rows : (stage + 1) * tally_rows, :]

    def told(from_z, to_z, j):
        index = from_z * zn + to_z
        return pltpu.make_async_remote_copy(
            src_ref=total_ref,
            dst_ref=line_ref.at[pl.ds(pl.multiple_of(from_z * tally_rows, 8), tally_rows), :],
            send_sem=line_send.at[index],
            recv_sem=line_recv.at[index],
            device_id={"dp": to_z * 2 + core},
            device_id_type=MESH,
        )

    for j in range(1, zn):
        told(z, (z + j) % zn, j).start()
    line_ref[pl.ds(pl.multiple_of(z * tally_rows, 8), tally_rows), :] = total_ref[...]
    for j in range(1, zn):
        told((z + j) % zn, z, j).wait_recv()
    grand = line_ref[0:tally_rows, :]
    for j in range(1, zn):
        grand = grand + line_ref[j * tally_rows : (j + 1) * tally_rows, :]
    for j in range(1, zn):
        told(z, (z + j) % zn, j).wait_send()
    total_ref[...] = grand
    show = pltpu.make_async_copy(total_ref, out_total, load_sem.at[count * zn])
    show.start()

    for a in range(count):
        finished(a, 0).wait_recv()
        finished(a, 2).start()
        finished(a, 1).wait_recv()
        finished(a, 3).start()
    for a in range(count):
        keep(a).wait()
        finished(a, 2).wait_recv()
        finished(a, 3).wait_recv()
        for kind in range(4):
            finished(a, kind).wait_send()
    for a, leg in items:
        k, upward = legs[leg]

        @pl.when(is_live(leg))
        def _(a=a, leg=leg, k=k, upward=upward):
            owner_z = owner_of(leg)
            give(a, owner_z).wait_send()
            for which in (0, 1):
                first_near(a, owner_z, which).wait_send()
                first_far(a, owner_z, which).wait_send()
            second_near(a, owner_z).wait_send()
            second_far(a, owner_z).wait_send()
            if k > 0:
                onward(a, owner_z, upward, k == 1).wait_send()

    show.wait()


def reduce_blocks(blocks, tally, result_types):
    count = len(blocks)
    dp_size = lax.axis_size("dp")
    zn = dp_size // 2
    tally_rows = 8 + tally.shape[0]
    shapes = [(member.shape[0] // dp_size, member.shape[1]) for member in blocks]
    vmem = lambda rows, columns, dtype=jnp.bfloat16: pltpu.VMEM((rows, columns), dtype)
    anywhere = pl.BlockSpec(memory_space=pl.ANY)
    moves = 12 * count * (zn + 1)
    return pl.pallas_call(
        functools.partial(reduce_kernel, count, zn),
        in_specs=[anywhere] * (count + 1),
        out_specs=[anywhere] * (count + 1),
        out_shape=[jax.ShapeDtypeStruct(shape, kind) for shape, kind in zip(shapes, result_types)]
        + [jax.ShapeDtypeStruct((tally_rows, 128), jnp.float32)],
        scratch_shapes=[vmem(zn * r, w) for r, w in shapes]
        + [vmem(zn * 2 * upper_rows(r), w // 4) for r, w in shapes]
        + [vmem(zn * 2 * (r - upper_rows(r)), w // 4) for r, w in shapes]
        + [vmem(zn * upper_rows(r), w // 4) for r, w in shapes]
        + [vmem(zn * (r - upper_rows(r)), w // 4) for r, w in shapes]
        + [vmem((zn + 1) * r, w // 4) for r, w in shapes]
        + [vmem(zn * r, w) for r, w in shapes]
        + [vmem(r, w // 4, jnp.float32) for r, w in shapes]
        + [vmem(r, w // 4, kind) for (r, w), kind in zip(shapes, result_types)]
        + [
            vmem(tally_rows, 128, jnp.float32),
            vmem(3 * tally_rows, 128, jnp.float32),
            vmem(zn * tally_rows, 128, jnp.float32),
            pltpu.SemaphoreType.DMA((count * zn + 1,)),
            pltpu.SemaphoreType.DMA((moves,)),
            pltpu.SemaphoreType.DMA((moves,)),
            pltpu.SemaphoreType.DMA((3,)),
            pltpu.SemaphoreType.DMA((3,)),
            pltpu.SemaphoreType.DMA((zn * zn,)),
            pltpu.SemaphoreType.DMA((zn * zn,)),
        ],
        compiler_params=pltpu.CompilerParams(
            collective_id=1, has_side_effects=True, vmem_limit_bytes=60 * 1024 * 1024
        ),
    )(*blocks, tally)


def adamw_step(weight, grad_now, first, second, decay, rate):
    first = BETA_ONE * first + (1.0 - BETA_ONE) * grad_now
    second = BETA_TWO * second + (1.0 - BETA_TWO) * grad_now * grad_now
    ratio = first / (1.0 - BETA_ONE**STEP) / (jnp.sqrt(second / (1.0 - BETA_TWO**STEP)) + EPSILON)
    return (weight - rate * (ratio + decay * weight), first, second)


def local(
    pixels,
    token_order,
    visible,
    wide_weight,
    tall_weight,
    pred_weight,
    pred_down,
    enc_gains,
    pred_gains,
    wide_first,
    tall_first,
    pred_first,
    pred_down_first,
    enc_gains_first,
    pred_gains_first,
    wide_second,
    tall_second,
    pred_second,
    pred_down_second,
    enc_gains_second,
    pred_gains_second,
    teacher_wide,
    teacher_tall,
    teacher_gains,
):
    masters = (wide_weight, tall_weight, pred_weight, pred_down, enc_gains, pred_gains)
    section_idx = lax.axis_index("section")
    section_count = lax.axis_size("section")
    core = lax.axis_index("dp") % 2
    clips_here = pixels.shape[0]
    assert section_count == 2 * clips_here

    owner = section_idx // clips_here
    clip = section_idx % clips_here
    holds = core == owner
    counts_own = lax.dynamic_index_in_dim(visible, clip, 0)
    order_own = lax.dynamic_index_in_dim(token_order, clip, 0, keepdims=False)
    clip_facts = jnp.concatenate([order_own, counts_own])
    clip_facts = jnp.where(holds, clip_facts, swapped(clip_facts))
    seen = clip_facts[L]
    order_pairs = clip_facts[:L].reshape(HALF, 2)
    order = jnp.where(core == 0, order_pairs[:, 0], order_pairs[:, 1])
    pairs_own = order_own.reshape(HALF, 2)
    order_here = jnp.where(core == 0, pairs_own[:, 0], pairs_own[:, 1])
    order_there = jnp.where(core == 0, pairs_own[:, 1], pairs_own[:, 0])
    seen_near = (seen - core + 1) // 2
    seen_far = (seen + core) // 2
    kept = jnp.stack([seen_near, seen_far])
    visible_high, visible_low = visible // LANES, visible % LANES
    dp_size = lax.axis_size("dp")
    row_count = wide_weight.shape[0]
    small = jnp.concatenate(
        [
            wide_weight[:, 4 * D + FF :],
            enc_gains,
            teacher_gains,
            jnp.pad(pred_gains, ((0, row_count - pred_gains.shape[0]), (0, 0))),
            jnp.zeros((row_count, LANES - 10 - 2 * clips_here), jnp.float32),
            jnp.broadcast_to(
                jnp.concatenate([visible_high, visible_low]).astype(jnp.float32)[None, :],
                (row_count, 2 * clips_here),
            ),
        ],
        axis=1,
    ).astype(jnp.bfloat16)
    pred_block = pred_weight.shape if pred_weight.shape[0] % 16 == 0 else (-1, D)
    pred_form = (PD, pred_weight.shape[1]) if pred_weight.shape[0] % 16 == 0 else (-1, D)
    blocks = (
        small,
        teacher_tall,
        teacher_wide,
        tall_weight,
        wide_weight,
        pred_weight.reshape(pred_block),
        jnp.pad(pred_down.astype(jnp.bfloat16), ((0, 0), (0, LANES))),
    )
    w_small, teach_tall, teach_wide, w_tall, w_wide, w_pred, w_down, goal, enc_chosen, table = gather_and_teach(
        blocks,
        [4 * D + FF if member is wide_weight else member.shape[1] for member in blocks],
        pixels,
        order_here,
        order_there,
        order,
    )
    goal = goal.astype(jnp.float32)
    w_pred = w_pred.reshape(PD, -1)
    w_down = w_down[:, :PD]
    pred_embed = w_small[:, :PD]
    enc_copy = w_small[:, PD : PD + 3]
    pred_copy = w_small[:, PD + 6 : PD + 10].reshape(dp_size, row_count, 4)
    pred_copy = pred_copy[:, : pred_gains.shape[0]].reshape(PD, 4)
    counts = w_small[::row_count, PD + LANES - 2 * clips_here :].astype(jnp.float32)
    counts = counts[:, :clips_here] * LANES + counts[:, clips_here:]
    target_total = jnp.sum(L - counts)
    enc_gain = enc_copy.astype(jnp.float32)
    pred_gain = pred_copy.astype(jnp.float32)
    enc_attn = (w_wide[:, : 3 * D], w_wide[:, 3 * D : 4 * D])
    enc_feed = (w_wide[:, 4 * D : 4 * D + FF], w_tall[PATCH:])
    pred_attn = (w_pred[:, : 3 * PD], w_pred[:, 3 * PD : 4 * PD])
    pred_feed = (w_pred[:, 4 * PD : 4 * PD + PF], w_down)
    pred_head = w_pred[:, 4 * PD + PF :]

    pred_table = position_table(order, PD)
    row_ids = lax.iota(jnp.int32, HALF)
    context = (row_ids < seen_near)[:, None]

    stream_a = matmul(enc_chosen, w_tall[:PATCH]) + table
    stream_b, stored_a = attend_fwd(
        stream_a, enc_gain[:, 0], enc_attn[0], enc_attn[1], HE, kept, 0, SEEN
    )
    stream_b = stream_b.astype(jnp.bfloat16).astype(jnp.float32)
    stream_c, stored_b = feed_fwd(stream_b, enc_gain[:, 1], enc_feed[0], enc_feed[1])
    encoded = scaled(stream_c, enc_gain[:, 2]).astype(jnp.bfloat16)

    projected = padded_rows(matmul(encoded, pred_embed), 0, HALF - SEEN)
    stream_d = jnp.where(context, projected, pred_gain[:, 3][None, :]) + pred_table
    stream_e, stored_d = attend_fwd(
        stream_d, pred_gain[:, 0], pred_attn[0], pred_attn[1], PH, None, SKIP, HALF - SKIP
    )
    stream_e = stream_e.astype(jnp.bfloat16).astype(jnp.float32)
    stream_f, stored_e = feed_fwd(stream_e, pred_gain[:, 1], pred_feed[0], pred_feed[1])
    final = scaled(stream_f, pred_gain[:, 2]).astype(jnp.bfloat16)
    residual = matmul(final, pred_head) - goal
    smooth_err = jnp.sqrt(residual * residual + 1.0)
    target_mask = jnp.logical_not(context[SKIP:])
    loss_part = jnp.sum(jnp.where(target_mask, smooth_err - 1.0, 0.0))
    grad_guess = (jnp.where(target_mask, residual / smooth_err, 0.0) / target_total).astype(
        jnp.bfloat16
    )

    grad_head = inner_rows(final, grad_guess)
    grad_final = outer_rows(grad_guess, pred_head).astype(jnp.bfloat16).astype(jnp.float32)
    grad_stream, grad_pg2 = scaled_back(stream_f, pred_gain[:, 2], grad_final)
    grad_stream, grad_pup, branch_grad, grad_pg1 = feed_back(
        stream_e, pred_gain[:, 1], pred_feed[0], pred_feed[1], stored_e, grad_stream
    )
    grad_down = inner_rows(stored_e[2], branch_grad)
    grad_stream = grad_stream.astype(jnp.bfloat16).astype(jnp.float32)
    grad_stream, grad_pin, grad_pout, grad_pg0 = attend_back(
        stream_d, pred_gain[:, 0], pred_attn[0], pred_attn[1], PH, None, SKIP, HALF - SKIP, stored_d, grad_stream
    )
    grad_token = jnp.sum(jnp.where(context, 0.0, grad_stream), axis=0)
    grad_projected = jnp.where(context, grad_stream, 0.0)[:SEEN].astype(jnp.bfloat16)
    grad_embed = inner_rows(encoded, grad_projected)
    grad_encoded = outer_rows(grad_projected, pred_embed).astype(jnp.bfloat16).astype(jnp.float32)
    grad_stream, grad_eg2 = scaled_back(stream_c, enc_gain[:, 2], grad_encoded)
    grad_stream, grad_eup, branch_grad, grad_eg1 = feed_back(
        stream_b, enc_gain[:, 1], enc_feed[0], enc_feed[1], stored_b, grad_stream
    )
    grad_stream = grad_stream.astype(jnp.bfloat16).astype(jnp.float32)
    grad_stream, grad_ein, grad_eout, grad_eg0 = attend_back(
        stream_a, enc_gain[:, 0], enc_attn[0], enc_attn[1], HE, kept, 0, SEEN, stored_a, grad_stream
    )
    grad_tall = tall_grad(
        enc_chosen, grad_stream.astype(jnp.bfloat16), stored_b[2], branch_grad
    )

    gain_grads = jnp.concatenate(
        [
            jnp.stack([grad_eg0, grad_eg1, grad_eg2], axis=1).reshape(-1, LANES),
            jnp.stack([grad_pg0, grad_pg1, grad_pg2, grad_token], axis=1).reshape(-1, LANES),
        ],
        axis=0,
    )
    gain_rows = 3 * D // LANES
    loss_tile = jnp.zeros((8, LANES), jnp.float32).at[0, 0].set(loss_part)
    tally = jnp.concatenate(
        [loss_tile, gain_grads, jnp.zeros((4, LANES), jnp.float32)], axis=0
    )
    blocks = shortened(
        (
            grad_ein,
            grad_eout,
            grad_eup,
            jnp.pad(grad_embed, ((0, 0), (0, LANES))),
            grad_tall,
            jnp.concatenate(shortened([grad_pin, grad_pout, grad_pup, grad_head]), axis=1).reshape(pred_form),
            jnp.pad(grad_down, ((0, 0), (0, LANES))),
        )
    )
    *summed, tally = reduce_blocks(
        blocks, tally, [jnp.bfloat16] * 5 + [jnp.float32] * 2
    )
    wide_parts = [summed[0], summed[1], summed[2], summed[3][:, :PD]]
    place = lax.axis_index("dp")
    gains_all = tally[16 : 16 + gain_rows].reshape(D, 3)
    pred_gains_all = tally[16 + gain_rows : 16 + gain_rows + 4 * PD // LANES].reshape(PD, 4)
    shares = (
        jnp.concatenate(wide_parts, axis=1).astype(jnp.float32),
        summed[4].astype(jnp.float32),
        summed[5].reshape(pred_weight.shape).astype(jnp.float32),
        summed[6][:, :PD].astype(jnp.float32),
        lax.dynamic_slice_in_dim(gains_all, place * enc_gains.shape[0], enc_gains.shape[0], 0),
        lax.dynamic_slice_in_dim(pred_gains_all, place * pred_gains.shape[0], pred_gains.shape[0], 0),
    )
    loss_sum = tally[8, 0]
    square_total = jnp.sum(tally[:8]) + jnp.sum(jnp.square(tally[16:]))
    grad_norm = jnp.sqrt(square_total)
    factor = jnp.minimum(1.0, CLIP_AT / (grad_norm + 1e-06))
    firsts = (
        wide_first,
        tall_first,
        pred_first,
        pred_down_first,
        enc_gains_first,
        pred_gains_first,
    )
    seconds = (
        wide_second,
        tall_second,
        pred_second,
        pred_down_second,
        enc_gains_second,
        pred_gains_second,
    )
    decays = (DECAY, DECAY, DECAY, DECAY, 0.0, 0.0)
    rates = (RATE, RATE, RATE, RATE, GAIN_RATE, GAIN_RATE)
    results = [
        adamw_step(
            masters[group_idx],
            shares[group_idx] * factor,
            firsts[group_idx],
            seconds[group_idx],
            decays[group_idx],
            rates[group_idx],
        )
        for group_idx in range(6)
    ]
    news = [entry[0] for entry in results]
    teacher_wide_new = KEEP_RATE * teacher_wide + (1.0 - KEEP_RATE) * news[0][:, : 4 * D + FF]
    teacher_tall_new = KEEP_RATE * teacher_tall + (1.0 - KEEP_RATE) * news[1]
    teacher_gains_new = KEEP_RATE * teacher_gains + (1.0 - KEEP_RATE) * news[4]
    return (
        loss_sum,
        target_total,
        grad_norm,
        news[0],
        news[1],
        news[2],
        news[3],
        news[4],
        news[5],
        results[0][1],
        results[1][1],
        results[2][1],
        results[3][1],
        results[4][1],
        results[5][1],
        results[0][2],
        results[1][2],
        results[2][2],
        results[3][2],
        results[4][2],
        results[5][2],
        news[0].astype(jnp.bfloat16),
        news[1].astype(jnp.bfloat16),
        news[2].astype(jnp.bfloat16),
        news[3].astype(jnp.bfloat16),
        news[4].astype(jnp.bfloat16),
        news[5].astype(jnp.bfloat16),
        teacher_wide_new,
        teacher_tall_new,
        teacher_gains_new,
    )


def solution(mesh):
    return jax.shard_map(
        local,
        mesh=mesh,
        in_specs=(
            P("dp", None, None),
            P("dp", None),
            P("dp"),
            P("dp", None),
            P("dp", None),
            P("dp", None),
            P("dp", None),
            P("dp", None),
            P("dp", None),
            P("dp", None),
            P("dp", None),
            P("dp", None),
            P("dp", None),
            P("dp", None),
            P("dp", None),
            P("dp", None),
            P("dp", None),
            P("dp", None),
            P("dp", None),
            P("dp", None),
            P("dp", None),
            P("dp", None),
            P("dp", None),
            P("dp", None),
        ),
        out_specs=(
            P(),
            P(),
            P(),
            P("dp", None),
            P("dp", None),
            P("dp", None),
            P("dp", None),
            P("dp", None),
            P("dp", None),
            P("dp", None),
            P("dp", None),
            P("dp", None),
            P("dp", None),
            P("dp", None),
            P("dp", None),
            P("dp", None),
            P("dp", None),
            P("dp", None),
            P("dp", None),
            P("dp", None),
            P("dp", None),
            P("dp", None),
            P("dp", None),
            P("dp", None),
            P("dp", None),
            P("dp", None),
            P("dp", None),
            P("dp", None),
            P("dp", None),
            P("dp", None),
        ),
        check_vma=False,
    )
```

```python
import functools
import math

import jax
import jax.numpy as jnp
from jax import lax
from jax.experimental import pallas as pl
from jax.experimental.pallas import tpu as pltpu
from jax.sharding import PartitionSpec as P

D = 1024
HE = 16
FF = 4096
PD = 384
PH = 12
PF = 1536
PATCH = 1536
L = 1536
STEP = 10
VIS = 576
VIS_LO = 192
HALF = L // 2
SEEN = VIS // 2
SKIP = VIS_LO // 2
LANES = 128
VMEM_LIMIT = 50 * 1024 * 1024


BETA_ONE = 0.9
BETA_TWO = 0.999
EPSILON = 1e-08
RATE = 0.02
GAIN_RATE = 0.5
DECAY = 0.05
CLIP_AT = 0.05
KEEP_RATE = 0.8
NEGATIVE = -1e30


def shortened(x):
    return jax.tree.map(lambda a: a.astype(jnp.bfloat16) if a.dtype == jnp.float32 else a, x)


def normed(stream):
    centred = stream - jnp.mean(stream, axis=-1, keepdims=True)
    return centred * lax.rsqrt(jnp.mean(centred * centred, axis=-1, keepdims=True) + 1e-06)


def scaled(stream, gain_vec):
    return normed(stream) * gain_vec


def position_table(positions, feature_width):
    frequency = jnp.exp(
        jnp.arange(feature_width // 2, dtype=jnp.float32)
        * (-2.0 * math.log(10000.0) / feature_width)
    )
    angles = positions.astype(jnp.float32)[:, None] * frequency[None, :]
    return jnp.concatenate([jnp.sin(angles), jnp.cos(angles)], axis=1)


def matmul(left, right):
    return jnp.dot(left, right, preferred_element_type=jnp.float32)


def inner_rows(left, right):
    return lax.dot_general(
        left, right, (((0,), (0,)), ((), ())), preferred_element_type=jnp.float32
    )


def outer_rows(left, right):
    return lax.dot_general(
        left, right, (((1,), (1,)), ((), ())), preferred_element_type=jnp.float32
    )


def head_scores(queries, key_heads, kept):
    logits = outer_rows(queries, key_heads)
    if kept is None:
        return logits
    key_ids = lax.broadcasted_iota(jnp.int32, logits.shape, 1)
    return jnp.where(key_ids < kept, logits, NEGATIVE)


def attend_kernel(head_size, masked, kept_ref, q_ref, k0_ref, v0_ref, k1_ref, v1_ref, o_ref, l_ref):
    exponent = head_size ** (-0.5) * math.log2(math.e)
    lane_head = lax.broadcasted_iota(jnp.int32, (1, LANES), 1) // head_size
    kept = (kept_ref[0], kept_ref[1]) if masked else (None, None)
    queries = q_ref[...]
    merged = jnp.zeros(o_ref.shape, jnp.float32)
    log_totals = jnp.zeros(o_ref.shape, jnp.float32)
    for head in range(LANES // head_size):
        chosen = lane_head == head
        head_queries = jnp.where(chosen, queries, jnp.zeros_like(queries))
        near = head_scores(head_queries, k0_ref[...], kept[0])
        far = head_scores(head_queries, k1_ref[...], kept[1])
        row_max = exponent * jnp.maximum(
            jnp.max(near, axis=1, keepdims=True), jnp.max(far, axis=1, keepdims=True)
        )
        near = jnp.exp2(near * exponent - row_max)
        far = jnp.exp2(far * exponent - row_max)
        row_total = jnp.sum(near, axis=1, keepdims=True) + jnp.sum(far, axis=1, keepdims=True)
        outcome = matmul(near.astype(jnp.bfloat16), v0_ref[...]) + matmul(
            far.astype(jnp.bfloat16), v1_ref[...]
        )
        merged = jnp.where(chosen, outcome / row_total, merged)
        log_totals = jnp.where(chosen, row_max + jnp.log2(row_total), log_totals)
    o_ref[...] = merged.astype(o_ref.dtype)
    if l_ref is not None:
        l_ref[...] = log_totals


def attend_rows(queries, kv_near, kv_far, kept, num_heads, block_rows):
    row_count, width = queries.shape
    keys = kv_near.shape[0]
    groups = width // LANES
    masked = kept is not None
    if not masked:
        kept = jnp.zeros((2,), jnp.int32)
    row_spec = pl.BlockSpec((block_rows, LANES), lambda g, b, kept: (b, g))
    k_spec = pl.BlockSpec((keys, LANES), lambda g, b, kept: (0, g))
    v_spec = pl.BlockSpec((keys, LANES), lambda g, b, kept: (0, g + groups))
    return pl.pallas_call(
        functools.partial(attend_kernel, width // num_heads, masked),
        grid_spec=pltpu.PrefetchScalarGridSpec(
            num_scalar_prefetch=1,
            grid=(groups, row_count // block_rows),
            in_specs=[row_spec, k_spec, v_spec, k_spec, v_spec],
            out_specs=[row_spec, row_spec],
        ),
        out_shape=[
            jax.ShapeDtypeStruct((row_count, width), jnp.bfloat16),
            jax.ShapeDtypeStruct((row_count, width), jnp.float32),
        ],
        compiler_params=pltpu.CompilerParams(vmem_limit_bytes=VMEM_LIMIT),
        cost_estimate=pl.CostEstimate(
            flops=8 * row_count * keys * width,
            bytes_accessed=8 * (row_count + keys) * width,
            transcendentals=2 * row_count * keys * num_heads,
        ),
    )(kept, queries, kv_near, kv_near, kv_far, kv_far)


def attend_back_kernel(
    head_size, masked, kept_ref, q_ref, g_ref, l_ref, k0_ref, v0_ref, k1_ref, v1_ref,
    dq_ref, dk0_ref, dv0_ref, dk1_ref, dv1_ref,
):
    scaling = head_size ** (-0.5)
    exponent = scaling * math.log2(math.e)
    lane_head = lax.broadcasted_iota(jnp.int32, (1, LANES), 1) // head_size
    kept = (kept_ref[0], kept_ref[1]) if masked else (None, None)

    @pl.when(pl.program_id(1) == 0)
    def _():
        for ref in (dk0_ref, dv0_ref, dk1_ref, dv1_ref):
            ref[...] = jnp.zeros_like(ref)

    queries, grads, log_totals = q_ref[...], g_ref[...], l_ref[...]
    grad_queries = jnp.zeros(dq_ref.shape, jnp.float32)
    for head in range(LANES // head_size):
        chosen = lane_head == head
        head_queries = jnp.where(chosen, queries, jnp.zeros_like(queries))
        head_grads = jnp.where(chosen, grads, jnp.zeros_like(grads))
        log_total = log_totals[:, head * head_size : head * head_size + 1]
        probs, steps, totals = [], [], 0.0
        for k_ref, v_ref, count in ((k0_ref, v0_ref, kept[0]), (k1_ref, v1_ref, kept[1])):
            attn = jnp.exp2(head_scores(head_queries, k_ref[...], count) * exponent - log_total)
            step = outer_rows(head_grads, v_ref[...]) * attn
            totals = totals + jnp.sum(step, axis=1, keepdims=True)
            probs.append(attn)
            steps.append(step)
        outcome = 0.0
        for attn, step, k_ref, dk_ref, dv_ref in zip(
            probs, steps, (k0_ref, k1_ref), (dk0_ref, dk1_ref), (dv0_ref, dv1_ref)
        ):
            grad_logits = (step - attn * totals).astype(jnp.bfloat16)
            dv_ref[...] += jnp.transpose(inner_rows(head_grads, attn.astype(jnp.bfloat16)))
            dk_ref[...] += jnp.transpose(inner_rows(head_queries, grad_logits)) * scaling
            outcome = outcome + matmul(grad_logits, k_ref[...])
        grad_queries = jnp.where(chosen, outcome * scaling, grad_queries)
    dq_ref[...] = grad_queries.astype(dq_ref.dtype)


def attend_rows_back(queries, grads, log_totals, kv_near, kv_far, kept, num_heads, block_rows):
    row_count, width = queries.shape
    keys = kv_near.shape[0]
    groups = width // LANES
    masked = kept is not None
    if not masked:
        kept = jnp.zeros((2,), jnp.int32)
    row_spec = pl.BlockSpec((block_rows, LANES), lambda g, b, kept: (b, g))
    k_spec = pl.BlockSpec((keys, LANES), lambda g, b, kept: (0, g))
    v_spec = pl.BlockSpec((keys, LANES), lambda g, b, kept: (0, g + groups))
    key_shape = jax.ShapeDtypeStruct((keys, width), jnp.float32)
    return pl.pallas_call(
        functools.partial(attend_back_kernel, width // num_heads, masked),
        grid_spec=pltpu.PrefetchScalarGridSpec(
            num_scalar_prefetch=1,
            grid=(groups, row_count // block_rows),
            in_specs=[row_spec, row_spec, row_spec, k_spec, v_spec, k_spec, v_spec],
            out_specs=[row_spec, k_spec, k_spec, k_spec, k_spec],
        ),
        out_shape=[jax.ShapeDtypeStruct((row_count, width), jnp.bfloat16)] + [key_shape] * 4,
        compiler_params=pltpu.CompilerParams(vmem_limit_bytes=VMEM_LIMIT),
        cost_estimate=pl.CostEstimate(
            flops=20 * row_count * keys * width,
            bytes_accessed=8 * (row_count + 4 * keys) * width,
            transcendentals=2 * row_count * keys * num_heads,
        ),
    )(kept, queries, grads, log_totals, kv_near, kv_near, kv_far, kv_far)


def padded_rows(block, before, after):
    return jnp.pad(block, ((before, after), (0, 0)))


def scaled_back(stream, gain_vec, grad_out):
    discarded_value, backward_fn = jax.vjp(scaled, stream, gain_vec)
    return backward_fn(grad_out)


def gelu_erf(raised):
    return 0.5 * raised * (1.0 + lax.erf(raised * 0.5**0.5))


def gelu_slope(raised):
    bell = jnp.exp(-0.5 * raised * raised) * (2.0 * math.pi) ** (-0.5)
    return 0.5 * (1.0 + lax.erf(raised * 0.5**0.5)) + raised * bell


def feed_fwd(stream, gain_vec, w_up, w_down):
    normal_in = scaled(stream, gain_vec).astype(jnp.bfloat16)
    raised = matmul(normal_in, w_up)
    hidden = gelu_erf(raised).astype(jnp.bfloat16)
    return (stream + matmul(hidden, w_down), (normal_in, raised, hidden))


def feed_back(stream, gain_vec, w_up, w_down, stored, grad_out):
    normal_in, raised, hidden = stored
    branch_grad = grad_out.astype(jnp.bfloat16)
    grad_hidden = outer_rows(branch_grad, w_down).astype(jnp.bfloat16).astype(jnp.float32)
    grad_raised = (grad_hidden * gelu_slope(raised)).astype(jnp.bfloat16)
    grad_wup = inner_rows(normal_in, grad_raised)
    grad_normal = outer_rows(grad_raised, w_up).astype(jnp.bfloat16).astype(jnp.float32)
    grad_stream, grad_gain = scaled_back(stream, gain_vec, grad_normal)
    return (grad_out + grad_stream, grad_wup, branch_grad, grad_gain)


def swapped(block):
    devices = range(lax.axis_size("dp"))
    return lax.ppermute(block, "dp", [(i, i ^ 1) for i in devices])


def attend_fwd(stream, gain_vec, w_in, w_out, num_heads, kept, skip, block_rows):
    width = stream.shape[1]
    normal_in = scaled(stream, gain_vec).astype(jnp.bfloat16)
    kv_near = matmul(normal_in, w_in[:, width:]).astype(jnp.bfloat16)
    kv_far = swapped(kv_near)
    queries = matmul(normal_in[skip:], w_in[:, :width]).astype(jnp.bfloat16)
    merged, log_totals = attend_rows(queries, kv_near, kv_far, kept, num_heads, block_rows)
    outcome = stream[skip:] + matmul(merged, w_out)
    return (outcome, (normal_in, queries, kv_near, kv_far, merged, log_totals))


def attend_back(stream, gain_vec, w_in, w_out, num_heads, kept, skip, block_rows, stored, grad_out):
    normal_in, queries, kv_near, kv_far, merged, log_totals = stored
    branch_grad = grad_out.astype(jnp.bfloat16)
    grad_wout = inner_rows(merged, branch_grad)
    grad_merged = outer_rows(branch_grad, w_out).astype(jnp.bfloat16)
    dq, dk_near, dv_near, dk_far, dv_far = attend_rows_back(
        queries, grad_merged, log_totals, kv_near, kv_far, kept, num_heads, block_rows
    )
    dk = (dk_near + swapped(dk_far)).astype(jnp.bfloat16)
    dv = (dv_near + swapped(dv_far)).astype(jnp.bfloat16)
    grad_packed = jnp.concatenate([padded_rows(dq, skip, 0), dk, dv], axis=1)
    grad_win = inner_rows(normal_in, grad_packed)
    grad_normal = outer_rows(grad_packed, w_in).astype(jnp.bfloat16).astype(jnp.float32)
    grad_stream, grad_gain = scaled_back(stream, gain_vec, grad_normal)
    return (padded_rows(grad_out, skip, 0) + grad_stream, grad_win, grad_wout, grad_gain)


def tall_grad_kernel(first_blocks, x_ref, gx_ref, h_ref, gh_ref, out_ref):
    @pl.when(pl.program_id(0) < first_blocks)
    def _():
        out_ref[...] = inner_rows(x_ref[...], gx_ref[...]).astype(out_ref.dtype)

    @pl.when(pl.program_id(0) >= first_blocks)
    def _():
        out_ref[...] = inner_rows(h_ref[...], gh_ref[...]).astype(out_ref.dtype)


def tall_grad(chosen, grad_stream, hidden, branch_grad):
    rows, width = grad_stream.shape
    block = 512
    first_blocks, blocks = PATCH // block, (PATCH + FF) // block
    return pl.pallas_call(
        functools.partial(tall_grad_kernel, first_blocks),
        grid=(blocks,),
        in_specs=[
            pl.BlockSpec((rows, block), lambda i: (0, jnp.minimum(i, first_blocks - 1))),
            pl.BlockSpec((rows, width), lambda i: (0, 0)),
            pl.BlockSpec((rows, block), lambda i: (0, jnp.maximum(i - first_blocks, 0))),
            pl.BlockSpec((rows, width), lambda i: (0, 0)),
        ],
        out_specs=pl.BlockSpec((block, width), lambda i: (i, 0)),
        out_shape=jax.ShapeDtypeStruct((PATCH + FF, width), jnp.bfloat16),
        compiler_params=pltpu.CompilerParams(vmem_limit_bytes=VMEM_LIMIT),
        cost_estimate=pl.CostEstimate(
            flops=2 * rows * width * (PATCH + FF),
            bytes_accessed=2 * (PATCH + FF) * (rows + width),
            transcendentals=0,
        ),
    )(chosen, grad_stream, hidden, branch_grad)


MESH = pl.DeviceIdType.MESH


def normed_rows(source, target, rows, gain_row, chunk, twice=False):
    def step(i, carried_through):
        at = pl.ds(pl.multiple_of(i * chunk, 16), chunk)
        values = normed(source[at, :]) * gain_row
        if twice:
            values = normed(values)
        target[at, :] = values.astype(target.dtype)
        return carried_through

    lax.fori_loop(0, rows // chunk, step, 0)


def gather_kernel(count, zn, *refs):
    ins, refs = refs[:count], refs[count:]
    pixels_ref, here_ref, there_ref, order_ref, high_ref, low_ref, *refs = refs
    outs, refs = refs[:count], refs[count:]
    goal_ref, picked_ref, table_ref, *refs = refs
    stages, refs = refs[:count], refs[count:]
    facts_ref, t0_ref, a_ref, near_ref, far_ref, q_ref, o_ref, h_ref, sum_ref, embed_buf, qkv_buf, up_buf, down_buf, *refs = refs
    pixel_buf, other_ref, chosen_ref, wide_buf, pred_buf, *refs = refs
    local_sem, z_send, z_recv, p_send, p_recv, w_sem, kv_sem = refs
    section, place = lax.axis_index("section"), lax.axis_index("dp")
    z, core = place // 2, place % 2
    near = {"section": section + 1 - 2 * (section % 2)}
    far = {"section": (section + 2) % 4}
    mate = {"dp": place + 1 - 2 * core}
    ahead = {"dp": place + 2}
    behind = {"dp": place - 2}

    def landing(a):
        rows, columns = stages[a].shape
        if ins[a].dtype == stages[a].dtype:
            return stages[a]
        buffer = t0_ref if columns == D and rows > 48 else wide_buf if columns == 8 * D else pred_buf
        return buffer.at[pl.ds(0, rows), pl.ds(0, columns)]

    def fetched(a):
        source = ins[a].at[:, pl.ds(0, stages[a].shape[1])]
        return pltpu.make_async_copy(source, landing(a), local_sem.at[a])

    for a in FIRST_IN:
        fetched(a).start()

    barrier = pltpu.get_barrier_semaphore()
    line = [{"dp": (z + j) % zn * 2 + core} for j in range(1, zn)]
    for other in [near, far, mate] + line:
        pl.semaphore_signal(barrier, inc=1, device_id=other, device_id_type=MESH)
    pl.semaphore_wait(barrier, 3 + len(line))

    def block(ref, a, owner_z, quarter=None, rows=None, owner_core=core):
        size = stages[a].shape[0]
        start, length = (0, size) if rows is None else rows
        offset = pl.multiple_of((owner_z * 2 + owner_core) * size + start, 16)
        if quarter is None:
            return ref.at[pl.ds(offset, length), :]
        width = stages[a].shape[1] // 4
        return ref.at[pl.ds(offset, length), pl.ds(pl.multiple_of(quarter * width, 128), width)]

    def own_quarter(a):
        width = stages[a].shape[1] // 4
        return stages[a].at[:, pl.ds(pl.multiple_of(section * width, 128), width)]

    def copy(src, dst, sends, recvs, index, device):
        return pltpu.make_async_remote_copy(
            src_ref=src,
            dst_ref=dst,
            send_sem=sends.at[index],
            recv_sem=recvs.at[index],
            device_id=device,
            device_id_type=MESH,
        )

    def along(a, step, upward):
        device = ahead if upward else behind
        source_z = z - (step - 1) if upward else z + (step - 1)
        src = own_quarter(a) if step == 1 else block(outs[a], a, source_z, section)
        index = (a * (zn - 1) + step - 1) * 2 + (0 if upward else 1)
        return copy(src, block(outs[a], a, source_z, section), z_send, z_recv, index, device)

    def beside(a, step, upward):
        device = ahead if upward else behind
        source_z = z - (step - 1) if upward else z + (step - 1)
        rows = (0, line_rows(a))
        quarter = (far["section"] + 1 - 2 * (far["section"] % 2)) % 4
        target = block(outs[a], a, source_z, quarter, rows)
        width = stages[a].shape[1] // 4
        src = (
            stages[a].at[pl.ds(0, rows[1]), pl.ds(pl.multiple_of(quarter * width, 128), width)]
            if step == 1
            else target
        )
        index = (a * (zn - 1) + step - 1) * 2 + (0 if upward else 1) + count * (zn - 1) * 2
        return copy(src, target, z_send, z_recv, index, device)

    def sends_along(step, upward):
        if upward:
            return (z - (step - 1) >= 0) & (z < zn - 1)
        return (z + (step - 1) <= zn - 1) & (z > 0)

    def line_rows(a):
        return stages[a].shape[0] // 16 // 3 * 16

    def first_half(a):
        start = line_rows(a)
        return (start, (stages[a].shape[0] - start + 31) // 32 * 16)

    def second_half(a):
        start = sum(first_half(a))
        return (start, stages[a].shape[0] - start)

    def in_plane(a, step, upward, kind):
        owner_z = z - step if upward else z + step
        index = ((a * (zn - 1) + step - 1) * 2 + (0 if upward else 1)) * 5 + kind
        x_quarter, y_quarter = near["section"], far["section"]
        part = [
            lambda: block(outs[a], a, owner_z, section),
            lambda: block(outs[a], a, owner_z, section),
            lambda: block(outs[a], a, owner_z, x_quarter, first_half(a)),
            lambda: block(outs[a], a, owner_z, y_quarter, second_half(a)),
            lambda: block(outs[a], a, owner_z),
        ][kind]()
        return copy(part, part, p_send, p_recv, index, (near, far, far, near, mate)[kind])

    def offered(a):
        for upward in (True, False):

            @pl.when(sends_along(1, upward))
            def _(upward=upward):
                along(a, 1, upward).start()
                if line_rows(a):
                    beside(a, 1, upward).start()

    own = []
    settled = []
    base = count * (zn - 1) * 10
    for a in ARRIVAL:
        fetched(a).wait()
        if ins[a].dtype != stages[a].dtype:
            source = landing(a)

            def rounded(i, carried_through):
                at = pl.ds(pl.multiple_of(i * 16, 16), 16)
                stages[a][at, :] = source[at, :].astype(stages[a].dtype)
                return carried_through

            lax.fori_loop(0, stages[a].shape[0] // 16, rounded, 0)
        if a in NEXT_IN:
            fetched(NEXT_IN[a]).start()
        keep = pltpu.make_async_copy(stages[a], block(outs[a], a, z), local_sem.at[a])
        give = copy(stages[a], block(outs[a], a, z), p_send, p_recv, base + a, mate)
        if a < 2:
            offered(a)
        keep.start()
        give.start()
        own.append((a, keep, give))
    own = [(keep, give) for a, keep, give in sorted(own, key=lambda entry: entry[0])]

    items = [
        (a, step, upward)
        for a in range(count)
        for step in range(1, zn)
        for upward in (True, False)
    ]

    def arrives(step, upward):
        return z - step >= 0 if upward else z + step <= zn - 1

    def received(a, step, upward):
        @pl.when(arrives(step, upward))
        def _():
            along(a, step, upward).wait_recv()
            in_plane(a, step, upward, 0).start()
            in_plane(a, step, upward, 1).start()

        if step < zn - 1:

            @pl.when(arrives(step, upward) & sends_along(step + 1, upward))
            def _():
                along(a, step + 1, upward).start()

    def passed_on(a, step, upward):
        if line_rows(a):

            @pl.when(arrives(step, upward))
            def _():
                beside(a, step, upward).wait_recv()

            if step < zn - 1:

                @pl.when(arrives(step, upward) & sends_along(step + 1, upward))
                def _():
                    beside(a, step + 1, upward).start()

        @pl.when(arrives(step, upward))
        def _():
            in_plane(a, step, upward, 0).wait_recv()
            in_plane(a, step, upward, 2).start()
            in_plane(a, step, upward, 1).wait_recv()
            in_plane(a, step, upward, 3).start()

    def completed(a, step, upward):
        @pl.when(arrives(step, upward))
        def _():
            in_plane(a, step, upward, 2).wait_recv()
            in_plane(a, step, upward, 3).wait_recv()
            in_plane(a, step, upward, 4).start()

    lag = 3
    group = 2 * (zn - 1)

    def advance(i):
        if i % group == group // 2 and 2 <= i // group + 1 < count:
            offered(i // group + 1)
        if 0 <= i - 2 * lag < len(items):
            completed(*items[i - 2 * lag])
        if 0 <= i - lag < len(items):
            passed_on(*items[i - lag])
        if i < len(items):
            received(*items[i])

    def settle(a):
        keep, give = own[a]
        keep.wait()
        give.wait_recv()
        for b, step, upward in items:
            if b == a:

                @pl.when(arrives(step, upward))
                def _(step=step, upward=upward):
                    in_plane(a, step, upward, 4).wait_recv()

        settled.append(a)

    def run_loop(length, body, steps):
        def step(i, carried_through):
            body(i)
            for at, move in enumerate(steps):
                pl.when(i == at * length // len(steps))(functools.partial(advance, move))
            return carried_through

        lax.fori_loop(0, length, step, 0)

    def streamed(length, fetches, body, steps):
        for fetch in fetches:
            fetch(0).start()

        def with_blocks(i):
            @pl.when(i + 1 < length)
            def _():
                for fetch in fetches:
                    fetch(i + 1).start()

            for fetch in fetches:
                fetch(i).wait()
            body(i, i % 2)

        run_loop(length, with_blocks, steps)

    def column_fetch(a, rows, first, width, buffer, sem):
        def fetch(i):
            columns = pl.ds(pl.multiple_of(first + i * width, 128), width)
            return pltpu.make_async_copy(
                outs[a].at[rows, columns], buffer.at[i % 2], w_sem.at[sem * 2 + i % 2]
            )

        return fetch

    ends = [group * (a + 1) + 2 * lag for a in range(count)]
    last = len(items) + 2 * lag
    SMALL, TALL, WIDE = 0, 1, 2
    clips_here = pixels_ref.shape[0]
    holds = core == section // clips_here
    first = list(range(min(ends[TALL], last)))
    pixel_copy = pltpu.make_async_copy(pixels_ref.at[section % clips_here], pixel_buf, kv_sem.at[2])
    handed = pltpu.make_async_remote_copy(
        src_ref=other_ref,
        dst_ref=chosen_ref,
        send_sem=kv_sem.at[3],
        recv_sem=kv_sem.at[4],
        device_id=mate,
        device_id_type=MESH,
    )

    @pl.when(holds)
    def _():
        pixel_copy.start()

    def tabulate(i):
        rows = pl.ds(pl.multiple_of(i * 96, 16), 96)
        order = order_ref[rows, :]

        def wave(table, index):
            choice = lax.broadcasted_iota(jnp.int32, (96, table.shape[0]), 1) == index
            return jnp.dot(
                choice.astype(jnp.float32), table[...],
                precision=lax.Precision.HIGHEST, preferred_element_type=jnp.float32,
            )

        high, low = wave(high_ref, order // 32), wave(low_ref, order % 32)
        sin_high, cos_high = high[:, : D // 2], high[:, D // 2 :]
        sin_low, cos_low = low[:, : D // 2], low[:, D // 2 :]
        t0_ref[rows, : D // 2] = sin_high * cos_low + cos_high * sin_low
        t0_ref[rows, D // 2 :] = cos_high * cos_low - sin_high * sin_low

    run_loop(HALF // 96, tabulate, first[:2])
    table_ref[...] = t0_ref[:SEEN, :]

    @pl.when(holds)
    def _():
        pixel_copy.wait()

    def pick(source, target):
        def rows_picked(i):
            @pl.when(holds)
            def _():
                rows = pl.ds(pl.multiple_of(i * 96, 16), 96)
                choice = lax.broadcasted_iota(jnp.int32, (96, L), 1) == source[rows, :]
                target[rows, :] = matmul(choice.astype(jnp.bfloat16), pixel_buf[...]).astype(jnp.bfloat16)

        return rows_picked

    run_loop(HALF // 96, pick(there_ref, other_ref), first[2:5])

    @pl.when(holds)
    def _():
        handed.start()

    run_loop(HALF // 96, pick(here_ref, chosen_ref), first[5:8])
    for i in first[8:]:
        advance(i)

    @pl.when(holds)
    def _():
        handed.wait_send()

    @pl.when(jnp.logical_not(holds))
    def _():
        handed.wait_recv()

    picked_ref[...] = chosen_ref[:SEEN, :]
    settle(SMALL)
    settle(TALL)
    facts = pltpu.make_async_copy(outs[SMALL].at[:, PD : PD + LANES], facts_ref, local_sem.at[SMALL])
    facts.start()

    def embed(i, slot):
        at = pl.ds(pl.multiple_of(i * 256, 128), 256)
        t0_ref[:, at] += matmul(chosen_ref[...], embed_buf[slot])

    waiting = list(range(ends[TALL], min(ends[WIDE], last)))
    streamed(4, [column_fetch(TALL, pl.ds(0, PATCH), 0, 256, embed_buf, 0)], embed, waiting[:2])
    facts.wait()
    gain_rows = jnp.transpose(facts_ref[...].astype(jnp.float32))
    normed_rows(t0_ref, a_ref, HALF, gain_rows[3:4, :], 96)
    for i in waiting[2:]:
        advance(i)
    settle(WIDE)

    rest = list(range(ends[WIDE], last))
    cuts = [len(rest) * part // 80 for part in (0, 6, 9, 42, 48, 80)]
    rest = [rest[cuts[i] : cuts[i + 1]] for i in range(5)]
    whole_rows = pl.ds(0, D)

    def keys_values(i, slot):
        at = pl.ds(pl.multiple_of(i * 256, 128), 256)
        near_ref[:, at] = matmul(a_ref[...], qkv_buf[slot]).astype(jnp.bfloat16)

    def queries(i, slot):
        at = pl.ds(pl.multiple_of(i * 256, 128), 256)
        q_ref[:, at] = matmul(a_ref[SKIP:, :], qkv_buf[slot]).astype(jnp.bfloat16)

    streamed(8, [column_fetch(WIDE, whole_rows, D, 256, qkv_buf, 1)], keys_values, rest[0])
    share = pltpu.make_async_remote_copy(
        src_ref=near_ref,
        dst_ref=far_ref,
        send_sem=kv_sem.at[0],
        recv_sem=kv_sem.at[1],
        device_id=mate,
        device_id_type=MESH,
    )
    share.start()
    streamed(4, [column_fetch(WIDE, whole_rows, 0, 256, qkv_buf, 1)], queries, rest[1])
    share.wait()
    block_rows = (HALF - SKIP) // 2

    def attention(i):
        lanes = pl.ds(pl.multiple_of(i // 2 * LANES, LANES), LANES)
        values = pl.ds(pl.multiple_of(D + i // 2 * LANES, LANES), LANES)
        rows = pl.ds(pl.multiple_of(i % 2 * block_rows, 16), block_rows)
        attend_kernel(
            D // HE, False, None, q_ref.at[rows, lanes], near_ref.at[:, lanes],
            near_ref.at[:, values], far_ref.at[:, lanes], far_ref.at[:, values],
            o_ref.at[rows, lanes], None,
        )

    run_loop(2 * D // LANES, attention, rest[2])

    def merge(i, slot):
        at = pl.ds(pl.multiple_of(i * 256, 128), 256)
        stream = t0_ref[SKIP:, at] + matmul(o_ref[...], qkv_buf[slot])
        sum_ref[:, at] = stream.astype(jnp.bfloat16).astype(jnp.float32)

    streamed(4, [column_fetch(WIDE, whole_rows, 3 * D, 256, qkv_buf, 1)], merge, rest[3])

    row_count = HALF - SKIP
    normed_rows(sum_ref, a_ref, row_count, gain_rows[4:5, :], 96)

    def down_fetch(i):
        rows = pl.ds(pl.multiple_of(PATCH + i * 512, 16), 512)
        return pltpu.make_async_copy(outs[TALL].at[rows, :], down_buf.at[i % 2], w_sem.at[6 + i % 2])

    def feed(i, slot):
        for part in range(2):
            rows = pl.ds(part * block_rows, block_rows)
            h_ref[...] = gelu_erf(matmul(a_ref[rows, :], up_buf[slot])).astype(jnp.bfloat16)
            sum_ref[rows, :] += matmul(h_ref[...], down_buf[slot])

    streamed(
        8,
        [column_fetch(WIDE, whole_rows, 4 * D, 512, up_buf, 2), down_fetch],
        feed,
        rest[4],
    )
    normed_rows(sum_ref, goal_ref, row_count, gain_rows[5:6, :], 96, twice=True)

    for a in range(count):
        if a not in settled:
            settle(a)
    for keep, give in own:
        give.wait_send()
    for a, step, upward in items:

        @pl.when(sends_along(step, upward))
        def _(a=a, step=step, upward=upward):
            along(a, step, upward).wait_send()
            if line_rows(a):
                beside(a, step, upward).wait_send()

        @pl.when(arrives(step, upward))
        def _(a=a, step=step, upward=upward):
            for kind in range(5):
                in_plane(a, step, upward, kind).wait_send()


FIRST_IN = (0, 1, 2, 5, 6)
ARRIVAL = (0, 1, 2, 3, 4, 5, 6)
NEXT_IN = {1: 3, 2: 4}


def gather_and_teach(blocks, widths, pixels, order_here, order_there, order):
    count = len(blocks)
    dp_size = lax.axis_size("dp")
    zn = dp_size // 2
    return pl.pallas_call(
        functools.partial(gather_kernel, count, zn),
        in_specs=[pl.BlockSpec(memory_space=pl.ANY)] * count
        + [pl.BlockSpec(memory_space=pl.ANY)]
        + [pl.BlockSpec(memory_space=pltpu.VMEM)] * 5,
        out_specs=[pl.BlockSpec(memory_space=pl.ANY)] * count
        + [pl.BlockSpec(memory_space=pltpu.VMEM)] * 3,
        out_shape=[
            jax.ShapeDtypeStruct((member.shape[0] * dp_size, width), jnp.bfloat16)
            for member, width in zip(blocks, widths)
        ]
        + [
            jax.ShapeDtypeStruct((HALF - SKIP, D), jnp.bfloat16),
            jax.ShapeDtypeStruct((SEEN, PATCH), jnp.bfloat16),
            jax.ShapeDtypeStruct((SEEN, D), jnp.float32),
        ],
        scratch_shapes=[
            pltpu.VMEM((member.shape[0], width), jnp.bfloat16)
            for member, width in zip(blocks, widths)
        ]
        + [
            pltpu.VMEM((D, LANES), jnp.bfloat16),
            pltpu.VMEM((HALF, D), jnp.float32),
            pltpu.VMEM((HALF, D), jnp.bfloat16),
            pltpu.VMEM((HALF, 2 * D), jnp.bfloat16),
            pltpu.VMEM((HALF, 2 * D), jnp.bfloat16),
            pltpu.VMEM((HALF - SKIP, D), jnp.bfloat16),
            pltpu.VMEM((HALF - SKIP, D), jnp.bfloat16),
            pltpu.VMEM(((HALF - SKIP) // 2, 512), jnp.bfloat16),
            pltpu.VMEM((HALF - SKIP, D), jnp.float32),
            pltpu.VMEM((2, PATCH, 256), jnp.bfloat16),
            pltpu.VMEM((2, D, 256), jnp.bfloat16),
            pltpu.VMEM((2, D, 512), jnp.bfloat16),
            pltpu.VMEM((2, 512, D), jnp.bfloat16),
            pltpu.VMEM((L, PATCH), jnp.bfloat16),
            pltpu.VMEM((HALF, PATCH), jnp.bfloat16),
            pltpu.VMEM((HALF, PATCH), jnp.bfloat16),
            pltpu.VMEM((blocks[2].shape[0], 8 * D), jnp.float32),
            pltpu.VMEM(blocks[5].shape, jnp.float32),
        ]
        + [
            pltpu.SemaphoreType.DMA((count,)),
            pltpu.SemaphoreType.DMA((count * (zn - 1) * 4,)),
            pltpu.SemaphoreType.DMA((count * (zn - 1) * 4,)),
            pltpu.SemaphoreType.DMA((count * ((zn - 1) * 10 + 1),)),
            pltpu.SemaphoreType.DMA((count * ((zn - 1) * 10 + 1),)),
            pltpu.SemaphoreType.DMA((8,)),
            pltpu.SemaphoreType.DMA((5,)),
        ],
        compiler_params=pltpu.CompilerParams(
            collective_id=0, has_side_effects=True, vmem_limit_bytes=58 * 1024 * 1024
        ),
    )(
        *blocks,
        pixels,
        order_here[:, None],
        order_there[:, None],
        order[:, None],
        position_table(32 * lax.iota(jnp.int32, L // 32), D),
        position_table(lax.iota(jnp.int32, 32), D),
    )


def upper_rows(size):
    return (size + 31) // 32 * 16


def add_blocks(rows, targets):
    def step(i, carried_through):
        at = pl.ds(pl.multiple_of(i * 16, 16), 16)
        for out, terms in targets:
            out[at, :] = sum(term[at, :].astype(jnp.float32) for term in terms).astype(out.dtype)
        return carried_through

    lax.fori_loop(0, rows // 16, step, 0)


def reduce_kernel(count, zn, *refs):
    ins, refs = refs[: count + 1], refs[count + 1 :]
    outs, refs = refs[: count + 1], refs[count + 1 :]
    whole, refs = refs[:count], refs[count:]
    near_one, refs = refs[:count], refs[count:]
    far_one, refs = refs[:count], refs[count:]
    far_two, refs = refs[:count], refs[count:]
    near_two, refs = refs[:count], refs[count:]
    along, refs = refs[:count], refs[count:]
    loaded, refs = refs[:count], refs[count:]
    held, refs = refs[:count], refs[count:]
    done, refs = refs[:count], refs[count:]
    total_ref, side_ref, line_ref, load_sem, move_send, move_recv, side_send, side_recv, line_send, line_recv = refs
    tally, out_total = ins[count], outs[count]
    tally_rows = out_total.shape[0]

    section, place = lax.axis_index("section"), lax.axis_index("dp")
    z, core = place // 2, place % 2
    x_quarter = section + 1 - 2 * (section % 2)
    y_quarter = (section + 2) % 4
    xy_quarter = (x_quarter + 2) % 4
    near, far = {"section": x_quarter}, {"section": y_quarter}
    mate = {"dp": place + 1 - 2 * core}
    sizes = [out.shape[0] for out in outs[:count]]
    widths = [out.shape[1] // 4 for out in outs[:count]]

    barrier = pltpu.get_barrier_semaphore()
    line = [{"dp": (z + j) % zn * 2 + core} for j in range(1, zn)]
    for other in [near, far, mate] + line:
        pl.semaphore_signal(barrier, inc=1, device_id=other, device_id_type=MESH)
    pl.semaphore_wait(barrier, 3 + len(line))

    def rows_at(a, slot, start=0, length=None):
        return pl.ds(pl.multiple_of(slot * sizes[a] + start, 16), sizes[a] if length is None else length)

    def quarter_at(a, quarter):
        return pl.ds(pl.multiple_of(quarter * widths[a], 128), widths[a])

    def upper(a):
        return upper_rows(sizes[a])

    def lower(a):
        return sizes[a] - upper_rows(sizes[a])

    def sent(src, dst, kind, a, slot, device):
        index = (kind * count + a) * (zn + 1) + slot
        return pltpu.make_async_remote_copy(
            src_ref=src,
            dst_ref=dst,
            send_sem=move_send.at[index],
            recv_sem=move_recv.at[index],
            device_id=device,
            device_id_type=MESH,
        )

    def load(a, owner_z):
        source = pl.ds(pl.multiple_of((owner_z * 2 + core) * sizes[a], 16), sizes[a])
        return pltpu.make_async_copy(
            ins[a].at[source, :], loaded[a].at[rows_at(a, owner_z), :], load_sem.at[a * zn + owner_z]
        )

    def give(a, owner_z):
        source = pl.ds(pl.multiple_of((owner_z * 2 + 1 - core) * sizes[a], 16), sizes[a])
        return sent(ins[a].at[source, :], whole[a].at[rows_at(a, owner_z), :], 0, a, owner_z, mate)

    def first_near(a, owner_z, which):
        quarter = (x_quarter, xy_quarter)[which]
        return sent(
            whole[a].at[rows_at(a, owner_z, 0, upper(a)), quarter_at(a, quarter)],
            near_one[a].at[pl.ds(pl.multiple_of((owner_z * 2 + which) * upper(a), 16), upper(a)), :],
            1 + which, a, owner_z, near,
        )

    def first_far(a, owner_z, which):
        quarter = (y_quarter, xy_quarter)[which]
        return sent(
            whole[a].at[rows_at(a, owner_z, upper(a), lower(a)), quarter_at(a, quarter)],
            far_one[a].at[pl.ds(pl.multiple_of((owner_z * 2 + which) * lower(a), 16), lower(a)), :],
            3 + which, a, owner_z, far,
        )

    def second_far(a, owner_z):
        return sent(
            whole[a].at[rows_at(a, owner_z, 0, upper(a)), quarter_at(a, y_quarter)],
            far_two[a].at[pl.ds(pl.multiple_of(owner_z * upper(a), 16), upper(a)), :],
            5, a, owner_z, far,
        )

    def second_near(a, owner_z):
        return sent(
            whole[a].at[rows_at(a, owner_z, upper(a), lower(a)), quarter_at(a, x_quarter)],
            near_two[a].at[pl.ds(pl.multiple_of(owner_z * lower(a), 16), lower(a)), :],
            6, a, owner_z, near,
        )

    def onward(a, owner_z, upward, last):
        slot = zn if last and not upward else owner_z
        return sent(
            whole[a].at[rows_at(a, owner_z), quarter_at(a, section)],
            along[a].at[rows_at(a, slot), :],
            7, a, slot, {"dp": place + 2 if upward else place - 2},
        )

    def finished(a, kind):
        quarter = (section, section, x_quarter, y_quarter)[kind]
        columns = quarter_at(a, quarter)
        part = (
            pl.ds(0, sizes[a]), pl.ds(0, sizes[a]), pl.ds(0, upper(a)), pl.ds(upper(a), lower(a))
        )[kind]
        src = done[a] if kind < 2 else outs[a].at[part, columns]
        return sent(src, outs[a].at[part, columns], 8 + kind, a, 0, (near, far, far, near)[kind])

    def keep(a):
        return pltpu.make_async_copy(
            done[a], outs[a].at[:, quarter_at(a, section)], load_sem.at[a * zn]
        )

    legs = [(k, upward) for k in range(zn - 1, 0, -1) for upward in (True, False)] + [(0, True)]
    items = [(a, leg) for leg in range(len(legs)) for a in range(count)]

    def owner_of(leg):
        k, upward = legs[leg]
        return z + k if upward else z - k

    def is_live(leg):
        k, upward = legs[leg]
        return (z + k <= zn - 1) if upward else (z - k >= 0)

    def started(a, leg):
        @pl.when(is_live(leg))
        def _():
            give(a, owner_of(leg)).start()

    def load_started(a, leg):
        @pl.when(is_live(leg))
        def _():
            load(a, owner_of(leg)).start()

    def parts(a, owner_z, is_upper, quarter):
        size = (0, upper(a)) if is_upper else (upper(a), lower(a))
        at = (rows_at(a, owner_z, *size), quarter_at(a, quarter))
        return (whole[a].at[at], loaded[a].at[at])

    def pair_up(a, owner_z, is_upper, quarter):
        both = parts(a, owner_z, is_upper, quarter)
        add_blocks(upper(a) if is_upper else lower(a), [(both[0], both)])

    def paired(a, leg):
        @pl.when(is_live(leg))
        def _():
            owner_z = owner_of(leg)
            load(a, owner_z).wait()
            give(a, owner_z).wait_recv()
            for quarter in (xy_quarter, x_quarter):
                pair_up(a, owner_z, True, quarter)
            for quarter in (xy_quarter, y_quarter):
                pair_up(a, owner_z, False, quarter)
            for which in (1, 0):
                first_near(a, owner_z, which).start()
                first_far(a, owner_z, which).start()


    def from_near(a, owner_z, which):
        start = pl.multiple_of((owner_z * 2 + which) * upper(a), 16)
        return near_one[a].at[pl.ds(start, upper(a)), :]

    def from_far(a, owner_z, which):
        start = pl.multiple_of((owner_z * 2 + which) * lower(a), 16)
        return far_one[a].at[pl.ds(start, lower(a)), :]

    def halved(a, leg):
        @pl.when(is_live(leg))
        def _():
            owner_z = owner_of(leg)
            first_near(a, owner_z, 1).wait_recv()
            both = parts(a, owner_z, True, y_quarter)
            add_blocks(upper(a), [(both[0], both + (from_near(a, owner_z, 1),))])
            second_far(a, owner_z).start()
            first_far(a, owner_z, 1).wait_recv()
            both = parts(a, owner_z, False, x_quarter)
            add_blocks(lower(a), [(both[0], both + (from_far(a, owner_z, 1),))])
            second_near(a, owner_z).start()

    def quartered(a, leg):
        k, upward = legs[leg]

        @pl.when(is_live(leg))
        def _():
            owner_z = owner_of(leg)
            own = quarter_at(a, section)
            first_near(a, owner_z, 0).wait_recv()
            second_far(a, owner_z).wait_recv()
            start = pl.multiple_of(owner_z * upper(a), 16)
            terms = parts(a, owner_z, True, section) + (
                from_near(a, owner_z, 0), far_two[a].at[pl.ds(start, upper(a)), :]
            )
            add_blocks(upper(a), [(held[a].at[pl.ds(0, upper(a)), :], terms)])
            first_far(a, owner_z, 0).wait_recv()
            second_near(a, owner_z).wait_recv()
            start = pl.multiple_of(owner_z * lower(a), 16)
            terms = parts(a, owner_z, False, section) + (
                from_far(a, owner_z, 0), near_two[a].at[pl.ds(start, lower(a)), :]
            )
            add_blocks(lower(a), [(held[a].at[pl.ds(upper(a), lower(a)), :], terms)])
            target = held[a]

            def join(upward_from, slot):
                onward(a, owner_z, upward_from, slot is not owner_z or k == 0).wait_recv()
                add_blocks(sizes[a], [(target, (target, along[a].at[rows_at(a, slot), :]))])

            if k > 0:

                @pl.when(z > 0 if upward else z < zn - 1)
                def _():
                    join(upward, owner_z)

                add_blocks(sizes[a], [(whole[a].at[rows_at(a, owner_z), own], (target,))])
                onward(a, owner_z, upward, k == 1).start()
            else:

                @pl.when(z > 0)
                def _():
                    join(True, owner_z)

                @pl.when(z < zn - 1)
                def _():
                    join(False, zn)

                def settle(i, carried_through):
                    at = pl.ds(pl.multiple_of(i * 16, 16), 16)
                    values = target[at, :]
                    done[a][at, :] = values.astype(done[a].dtype)
                    squares = values * values
                    squares = squares[:8] + squares[8:]
                    carried = total_ref[0:8, :]
                    for column in range(0, widths[a], 128):
                        carried = carried + squares[:, column : column + 128]
                    total_ref[0:8, :] = carried
                    return carried_through

                lax.fori_loop(0, sizes[a] // 16, settle, 0)
                keep(a).start()
                finished(a, 0).start()
                finished(a, 1).start()

    total_ref[0:8, :] = jnp.zeros((8, 128), jnp.float32)
    tally_copy = pltpu.make_async_copy(tally, total_ref.at[8:, :], load_sem.at[count * zn])
    tally_copy.start()
    for a, leg in items:
        started(a, leg)
        load_started(a, leg)
    lag = 5
    for i in range(len(items) + 2 * lag):
        if i < len(items):
            paired(*items[i])
        if 0 <= i - lag < len(items):
            halved(*items[i - lag])
        if 0 <= i - 2 * lag < len(items):
            quartered(*items[i - 2 * lag])

    tally_copy.wait()

    def exchanged(stage, device):
        return pltpu.make_async_remote_copy(
            src_ref=total_ref,
            dst_ref=side_ref.at[pl.ds(stage * tally_rows, tally_rows), :],
            send_sem=side_send.at[stage],
            recv_sem=side_recv.at[stage],
            device_id=device,
            device_id_type=MESH,
        )

    for stage, device in enumerate((mate, near, far)):
        swap = exchanged(stage, device)
        swap.start()
        swap.wait()
        total_ref[...] += side_ref[stage * tally_rows : (stage + 1) * tally_rows, :]

    def told(from_z, to_z, j):
        index = from_z * zn + to_z
        return pltpu.make_async_remote_copy(
            src_ref=total_ref,
            dst_ref=line_ref.at[pl.ds(pl.multiple_of(from_z * tally_rows, 8), tally_rows), :],
            send_sem=line_send.at[index],
            recv_sem=line_recv.at[index],
            device_id={"dp": to_z * 2 + core},
            device_id_type=MESH,
        )

    for j in range(1, zn):
        told(z, (z + j) % zn, j).start()
    line_ref[pl.ds(pl.multiple_of(z * tally_rows, 8), tally_rows), :] = total_ref[...]
    for j in range(1, zn):
        told((z + j) % zn, z, j).wait_recv()
    grand = line_ref[0:tally_rows, :]
    for j in range(1, zn):
        grand = grand + line_ref[j * tally_rows : (j + 1) * tally_rows, :]
    for j in range(1, zn):
        told(z, (z + j) % zn, j).wait_send()
    total_ref[...] = grand
    show = pltpu.make_async_copy(total_ref, out_total, load_sem.at[count * zn])
    show.start()

    for a in range(count):
        finished(a, 0).wait_recv()
        finished(a, 2).start()
        finished(a, 1).wait_recv()
        finished(a, 3).start()
    for a in range(count):
        keep(a).wait()
        finished(a, 2).wait_recv()
        finished(a, 3).wait_recv()
        for kind in range(4):
            finished(a, kind).wait_send()
    for a, leg in items:
        k, upward = legs[leg]

        @pl.when(is_live(leg))
        def _(a=a, leg=leg, k=k, upward=upward):
            owner_z = owner_of(leg)
            give(a, owner_z).wait_send()
            for which in (0, 1):
                first_near(a, owner_z, which).wait_send()
                first_far(a, owner_z, which).wait_send()
            second_near(a, owner_z).wait_send()
            second_far(a, owner_z).wait_send()
            if k > 0:
                onward(a, owner_z, upward, k == 1).wait_send()

    show.wait()


def reduce_blocks(blocks, tally, result_types):
    count = len(blocks)
    dp_size = lax.axis_size("dp")
    zn = dp_size // 2
    tally_rows = 8 + tally.shape[0]
    shapes = [(member.shape[0] // dp_size, member.shape[1]) for member in blocks]
    vmem = lambda rows, columns, dtype=jnp.bfloat16: pltpu.VMEM((rows, columns), dtype)
    anywhere = pl.BlockSpec(memory_space=pl.ANY)
    moves = 12 * count * (zn + 1)
    return pl.pallas_call(
        functools.partial(reduce_kernel, count, zn),
        in_specs=[anywhere] * (count + 1),
        out_specs=[anywhere] * (count + 1),
        out_shape=[jax.ShapeDtypeStruct(shape, kind) for shape, kind in zip(shapes, result_types)]
        + [jax.ShapeDtypeStruct((tally_rows, 128), jnp.float32)],
        scratch_shapes=[vmem(zn * r, w) for r, w in shapes]
        + [vmem(zn * 2 * upper_rows(r), w // 4) for r, w in shapes]
        + [vmem(zn * 2 * (r - upper_rows(r)), w // 4) for r, w in shapes]
        + [vmem(zn * upper_rows(r), w // 4) for r, w in shapes]
        + [vmem(zn * (r - upper_rows(r)), w // 4) for r, w in shapes]
        + [vmem((zn + 1) * r, w // 4) for r, w in shapes]
        + [vmem(zn * r, w) for r, w in shapes]
        + [vmem(r, w // 4, jnp.float32) for r, w in shapes]
        + [vmem(r, w // 4, kind) for (r, w), kind in zip(shapes, result_types)]
        + [
            vmem(tally_rows, 128, jnp.float32),
            vmem(3 * tally_rows, 128, jnp.float32),
            vmem(zn * tally_rows, 128, jnp.float32),
            pltpu.SemaphoreType.DMA((count * zn + 1,)),
            pltpu.SemaphoreType.DMA((moves,)),
            pltpu.SemaphoreType.DMA((moves,)),
            pltpu.SemaphoreType.DMA((3,)),
            pltpu.SemaphoreType.DMA((3,)),
            pltpu.SemaphoreType.DMA((zn * zn,)),
            pltpu.SemaphoreType.DMA((zn * zn,)),
        ],
        compiler_params=pltpu.CompilerParams(
            collective_id=1, has_side_effects=True, vmem_limit_bytes=60 * 1024 * 1024
        ),
    )(*blocks, tally)


def adamw_step(weight, grad_now, first, second, decay, rate):
    first = BETA_ONE * first + (1.0 - BETA_ONE) * grad_now
    second = BETA_TWO * second + (1.0 - BETA_TWO) * grad_now * grad_now
    ratio = first / (1.0 - BETA_ONE**STEP) / (jnp.sqrt(second / (1.0 - BETA_TWO**STEP)) + EPSILON)
    return (weight - rate * (ratio + decay * weight), first, second)


def local(
    pixels,
    token_order,
    visible,
    wide_weight,
    tall_weight,
    pred_weight,
    pred_down,
    enc_gains,
    pred_gains,
    wide_first,
    tall_first,
    pred_first,
    pred_down_first,
    enc_gains_first,
    pred_gains_first,
    wide_second,
    tall_second,
    pred_second,
    pred_down_second,
    enc_gains_second,
    pred_gains_second,
    teacher_wide,
    teacher_tall,
    teacher_gains,
):
    masters = (wide_weight, tall_weight, pred_weight, pred_down, enc_gains, pred_gains)
    section_idx = lax.axis_index("section")
    section_count = lax.axis_size("section")
    core = lax.axis_index("dp") % 2
    clips_here = pixels.shape[0]
    assert section_count == 2 * clips_here

    owner = section_idx // clips_here
    clip = section_idx % clips_here
    holds = core == owner
    counts_own = lax.dynamic_index_in_dim(visible, clip, 0)
    order_own = lax.dynamic_index_in_dim(token_order, clip, 0, keepdims=False)
    clip_facts = jnp.concatenate([order_own, counts_own])
    clip_facts = jnp.where(holds, clip_facts, swapped(clip_facts))
    seen = clip_facts[L]
    order_pairs = clip_facts[:L].reshape(HALF, 2)
    order = jnp.where(core == 0, order_pairs[:, 0], order_pairs[:, 1])
    pairs_own = order_own.reshape(HALF, 2)
    order_here = jnp.where(core == 0, pairs_own[:, 0], pairs_own[:, 1])
    order_there = jnp.where(core == 0, pairs_own[:, 1], pairs_own[:, 0])
    seen_near = (seen - core + 1) // 2
    seen_far = (seen + core) // 2
    kept = jnp.stack([seen_near, seen_far])
    visible_high, visible_low = visible // LANES, visible % LANES
    dp_size = lax.axis_size("dp")
    row_count = wide_weight.shape[0]
    small = jnp.concatenate(
        [
            wide_weight[:, 4 * D + FF :],
            enc_gains,
            teacher_gains,
            jnp.pad(pred_gains, ((0, row_count - pred_gains.shape[0]), (0, 0))),
            jnp.zeros((row_count, LANES - 10 - 2 * clips_here), jnp.float32),
            jnp.broadcast_to(
                jnp.concatenate([visible_high, visible_low]).astype(jnp.float32)[None, :],
                (row_count, 2 * clips_here),
            ),
        ],
        axis=1,
    ).astype(jnp.bfloat16)
    pred_block = pred_weight.shape if pred_weight.shape[0] % 16 == 0 else (-1, D)
    pred_form = (PD, pred_weight.shape[1]) if pred_weight.shape[0] % 16 == 0 else (-1, D)
    blocks = (
        small,
        teacher_tall,
        teacher_wide,
        tall_weight,
        wide_weight,
        pred_weight.reshape(pred_block),
        jnp.pad(pred_down.astype(jnp.bfloat16), ((0, 0), (0, LANES))),
    )
    w_small, teach_tall, teach_wide, w_tall, w_wide, w_pred, w_down, goal, enc_chosen, table = gather_and_teach(
        blocks,
        [4 * D + FF if member is wide_weight else member.shape[1] for member in blocks],
        pixels,
        order_here,
        order_there,
        order,
    )
    goal = goal.astype(jnp.float32)
    w_pred = w_pred.reshape(PD, -1)
    w_down = w_down[:, :PD]
    pred_embed = w_small[:, :PD]
    enc_copy = w_small[:, PD : PD + 3]
    pred_copy = w_small[:, PD + 6 : PD + 10].reshape(dp_size, row_count, 4)
    pred_copy = pred_copy[:, : pred_gains.shape[0]].reshape(PD, 4)
    counts = w_small[::row_count, PD + LANES - 2 * clips_here :].astype(jnp.float32)
    counts = counts[:, :clips_here] * LANES + counts[:, clips_here:]
    target_total = jnp.sum(L - counts)
    enc_gain = enc_copy.astype(jnp.float32)
    pred_gain = pred_copy.astype(jnp.float32)
    enc_attn = (w_wide[:, : 3 * D], w_wide[:, 3 * D : 4 * D])
    enc_feed = (w_wide[:, 4 * D : 4 * D + FF], w_tall[PATCH:])
    pred_attn = (w_pred[:, : 3 * PD], w_pred[:, 3 * PD : 4 * PD])
    pred_feed = (w_pred[:, 4 * PD : 4 * PD + PF], w_down)
    pred_head = w_pred[:, 4 * PD + PF :]

    pred_table = position_table(order, PD)
    row_ids = lax.iota(jnp.int32, HALF)
    context = (row_ids < seen_near)[:, None]

    stream_a = matmul(enc_chosen, w_tall[:PATCH]) + table
    stream_b, stored_a = attend_fwd(
        stream_a, enc_gain[:, 0], enc_attn[0], enc_attn[1], HE, kept, 0, SEEN
    )
    stream_b = stream_b.astype(jnp.bfloat16).astype(jnp.float32)
    stream_c, stored_b = feed_fwd(stream_b, enc_gain[:, 1], enc_feed[0], enc_feed[1])
    encoded = scaled(stream_c, enc_gain[:, 2]).astype(jnp.bfloat16)

    projected = padded_rows(matmul(encoded, pred_embed), 0, HALF - SEEN)
    stream_d = jnp.where(context, projected, pred_gain[:, 3][None, :]) + pred_table
    stream_e, stored_d = attend_fwd(
        stream_d, pred_gain[:, 0], pred_attn[0], pred_attn[1], PH, None, SKIP, HALF - SKIP
    )
    stream_e = stream_e.astype(jnp.bfloat16).astype(jnp.float32)
    stream_f, stored_e = feed_fwd(stream_e, pred_gain[:, 1], pred_feed[0], pred_feed[1])
    final = scaled(stream_f, pred_gain[:, 2]).astype(jnp.bfloat16)
    residual = matmul(final, pred_head) - goal
    smooth_err = jnp.sqrt(residual * residual + 1.0)
    target_mask = jnp.logical_not(context[SKIP:])
    loss_part = jnp.sum(jnp.where(target_mask, smooth_err - 1.0, 0.0))
    grad_guess = (jnp.where(target_mask, residual / smooth_err, 0.0) / target_total).astype(
        jnp.bfloat16
    )

    grad_head = inner_rows(final, grad_guess)
    grad_final = outer_rows(grad_guess, pred_head).astype(jnp.bfloat16).astype(jnp.float32)
    grad_stream, grad_pg2 = scaled_back(stream_f, pred_gain[:, 2], grad_final)
    grad_stream, grad_pup, branch_grad, grad_pg1 = feed_back(
        stream_e, pred_gain[:, 1], pred_feed[0], pred_feed[1], stored_e, grad_stream
    )
    grad_down = inner_rows(stored_e[2], jnp.pad(branch_grad, ((0, 0), (0, LANES))))
    grad_stream = grad_stream.astype(jnp.bfloat16).astype(jnp.float32)
    grad_stream, grad_pin, grad_pout, grad_pg0 = attend_back(
        stream_d, pred_gain[:, 0], pred_attn[0], pred_attn[1], PH, None, SKIP, HALF - SKIP, stored_d, grad_stream
    )
    grad_token = jnp.sum(jnp.where(context, 0.0, grad_stream), axis=0)
    grad_projected = jnp.where(context, grad_stream, 0.0)[:SEEN].astype(jnp.bfloat16)
    grad_embed = inner_rows(encoded, jnp.pad(grad_projected, ((0, 0), (0, LANES))))
    grad_encoded = outer_rows(grad_projected, pred_embed).astype(jnp.bfloat16).astype(jnp.float32)
    grad_stream, grad_eg2 = scaled_back(stream_c, enc_gain[:, 2], grad_encoded)
    grad_stream, grad_eup, branch_grad, grad_eg1 = feed_back(
        stream_b, enc_gain[:, 1], enc_feed[0], enc_feed[1], stored_b, grad_stream
    )
    grad_stream = grad_stream.astype(jnp.bfloat16).astype(jnp.float32)
    grad_stream, grad_ein, grad_eout, grad_eg0 = attend_back(
        stream_a, enc_gain[:, 0], enc_attn[0], enc_attn[1], HE, kept, 0, SEEN, stored_a, grad_stream
    )
    grad_tall = tall_grad(
        enc_chosen, grad_stream.astype(jnp.bfloat16), stored_b[2], branch_grad
    )

    gain_grads = jnp.concatenate(
        [
            jnp.stack([grad_eg0, grad_eg1, grad_eg2], axis=1).reshape(-1, LANES),
            jnp.stack([grad_pg0, grad_pg1, grad_pg2, grad_token], axis=1).reshape(-1, LANES),
        ],
        axis=0,
    )
    gain_rows = 3 * D // LANES
    loss_tile = jnp.zeros((8, LANES), jnp.float32).at[0, 0].set(loss_part)
    tally = jnp.concatenate(
        [loss_tile, gain_grads, jnp.zeros((4, LANES), jnp.float32)], axis=0
    )
    blocks = shortened(
        (
            grad_ein,
            grad_eout,
            grad_eup,
            grad_embed,
            grad_tall,
            jnp.concatenate(shortened([grad_pin, grad_pout, grad_pup, grad_head]), axis=1).reshape(pred_form),
            grad_down,
        )
    )
    *summed, tally = reduce_blocks(
        blocks, tally, [jnp.bfloat16] * 5 + [jnp.float32] * 2
    )
    wide_parts = [summed[0], summed[1], summed[2], summed[3][:, :PD]]
    place = lax.axis_index("dp")
    gains_all = tally[16 : 16 + gain_rows].reshape(D, 3)
    pred_gains_all = tally[16 + gain_rows : 16 + gain_rows + 4 * PD // LANES].reshape(PD, 4)
    shares = (
        jnp.concatenate(wide_parts, axis=1).astype(jnp.float32),
        summed[4].astype(jnp.float32),
        summed[5].reshape(pred_weight.shape).astype(jnp.float32),
        summed[6][:, :PD].astype(jnp.float32),
        lax.dynamic_slice_in_dim(gains_all, place * enc_gains.shape[0], enc_gains.shape[0], 0),
        lax.dynamic_slice_in_dim(pred_gains_all, place * pred_gains.shape[0], pred_gains.shape[0], 0),
    )
    loss_sum = tally[8, 0]
    square_total = jnp.sum(tally[:8]) + jnp.sum(jnp.square(tally[16:]))
    grad_norm = jnp.sqrt(square_total)
    factor = jnp.minimum(1.0, CLIP_AT / (grad_norm + 1e-06))
    firsts = (
        wide_first,
        tall_first,
        pred_first,
        pred_down_first,
        enc_gains_first,
        pred_gains_first,
    )
    seconds = (
        wide_second,
        tall_second,
        pred_second,
        pred_down_second,
        enc_gains_second,
        pred_gains_second,
    )
    decays = (DECAY, DECAY, DECAY, DECAY, 0.0, 0.0)
    rates = (RATE, RATE, RATE, RATE, GAIN_RATE, GAIN_RATE)
    results = [
        adamw_step(
            masters[group_idx],
            shares[group_idx] * factor,
            firsts[group_idx],
            seconds[group_idx],
            decays[group_idx],
            rates[group_idx],
        )
        for group_idx in range(6)
    ]
    news = [entry[0] for entry in results]
    teacher_wide_new = KEEP_RATE * teacher_wide + (1.0 - KEEP_RATE) * news[0][:, : 4 * D + FF]
    teacher_tall_new = KEEP_RATE * teacher_tall + (1.0 - KEEP_RATE) * news[1]
    teacher_gains_new = KEEP_RATE * teacher_gains + (1.0 - KEEP_RATE) * news[4]
    return (
        loss_sum,
        target_total,
        grad_norm,
        news[0],
        news[1],
        news[2],
        news[3],
        news[4],
        news[5],
        results[0][1],
        results[1][1],
        results[2][1],
        results[3][1],
        results[4][1],
        results[5][1],
        results[0][2],
        results[1][2],
        results[2][2],
        results[3][2],
        results[4][2],
        results[5][2],
        news[0].astype(jnp.bfloat16),
        news[1].astype(jnp.bfloat16),
        news[2].astype(jnp.bfloat16),
        news[3].astype(jnp.bfloat16),
        news[4].astype(jnp.bfloat16),
        news[5].astype(jnp.bfloat16),
        teacher_wide_new,
        teacher_tall_new,
        teacher_gains_new,
    )


def solution(mesh):
    return jax.shard_map(
        local,
        mesh=mesh,
        in_specs=(
            P("dp", None, None),
            P("dp", None),
            P("dp"),
            P("dp", None),
            P("dp", None),
            P("dp", None),
            P("dp", None),
            P("dp", None),
            P("dp", None),
            P("dp", None),
            P("dp", None),
            P("dp", None),
            P("dp", None),
            P("dp", None),
            P("dp", None),
            P("dp", None),
            P("dp", None),
            P("dp", None),
            P("dp", None),
            P("dp", None),
            P("dp", None),
            P("dp", None),
            P("dp", None),
            P("dp", None),
        ),
        out_specs=(
            P(),
            P(),
            P(),
            P("dp", None),
            P("dp", None),
            P("dp", None),
            P("dp", None),
            P("dp", None),
            P("dp", None),
            P("dp", None),
            P("dp", None),
            P("dp", None),
            P("dp", None),
            P("dp", None),
            P("dp", None),
            P("dp", None),
            P("dp", None),
            P("dp", None),
            P("dp", None),
            P("dp", None),
            P("dp", None),
            P("dp", None),
            P("dp", None),
            P("dp", None),
            P("dp", None),
            P("dp", None),
            P("dp", None),
            P("dp", None),
            P("dp", None),
            P("dp", None),
        ),
        check_vma=False,
    )
```
